32 devices in a mesh: dp: 4 (over y, core), expert: 8 (over z, x).
Axes of the slice: x: 2, y: 2, z: 4, core: 2. Of those that a mesh axis runs over, the one named last changes fastest.
Arguments:
- layer_input: bfloat16 [8192, 1536], P(('dp', 'expert')), may hold values from -6 to 6
- cotangent: float32 [8192, 1536], P(('dp', 'expert')), may hold values from -6 to 6
- lengths: int32 [32], P(('dp', 'expert')), may hold values from 64 to 256, as said below
- routes_a: int32 [8192, 6], P(('dp', 'expert')), may hold values from 0 to 15, all different within a row; in each aligned block of 128 rows (0 to 127, 128 to 255, ...) at most 60 rows name the same one
- routes_b: int32 [8192, 6], P(('dp', 'expert')), may hold values from 0 to 15, all different within a row; in each aligned block of 128 rows (0 to 127, 128 to 255, ...) at most 60 rows name the same one
- mixer_in: bfloat16 [1536, 6448], P(('dp', 'expert')), may hold values from -0.15625 to 0.15625
- mixer_out: bfloat16 [1536, 3072], P(('dp', 'expert')), may hold values from -0.109375 to 0.109375
- router_a: bfloat16 [1536, 16], P(('dp', 'expert')), may hold values from -0.078125 to 0.078125
- shared_in_a: bfloat16 [1536, 2048], P(('dp', 'expert')), may hold values from -0.15625 to 0.15625
- shared_out_a: bfloat16 [1536, 1024], P(('dp', 'expert')), may hold values from -0.1875 to 0.1875
- expert_in_a: bfloat16 [16, 1536, 1024], P('expert', 'dp'), may hold values from -0.15625 to 0.15625
- expert_out_a: bfloat16 [16, 1536, 512], P('expert', 'dp'), may hold values from -0.25 to 0.25
- attn_qkv: bfloat16 [1536, 2560], P(('dp', 'expert')), may hold values from -0.15625 to 0.15625
- attn_out: bfloat16 [1536, 1536], P(('dp', 'expert')), may hold values from -0.4375 to 0.4375
- router_b: bfloat16 [1536, 16], P(('dp', 'expert')), may hold values from -0.078125 to 0.078125
- shared_in_b: bfloat16 [1536, 2048], P(('dp', 'expert')), may hold values from -0.15625 to 0.15625
- shared_out_b: bfloat16 [1536, 1024], P(('dp', 'expert')), may hold values from -0.1875 to 0.1875
- expert_in_b: bfloat16 [16, 1536, 1024], P('expert', 'dp'), may hold values from -0.15625 to 0.15625
- expert_out_b: bfloat16 [16, 1536, 512], P('expert', 'dp'), may hold values from -0.25 to 0.25
- norm_gains: float32 [4, 1536], replicated, may hold values from 0.5 to 1.5
- mixer_gain: float32 [3072], replicated, may hold values from 0.5 to 1.5
- conv_weight: float32 [4, 3328], replicated, may hold values from -3 to 3
- conv_bias: float32 [3328], replicated, may hold values from -3 to 3
- decay_log: float32 [48], replicated, may hold values from -4.5 to 0.5
- step_bias: float32 [48], replicated, may hold values from -4 to -0.5
- skip_gain: float32 [48], replicated, may hold values from 0.5 to 1.5
Outputs:
- layer_output: float32 [8192, 1536], P(('dp', 'expert'))
- input_grad: float32 [8192, 1536], P(('dp', 'expert'))
- grad_mixer_in: float32 [1536, 6448], P(('dp', 'expert'))
- grad_mixer_out: float32 [1536, 3072], P(('dp', 'expert'))
- grad_router_a: float32 [1536, 16], P(('dp', 'expert'))
- grad_shared_in_a: float32 [1536, 2048], P(('dp', 'expert'))
- grad_shared_out_a: float32 [1536, 1024], P(('dp', 'expert'))
- grad_expert_in_a: float32 [16, 1536, 1024], P('expert', 'dp')
- grad_expert_out_a: float32 [16, 1536, 512], P('expert', 'dp')
- grad_attn_qkv: float32 [1536, 2560], P(('dp', 'expert'))
- grad_attn_out: float32 [1536, 1536], P(('dp', 'expert'))
- grad_router_b: float32 [1536, 16], P(('dp', 'expert'))
- grad_shared_in_b: float32 [1536, 2048], P(('dp', 'expert'))
- grad_shared_out_b: float32 [1536, 1024], P(('dp', 'expert'))
- grad_expert_in_b: float32 [16, 1536, 1024], P('expert', 'dp')
- grad_expert_out_b: float32 [16, 1536, 512], P('expert', 'dp')
- grad_norm_gains: float32 [4, 1536], replicated
- grad_mixer_gain: float32 [3072], replicated
- grad_conv_weight: float32 [4, 3328], replicated
- grad_conv_bias: float32 [3328], replicated
- grad_decay_log: float32 [48], replicated
- grad_step_bias: float32 [48], replicated
- grad_skip_gain: float32 [48], replicated
The draws below stay inside these ranges and needn't reach their ends.
Inputs may be any that keep to these rules, and one draw needn't show every extreme that they name: `routes_a`: in each aligned block of 128 rows, no expert is named by more than 60 rows. `routes_b`: in each aligned block of 128 rows, no expert is named by more than 60 rows. `lengths`: some slot has exactly 256 valid tokens and some exactly 64.
All inputs are finite; a program needn't handle non-finite values.
Results may differ from the reference program's by a relative error of at most 0.023.
Values may be sent and summed in bfloat16 or wider, within the bound.
A program may use at most 448 MiB of HBM per device.

```python
import math
import jax
import jax.numpy as jnp
import numpy as np
from jax import lax

D = 1536
MHEADS = 48
MHDIM = 64
NSTATE = 128
KCONV = 4
AHEADS = 12
KVHEADS = 4
AHDIM = 128
FE = 512
FS = 1024
TOP = 6
SLOT_LEN = 256
DI = 3072
CONVCH = 3328
PIN = 6448
QD = 1536
KVD = 512
QKV = 2560
EXPERTS = 16
HALF = 128
CAP = 60
SLOTS = 32
TOKENS = 8192


def draw_lengths(key, part):
    key = jax.random.fold_in(key, 11)
    keys_split = jax.random.split(key, 3)
    drawn_lengths = jax.random.randint(keys_split[0], (SLOTS,), SLOT_LEN // 4, SLOT_LEN + 1)
    longest = jax.random.randint(keys_split[1], (), 0, SLOTS)
    shortest = (longest + 1 + jax.random.randint(keys_split[2], (), 0, SLOTS - 1)) % SLOTS
    places = jnp.arange(SLOTS)
    drawn_lengths = jnp.where(places == longest, SLOT_LEN, drawn_lengths)
    return jnp.where(places == shortest, SLOT_LEN // 4, drawn_lengths).astype(jnp.int32)


def block_scale(key, extent, cuts, smallest, high):
    def one(dim, shards_of):
        heights = jax.random.uniform(jax.random.fold_in(jax.random.fold_in(key, 6), dim), (shards_of,), jnp.float32, smallest / len(cuts), high / len(cuts))
        return jnp.repeat(jnp.exp(heights), extent[dim] // shards_of).reshape((-1,) + (1,) * (len(extent) - dim - 1))

    factor_of = one(*cuts[0])
    for cut in cuts[1:]:
        factor_of = factor_of * one(*cut)
    return factor_of


def routed_block(key, own, number, rows, number_of, top, bound, lean):
    sequence = jax.random.permutation(key, number_of)
    packed, common = portions_of(number_of, rows * top, bound, lean, True), portions_of(number_of, rows * top, bound, lean, False)
    places = jnp.arange(number_of)

    def named(sizes, rotation):
        used = int((sizes > 0).sum())
        fixed = max(1, used // 4)
        moved = fixed + (places - fixed + rotation * (used - fixed)) % max(1, number_of - fixed)
        return jnp.zeros((number_of,), jnp.int32).at[sequence[jnp.where(places < fixed, places, moved)]].set(jnp.asarray(sizes, jnp.int32))

    sizes = jnp.where(number % 4 == 0, named(packed, number // 4), named(common, number - number // 4 - 1))
    mixed = jax.random.permutation(jax.random.fold_in(own, 3), number_of)
    giver, sink = mixed[0:number_of // 2 * 2:2], mixed[1:number_of // 2 * 2:2]
    room = jnp.minimum(sizes[giver] - 1, bound - sizes[sink]) // 2
    room = jnp.where((giver == sequence[0]) | (sink == sequence[0]) | (sizes[sink] == 0), 0, jnp.maximum(room, 0))
    moved = jax.random.randint(jax.random.fold_in(own, 4), (number_of // 2,), 0, 1 << 20) % (room + 1)
    sizes = sizes.at[giver].add(-moved).at[sink].add(moved)
    labels = jnp.searchsorted(jnp.cumsum(sizes), jnp.arange(rows * top), side="right").astype(jnp.int32)
    listing = labels.reshape(top, rows).T
    listing = listing[jax.random.permutation(jax.random.fold_in(own, 1), rows)]
    rotation = jax.random.randint(jax.random.fold_in(own, 2), (rows, 1), 0, top)
    return jnp.take_along_axis(listing, (jnp.arange(top)[None, :] + rotation) % top, axis=1)


def portions_of(amount, total, reach, lean, full):
    loads = [(1 << 20) // math.isqrt(rank ** lean) + 1 for rank in range(1, amount + 1)]
    largest = reach if full else min(reach, max(-(-total // amount), total * loads[0] // sum(loads)))
    least = 1 if total - largest >= amount - 1 else 0
    holding, surplus = [largest] + [least] * (amount - 1), total - largest - least * (amount - 1)
    while surplus > 0:
        free = [i for i in range(1, amount) if holding[i] < largest] or [i for i in range(1, amount) if holding[i] < reach]
        mass, remaining = sum([loads[i] for i in free]), surplus
        for i in free:
            extra = min(reach - holding[i], max(1, remaining * loads[i] // mass), surplus)
            holding[i] = holding[i] + extra
            surplus = surplus - extra
    return np.array(holding)


def bell_draw(rng, shape, width, limit, cuts=(), held_as=jnp.bfloat16):
    entries = width * jax.random.normal(rng, shape, jnp.float32)
    if cuts:
        entries = entries * block_scale(rng, shape, cuts, -0.22, 0.18)
    return jnp.clip(entries, -limit, limit).astype(held_as)


def setup_inputs(seed: int = 0) -> dict:
    keys = jax.random.split(jax.random.key(seed), 27)
    layer_input = bell_draw(keys[0], (TOKENS, D), 1.0, 6.0, ((0, 32),))
    cotangent = bell_draw(keys[1], (TOKENS, D), 1.0, 6.0, ((0, 32),), jnp.float32)
    lengths = draw_lengths(jax.random.fold_in(keys[26], 71), 0)
    routes_a_keys = jax.random.split(jax.random.fold_in(keys[3], 1), TOKENS // HALF)
    routes_a_turns = jax.random.permutation(jax.random.fold_in(keys[3], 3), TOKENS // HALF)
    routes_a = jax.vmap(lambda own, number: routed_block(jax.random.fold_in(keys[3], 2), own, number, HALF, EXPERTS, TOP, CAP, 2))(routes_a_keys, routes_a_turns).reshape((TOKENS, TOP))
    routes_b_keys = jax.random.split(jax.random.fold_in(keys[4], 1), TOKENS // HALF)
    routes_b_turns = jax.random.permutation(jax.random.fold_in(keys[4], 3), TOKENS // HALF)
    routes_b = jax.vmap(lambda own, number: routed_block(jax.random.fold_in(keys[4], 2), own, number, HALF, EXPERTS, TOP, CAP, 2))(routes_b_keys, routes_b_turns).reshape((TOKENS, TOP))
    mixer_in = bell_draw(keys[5], (D, PIN), D ** -0.5, 0.15625, ((0, 32),))
    mixer_out = bell_draw(keys[6], (D, DI), DI ** -0.5, 0.109375, ((0, 32),))
    router_a = bell_draw(keys[7], (D, EXPERTS), (4 * D) ** -0.5, 0.078125, ((0, 32),))
    shared_in_a = bell_draw(keys[8], (D, 2 * FS), D ** -0.5, 0.15625, ((0, 32),))
    shared_out_a = bell_draw(keys[9], (D, FS), FS ** -0.5, 0.1875, ((0, 32),))
    expert_in_a = bell_draw(keys[10], (EXPERTS, D, 2 * FE), D ** -0.5, 0.15625, ((0, 8), (1, 4)))
    expert_out_a = bell_draw(keys[11], (EXPERTS, D, FE), FE ** -0.5, 0.25, ((0, 8), (1, 4)))
    attn_qkv = bell_draw(keys[12], (D, QKV), D ** -0.5, 0.15625, ((0, 32),))
    attn_out = bell_draw(keys[13], (D, QD), (QD // 8) ** -0.5, 0.4375, ((0, 32),))
    router_b = bell_draw(keys[14], (D, EXPERTS), (4 * D) ** -0.5, 0.078125, ((0, 32),))
    shared_in_b = bell_draw(keys[15], (D, 2 * FS), D ** -0.5, 0.15625, ((0, 32),))
    shared_out_b = bell_draw(keys[16], (D, FS), FS ** -0.5, 0.1875, ((0, 32),))
    expert_in_b = bell_draw(keys[17], (EXPERTS, D, 2 * FE), D ** -0.5, 0.15625, ((0, 8), (1, 4)))
    expert_out_b = bell_draw(keys[18], (EXPERTS, D, FE), FE ** -0.5, 0.25, ((0, 8), (1, 4)))
    norm_gains = jnp.clip(1.0 + 0.1 * jax.random.normal(keys[19], (4, D), jnp.float32), 0.5, 1.5)
    mixer_gain = jnp.clip(1.0 + 0.1 * jax.random.normal(keys[20], (DI,), jnp.float32), 0.5, 1.5)
    conv_weight = bell_draw(keys[21], (KCONV, CONVCH), KCONV ** -0.5, 3.0, (), jnp.float32)
    conv_bias = bell_draw(keys[22], (CONVCH,), 0.5, 3.0, (), jnp.float32)
    decay_log = jnp.clip(jax.random.uniform(keys[23], (MHEADS,), jnp.float32, -4.5, 0.5), -4.5, 0.5)
    step_bias = jnp.clip(jax.random.uniform(keys[24], (MHEADS,), jnp.float32, -4.0, -0.5), -4.0, -0.5)
    skip_gain = jnp.clip(jax.random.uniform(keys[25], (MHEADS,), jnp.float32, 0.5, 1.5), 0.5, 1.5)
    return dict(layer_input=layer_input, cotangent=cotangent, lengths=lengths, routes_a=routes_a, routes_b=routes_b, mixer_in=mixer_in, mixer_out=mixer_out, router_a=router_a, shared_in_a=shared_in_a, shared_out_a=shared_out_a, expert_in_a=expert_in_a, expert_out_a=expert_out_a, attn_qkv=attn_qkv, attn_out=attn_out, router_b=router_b, shared_in_b=shared_in_b, shared_out_b=shared_out_b, expert_in_b=expert_in_b, expert_out_b=expert_out_b, norm_gains=norm_gains, mixer_gain=mixer_gain, conv_weight=conv_weight, conv_bias=conv_bias, decay_log=decay_log, step_bias=step_bias, skip_gain=skip_gain)


EPS = 1e-05
HIGH = lax.Precision.HIGHEST

@jax.custom_vjp
def low(v):
    return lax.optimization_barrier(v.astype(jnp.bfloat16)).astype(jnp.float32)

@jax.custom_vjp
def low_back(v):
    return v

def low_keep(v):
    return (low(v), None)

def low_pass(kept, grad):
    return (grad,)

def back_keep(v):
    return (v, None)

def back_low(kept, grad):
    return (low(grad),)
low.defvjp(low_keep, low_pass)
low_back.defvjp(back_keep, back_low)

def matmul(left, right):
    return jnp.dot(left, right, precision=HIGH, preferred_element_type=jnp.float32)

def silu_of(values):
    return values * jax.nn.sigmoid(values)

def softplus_of(values):
    return jnp.log1p(jnp.exp(values))

def rms_norm(values, norm_gain):
    return values * lax.rsqrt(lax.optimization_barrier(jnp.mean(values * values, axis=-1, keepdims=True)) + EPS) * norm_gain

def softmax_of(scores):
    largest = lax.optimization_barrier(jnp.max(scores, axis=-1, keepdims=True))
    raised = jnp.exp(scores - largest)
    return raised / lax.optimization_barrier(jnp.sum(raised, axis=-1, keepdims=True))

def swiglu(gate_up):
    half_width = gate_up.shape[-1] // 2
    return silu_of(gate_up[..., :half_width]) * gate_up[..., half_width:]

def state_mix(inputs, decay_rate, skip_gain):
    heads_in, b_rows, c_rows, step_size = inputs
    length = heads_in.shape[0]
    log_decay = jnp.cumsum(step_size * decay_rate, axis=0)
    spread = log_decay[:, None, :] - log_decay[None, :, :]
    causal = (jnp.arange(length)[:, None] >= jnp.arange(length)[None, :])[:, :, None]
    decay_mat = jnp.where(causal, jnp.exp(jnp.where(causal, spread, 0.0)), 0.0)
    intersection = jnp.dot(c_rows, b_rows.T, precision=HIGH, preferred_element_type=jnp.float32)
    mixing = intersection[:, :, None] * decay_mat * step_size[None, :, :]
    mixed_heads = jnp.einsum('tsh,shp->thp', mixing, heads_in, precision=HIGH)
    return mixed_heads + skip_gain[None, :, None] * heads_in

def mixer_core(projected, params):
    slot_count, length = (projected.shape[0], projected.shape[1])
    gate_part = projected[..., :DI]
    conv_part = projected[..., DI:DI + CONVCH]
    step_raw = projected[..., DI + CONVCH:]
    padded = jnp.pad(conv_part, ((0, 0), (KCONV - 1, 0), (0, 0)))
    conv_out = params['conv_bias'] + padded[:, 0:length] * params['conv_weight'][0]
    for tap_index in range(1, KCONV):
        conv_out = conv_out + padded[:, tap_index:tap_index + length] * params['conv_weight'][tap_index]
    conv_out = silu_of(conv_out)
    heads_in = conv_out[..., :DI].reshape(slot_count, length, MHEADS, MHDIM)
    b_rows = conv_out[..., DI:DI + NSTATE]
    c_rows = conv_out[..., DI + NSTATE:]
    step_size = softplus_of(step_raw + params['step_bias'])
    decay_rate = -jnp.exp(params['decay_log'])
    skip_gain = params['skip_gain']
    per_slot = jax.checkpoint(lambda inputs: state_mix(inputs, decay_rate, skip_gain))
    mixed_heads = lax.map(per_slot, (heads_in, b_rows, c_rows, step_size))
    gated_out = mixed_heads.reshape(slot_count, length, DI) * silu_of(gate_part)
    return rms_norm(gated_out, params['mixer_gain'])

def route_weights(logits, routes, valid_rows):
    chosen = jnp.take_along_axis(logits, routes, axis=1)
    return softmax_of(chosen) * valid_rows[:, None]

def experts_block(hidden, routes, valid_rows, norm_gain, router, shared_in, shared_out, expert_in, expert_out):
    normed = low(rms_norm(hidden, norm_gain))
    logits = low_back(matmul(normed, router))
    weights = route_weights(logits, routes, valid_rows)
    onehot = (routes[:, :, None] == jnp.arange(EXPERTS)[None, None, :]).astype(jnp.float32)
    dense_weights = lax.optimization_barrier(jnp.sum(weights[:, :, None] * onehot, axis=1))

    def one_expert(running, inputs):
        in_matrix, out_matrix, column = inputs
        copied = low_back(normed)
        gate_up = low_back(matmul(copied, in_matrix))
        inner_act = low(swiglu(gate_up))
        result = low(low_back(matmul(inner_act, out_matrix.T)))
        return (running + column[:, None] * result, None)
    routed = lax.scan(jax.checkpoint(one_expert), jnp.zeros_like(hidden), (expert_in, expert_out, dense_weights.T))[0]
    shared_gu = low_back(matmul(normed, shared_in))
    shared_mid = low(swiglu(shared_gu))
    shared_res = low_back(matmul(shared_mid, shared_out.T))
    return hidden + routed + shared_res

def attend_slot(inputs):
    queries, key_rows, value_rows = inputs
    length = queries.shape[0]
    raw_scores = jnp.einsum('tkgd,skd->kgts', queries, key_rows, precision=HIGH)
    causal = jnp.arange(length)[:, None] >= jnp.arange(length)[None, :]
    scores = jnp.where(causal, low_back(raw_scores) * AHDIM ** (-0.5), -1e+30)
    attn_probs = softmax_of(scores)
    return jnp.einsum('kgts,skd->tkgd', low(attn_probs), value_rows, precision=HIGH)

def attention_block(hidden, norm_gain, attn_qkv, attn_out):
    slot_count, length = (hidden.shape[0], hidden.shape[1])
    normed = low(rms_norm(hidden, norm_gain))
    qkv_rows = low(low_back(matmul(normed.reshape(-1, D), attn_qkv))).reshape(slot_count, length, QKV)
    queries = qkv_rows[..., :QD].reshape(slot_count, length, KVHEADS, AHEADS // KVHEADS, AHDIM)
    key_rows = qkv_rows[..., QD:QD + KVD].reshape(slot_count, length, KVHEADS, AHDIM)
    value_rows = qkv_rows[..., QD + KVD:].reshape(slot_count, length, KVHEADS, AHDIM)
    attended = lax.map(jax.checkpoint(attend_slot), (queries, key_rows, value_rows))
    mixed_rows = low(low_back(attended)).reshape(-1, QD)
    return hidden + low_back(matmul(mixed_rows, attn_out.T)).reshape(hidden.shape)

def forward(params, hidden, routes_one, routes_two, valid_rows):
    slot_count, length = (hidden.shape[0], hidden.shape[1])
    gains = params['norm_gains']
    normed = low(rms_norm(hidden, gains[0]))
    projected = low_back(matmul(normed.reshape(-1, D), params['mixer_in'])).reshape(slot_count, length, PIN)
    mixer_norm = low(mixer_core(projected, params))
    branch = low_back(matmul(mixer_norm.reshape(-1, DI), params['mixer_out'].T))
    after_mixer = hidden.reshape(-1, D) + branch
    flat_valid = valid_rows.reshape(-1)
    after_moe = experts_block(after_mixer, routes_one, flat_valid, gains[1], params['router_a'], params['shared_in_a'], params['shared_out_a'], params['expert_in_a'], params['expert_out_a'])
    after_attention = attention_block(after_moe.reshape(slot_count, length, D), gains[2], params['attn_qkv'], params['attn_out'])
    return experts_block(after_attention.reshape(-1, D), routes_two, flat_valid, gains[3], params['router_b'], params['shared_in_b'], params['shared_out_b'], params['expert_in_b'], params['expert_out_b'])

def reference(layer_input, cotangent, lengths, routes_a, routes_b, mixer_in, mixer_out, router_a, shared_in_a, shared_out_a, expert_in_a, expert_out_a, attn_qkv, attn_out, router_b, shared_in_b, shared_out_b, expert_in_b, expert_out_b, norm_gains, mixer_gain, conv_weight, conv_bias, decay_log, step_bias, skip_gain):
    raw_params = {'mixer_in': mixer_in, 'mixer_out': mixer_out, 'router_a': router_a, 'shared_in_a': shared_in_a, 'shared_out_a': shared_out_a, 'expert_in_a': expert_in_a, 'expert_out_a': expert_out_a, 'attn_qkv': attn_qkv, 'attn_out': attn_out, 'router_b': router_b, 'shared_in_b': shared_in_b, 'shared_out_b': shared_out_b, 'expert_in_b': expert_in_b, 'expert_out_b': expert_out_b, 'norm_gains': norm_gains, 'mixer_gain': mixer_gain, 'conv_weight': conv_weight, 'conv_bias': conv_bias, 'decay_log': decay_log, 'step_bias': step_bias, 'skip_gain': skip_gain}
    params = jax.tree.map(lambda array: array.astype(jnp.float32), raw_params)
    per_group = math.gcd(SLOTS, max(1, 4096 // SLOT_LEN))
    groups = SLOTS // per_group
    group_tokens = per_group * SLOT_LEN
    hidden = layer_input.astype(jnp.float32).reshape(groups, per_group, SLOT_LEN, D)
    valid_all = (jnp.arange(SLOT_LEN)[None, :] < lengths[:, None]).astype(jnp.float32)
    valid_all = valid_all.reshape(groups, per_group, SLOT_LEN)
    out_grad = cotangent.astype(jnp.float32).reshape(groups, per_group, SLOT_LEN, D) * valid_all[..., None]
    routes_one = routes_a.reshape(groups, group_tokens, TOP)
    routes_two = routes_b.reshape(groups, group_tokens, TOP)

    def one_group(totals, inputs):
        block_in, block_valid, block_grad, block_one, block_two = inputs

        def run(prm, hid):
            return forward(prm, hid, block_one, block_two, block_valid)
        output, pullback = jax.vjp(run, params, block_in)
        grad_params, grad_in = pullback(block_grad.reshape(output.shape))
        return (jax.tree.map(jnp.add, totals, grad_params), (output, grad_in))
    zeros = jax.tree.map(jnp.zeros_like, params)
    totals, (outputs, grads_in) = lax.scan(one_group, zeros, (hidden, valid_all, out_grad, routes_one, routes_two))
    return (outputs.reshape(TOKENS, D), grads_in.reshape(TOKENS, D), totals['mixer_in'], totals['mixer_out'], totals['router_a'], totals['shared_in_a'], totals['shared_out_a'], totals['expert_in_a'], totals['expert_out_a'], totals['attn_qkv'], totals['attn_out'], totals['router_b'], totals['shared_in_b'], totals['shared_out_b'], totals['expert_in_b'], totals['expert_out_b'], totals['norm_gains'], totals['mixer_gain'], totals['conv_weight'], totals['conv_bias'], totals['decay_log'], totals['step_bias'], totals['skip_gain'])
```

```python
import functools

import jax
import jax.numpy as jnp
from jax import lax
from jax.experimental import pallas as pl
from jax.experimental.pallas import tpu as pltpu
from jax.sharding import PartitionSpec as P

MHEADS = 48
MHDIM = 64
NSTATE = 128
KCONV = 4
AHEADS = 12
KVHEADS = 4
AHDIM = 128
SLOT_LEN = 256
HALF = 128
CAP = 60
DI = 3072
CONVCH = 3328
QD = 1536
KVD = 512
QKV = 2560

EPS = 1e-05
HIGH = lax.Precision.HIGHEST
FLOAT = jnp.float32
BRAIN = jnp.bfloat16
MESH = pl.DeviceIdType.MESH
BOTH = ("dp", "expert")
PICKED = SLOT_LEN // HALF * 64
MIB = 2**20


def matmul(left, right):
    return jnp.dot(left, right, preferred_element_type=FLOAT)


def matmul_nt(left, right):
    return lax.dot_general(left, right, (((1,), (1,)), ((), ())), preferred_element_type=FLOAT)


def matmul_tn(left, right):
    return lax.dot_general(left, right, (((0,), (0,)), ((), ())), preferred_element_type=FLOAT)


def silu_of(values):
    return values * jax.nn.sigmoid(values)


def softplus_of(values):
    return jnp.log1p(jnp.exp(values))


def rms_norm(values, norm_gain):
    return values * lax.rsqrt(jnp.mean(values * values, axis=-1, keepdims=True) + EPS) * norm_gain


def whole_spec(shape):
    return pl.BlockSpec(shape, lambda *at: (0,) * len(shape), pipeline_mode=pl.Buffered(1))


def expert_place(group):
    me = lax.axis_index("expert")
    return me // 2, lax.rem(me, 2)

def greet(z, x, line):
    barrier = pltpu.get_barrier_semaphore()
    def hello(device):
        pl.semaphore_signal(barrier, inc=1, device_id={"expert": device}, device_id_type=MESH)
    hello(2 * z + 1 - x)
    @pl.when(z > 0)
    def _():
        hello(2 * (z - 1) + x)
    @pl.when(z < line - 1)
    def _():
        hello(2 * (z + 1) + x)
    pl.semaphore_wait(barrier, 1 + jnp.where(z > 0, 1, 0) + jnp.where(z < line - 1, 1, 0))

def spread_kernel(count, group, *refs):
    ins, outs = refs[:count], refs[count:2 * count]
    up_sems, down_sems, cross_sems, recv_sems, own_sems = refs[2 * count:]
    line = group // 2
    z, x = expert_place(group)
    greet(z, x, line)

    def copy(i, src, place, sem, device):
        return pltpu.make_async_remote_copy(
            src_ref=src, dst_ref=outs[i].at[place], send_sem=sem, recv_sem=recv_sems.at[i, place],
            device_id={"expert": device}, device_id_type=MESH)

    def moves(i, s, rising):
        zz = z - s if rising else z + s
        place = 2 * zz + x
        src = ins[i] if s == 0 else outs[i].at[place]
        up = copy(i, src, place, up_sems.at[i, s], 2 * (z + 1) + x)
        down = copy(i, src, place, down_sems.at[i, s], 2 * (z - 1) + x)
        cross = copy(i, src, place, cross_sems.at[i, zz], 2 * z + 1 - x)
        return up, down, cross

    for i in range(count):
        pltpu.make_async_copy(ins[i], outs[i].at[2 * z + x], own_sems.at[i]).start()
    for s in range(line):
        for rising in (True, False) if s else (True,):
            valid = (z - s >= 0) if rising else (z + s < line)
            @pl.when(valid)
            def _():
                for i in range(count):
                    up, down, cross = moves(i, s, rising)
                    if s:
                        cross.wait_recv()
                    if rising:
                        pl.when(z < line - 1)(up.start)
                    if not rising or s == 0:
                        pl.when(z > 0)(down.start)
                    cross.start()
    for i in range(count):
        for zz in range(line):
            place = 2 * zz + 1 - x
            copy(i, ins[i], place, own_sems.at[i], 2 * z + 1 - x).wait_recv()
        pltpu.make_async_copy(ins[i], outs[i].at[2 * z + x], own_sems.at[i]).wait()
    for s in range(line):
        for rising in (True, False) if s else (True,):
            valid = (z - s >= 0) if rising else (z + s < line)
            @pl.when(valid)
            def _():
                for i in range(count):
                    up, down, cross = moves(i, s, rising)
                    if rising:
                        pl.when(z < line - 1)(up.wait_send)
                    if not rising or s == 0:
                        pl.when(z > 0)(down.wait_send)
                    cross.wait_send()

def spread(arrays, group, number):
    n = len(arrays); line = group // 2
    return pl.pallas_call(
        functools.partial(spread_kernel, n, group),
        out_shape=[jax.ShapeDtypeStruct((group,) + a.shape, a.dtype) for a in arrays],
        in_specs=[pl.BlockSpec(memory_space=pl.ANY)] * n,
        out_specs=[pl.BlockSpec(memory_space=pl.ANY)] * n,
        scratch_shapes=[
            pltpu.SemaphoreType.DMA((n, line)), pltpu.SemaphoreType.DMA((n, line)),
            pltpu.SemaphoreType.DMA((n, line)), pltpu.SemaphoreType.DMA((n, group)),
            pltpu.SemaphoreType.DMA((n,))],
        compiler_params=pltpu.CompilerParams(collective_id=number, has_side_effects=True),
        name="spread%d" % number,
    )(*arrays)

def gather_sum_kernel(count, group, *refs):
    ins, outs = refs[:count], refs[count:2 * count]
    line = group // 2
    bufs = refs[2 * count:2 * count + 4 * count]
    own_sems, cross_send, cross_recv, up_send, up_recv, down_send, down_recv = refs[6 * count:]
    held = [bufs[4 * i] for i in range(count)]
    crossed = [bufs[4 * i + 1] for i in range(count)]
    below = [bufs[4 * i + 2] for i in range(count)]
    above = [bufs[4 * i + 3] for i in range(count)]
    z, x = expert_place(group)
    greet(z, x, line)

    def own(i, d):
        return pltpu.make_async_copy(ins[i].at[2 * d + x], held[i].at[d], own_sems.at[i, d])

    def cross(i, d):
        return pltpu.make_async_remote_copy(
            src_ref=ins[i].at[2 * d + 1 - x], dst_ref=crossed[i].at[d], send_sem=cross_send.at[i, d],
            recv_sem=cross_recv.at[i, d], device_id={"expert": 2 * z + 1 - x}, device_id_type=MESH)

    def rise(i, d):
        return pltpu.make_async_remote_copy(
            src_ref=held[i].at[d], dst_ref=below[i].at[d], send_sem=up_send.at[i, d],
            recv_sem=up_recv.at[i, d], device_id={"expert": 2 * (z + 1) + x}, device_id_type=MESH)

    def fall(i, d):
        return pltpu.make_async_remote_copy(
            src_ref=held[i].at[d], dst_ref=above[i].at[d], send_sem=down_send.at[i, d],
            recv_sem=down_recv.at[i, d], device_id={"expert": 2 * (z - 1) + x}, device_id_type=MESH)

    def order(act):
        for k in range(line):
            pl.when(line - 1 - k > z)(functools.partial(act, line - 1 - k))
            pl.when(k < z)(functools.partial(act, k))
        for k in range(line):
            pl.when(k == z)(functools.partial(act, k))

    def start_cross(d):
        for i in range(count):
            cross(i, d).start()

    def start_own(d):
        for i in range(count):
            own(i, d).start()
    order(start_cross)
    order(start_own)

    def add_rows(i, d, target, sources):
        rows = held[i].shape[1]
        step = min(rows, 16)
        def body(j, carry):
            at = pl.ds(pl.multiple_of(j * step, step), step)
            total = held[i][d, at].astype(FLOAT)
            for source in sources:
                total = total + source[i][d, at].astype(FLOAT)
            if target is None:
                held[i][d, at] = total.astype(held[i].dtype)
            else:
                target[i][at] = total.astype(target[i].dtype)
            return carry
        lax.fori_loop(0, rows // step, body, 0)

    def ready(i, d):
        own(i, d).wait()
        cross(i, d).wait_recv()

    for k in range(line - 1):
        d = line - 1 - k
        @pl.when(d > z)
        def _():
            for i in range(count):
                ready(i, d)
                @pl.when(z > 0)
                def _():
                    rise(i, d).wait_recv()
                    add_rows(i, d, None, [crossed, below])
                @pl.when(z == 0)
                def _():
                    add_rows(i, d, None, [crossed])
                rise(i, d).start()
        d = k
        @pl.when(d < z)
        def _():
            for i in range(count):
                ready(i, d)
                @pl.when(z < line - 1)
                def _():
                    fall(i, d).wait_recv()
                    add_rows(i, d, None, [crossed, above])
                @pl.when(z == line - 1)
                def _():
                    add_rows(i, d, None, [crossed])
                fall(i, d).start()
    for d in range(line):
        @pl.when(d == z)
        def _():
            for i in range(count):
                ready(i, d)
                if d == 0:
                    fall(i, d).wait_recv()
                    add_rows(i, d, outs, [crossed, above])
                elif d == line - 1:
                    rise(i, d).wait_recv()
                    add_rows(i, d, outs, [crossed, below])
                else:
                    fall(i, d).wait_recv()
                    rise(i, d).wait_recv()
                    add_rows(i, d, outs, [crossed, below, above])
    for d in range(line):
        for i in range(count):
            cross(i, d).wait_send()
            pl.when(d > z)(rise(i, d).wait_send)
            pl.when(d < z)(fall(i, d).wait_send)

def gather_sum(arrays, group, number):
    n = len(arrays); line = group // 2
    scratch = []
    for a in arrays:
        scratch += [pltpu.VMEM((line,) + a.shape[1:], a.dtype)] * 4
    return pl.pallas_call(
        functools.partial(gather_sum_kernel, n, group),
        out_shape=[jax.ShapeDtypeStruct(a.shape[1:], FLOAT) for a in arrays],
        in_specs=[pl.BlockSpec(memory_space=pl.ANY)] * n,
        out_specs=[pl.BlockSpec(memory_space=pltpu.VMEM)] * n,
        scratch_shapes=scratch + [pltpu.SemaphoreType.DMA((n, line))] * 7,
        compiler_params=pltpu.CompilerParams(collective_id=number, has_side_effects=True, vmem_limit_bytes=40 * 2**20),
        name="gather_sum%d" % number,
    )(*arrays)


def swap_sum_kernel(steps, value_ref, out_ref, totals, landed, send_sems, recv_sems):
    barrier = pltpu.get_barrier_semaphore()

    def partner(axis, bit):
        me = lax.axis_index(axis)
        return {axis: me + bit * (1 - 2 * lax.rem(me // bit, 2))}

    for axis, bit in steps:
        pl.semaphore_signal(barrier, inc=1, device_id=partner(axis, bit), device_id_type=MESH)
    pl.semaphore_wait(barrier, len(steps))
    totals[0] = value_ref[...]
    for step, (axis, bit) in enumerate(steps):
        copy = pltpu.make_async_remote_copy(
            src_ref=totals.at[step],
            dst_ref=landed.at[step],
            send_sem=send_sems.at[step],
            recv_sem=recv_sems.at[step],
            device_id=partner(axis, bit),
            device_id_type=MESH,
        )
        copy.start()
        copy.wait()
        totals[step + 1] = totals[step] + landed[step]
    out_ref[...] = totals[len(steps)]


def swap_sum(value, number):
    steps = []
    for axis in BOTH:
        bit = 1
        while bit < lax.axis_size(axis):
            steps.append((axis, bit))
            bit *= 2
    vmem = pl.BlockSpec(memory_space=pltpu.VMEM)
    return pl.pallas_call(
        functools.partial(swap_sum_kernel, steps),
        out_shape=jax.ShapeDtypeStruct(value.shape, FLOAT),
        in_specs=[vmem],
        out_specs=vmem,
        scratch_shapes=[
            pltpu.VMEM((len(steps) + 1,) + value.shape, FLOAT),
            pltpu.VMEM((len(steps),) + value.shape, FLOAT),
            pltpu.SemaphoreType.DMA((len(steps),)),
            pltpu.SemaphoreType.DMA((len(steps),)),
        ],
        compiler_params=pltpu.CompilerParams(collective_id=number, has_side_effects=True),
        name="swap_sum",
    )(value)


def state_setup(step_ref, rate_ref, step_t_ref, rate_t_ref, b_ref, c_ref, cum, cum_t, cross):
    length = step_ref.shape[0]
    down = lax.broadcasted_iota(jnp.int32, (length, length), 0)
    along = lax.broadcasted_iota(jnp.int32, (length, length), 1)
    lower = jnp.where(down >= along, 1.0, 0.0)
    upper = jnp.where(down <= along, 1.0, 0.0)
    cum[...] = jnp.dot(
        lower, step_ref[...] * rate_ref[...], precision=HIGH, preferred_element_type=FLOAT
    )
    cum_t[...] = jnp.dot(
        step_t_ref[...] * rate_t_ref[...], upper, precision=HIGH, preferred_element_type=FLOAT
    )
    cross[...] = lax.dot_general(
        c_ref[...], b_ref[...], (((1,), (1,)), ((), ())), precision=HIGH, preferred_element_type=FLOAT
    )


def decay_of(head, cum, cum_t):
    length, heads = cum.shape
    lane = lax.broadcasted_iota(jnp.int32, (length, heads), 1)
    column = jnp.sum(jnp.where(lane == head, cum[...], 0.0), axis=1, keepdims=True)
    spread_out = column - cum_t[pl.ds(head, 1), :]
    down = lax.broadcasted_iota(jnp.int32, (length, length), 0)
    along = lax.broadcasted_iota(jnp.int32, (length, length), 1)
    return jnp.exp(jnp.where(down >= along, spread_out, -1e30))


def state_forward_kernel(
    x_ref, b_ref, c_ref, step_ref, rate_ref, step_t_ref, rate_t_ref, skip_ref, y_ref, cum, cum_t, cross
):
    pair = pl.program_id(0)

    @pl.when(pair == 0)
    def _():
        state_setup(step_ref, rate_ref, step_t_ref, rate_t_ref, b_ref, c_ref, cum, cum_t, cross)

    values = x_ref[...]
    values_low = values.astype(BRAIN)
    total = values * skip_ref[...]
    side = lax.broadcasted_iota(jnp.int32, values.shape, 1) // MHDIM
    for j in range(2):
        head = 2 * pair + j
        mixing = cross[...] * decay_of(head, cum, cum_t) * step_t_ref[pl.ds(head, 1), :]
        part = jnp.dot(mixing.astype(BRAIN), values_low, preferred_element_type=FLOAT)
        total = total + jnp.where(side == j, part, 0.0)
    y_ref[...] = total


def state_specs(length):
    column = lambda place: pl.BlockSpec((length, NSTATE), place)
    return [
        column(lambda i: (0, i)),
        column(lambda i: (0, DI // NSTATE)),
        column(lambda i: (0, DI // NSTATE + 1)),
        whole_spec((length, MHEADS)),
        whole_spec((1, MHEADS)),
        whole_spec((MHEADS, length)),
        whole_spec((MHEADS, 1)),
        pl.BlockSpec((1, 2 * MHDIM), lambda i: (0, i)),
    ]


def state_operands(conv_out, step_size, decay_rate, skip_gain):
    return (
        conv_out,
        conv_out,
        conv_out,
        step_size,
        decay_rate[None, :],
        step_size.T,
        decay_rate[:, None],
        jnp.repeat(skip_gain, MHDIM)[None, :],
    )


def state_forward(conv_out, step_size, decay_rate, skip_gain):
    length = conv_out.shape[0]
    return pl.pallas_call(
        state_forward_kernel,
        grid=(MHEADS // 2,),
        out_shape=jax.ShapeDtypeStruct((length, DI), FLOAT),
        in_specs=state_specs(length),
        out_specs=pl.BlockSpec((length, 2 * MHDIM), lambda i: (0, i)),
        scratch_shapes=[
            pltpu.VMEM((length, MHEADS), FLOAT),
            pltpu.VMEM((MHEADS, length), FLOAT),
            pltpu.VMEM((length, length), FLOAT),
        ],
        compiler_params=pltpu.CompilerParams(vmem_limit_bytes=32 * MIB),
        name="state_forward",
    )(*state_operands(conv_out, step_size, decay_rate, skip_gain))


def state_backward_kernel(
    x_ref, b_ref, c_ref, step_ref, rate_ref, step_t_ref, rate_t_ref, skip_ref, dy_ref,
    dx_ref, db_ref, dc_ref, row_ref, column_ref, cum, cum_t, cross, dcross,
):
    pair = pl.program_id(0)

    @pl.when(pair == 0)
    def _():
        state_setup(step_ref, rate_ref, step_t_ref, rate_t_ref, b_ref, c_ref, cum, cum_t, cross)
        dcross[...] = jnp.zeros_like(dcross)
        row_ref[...] = jnp.zeros_like(row_ref)

    values_low = x_ref[...].astype(BRAIN)
    grads = dy_ref[...]
    total = grads * skip_ref[...]
    side = lax.broadcasted_iota(jnp.int32, grads.shape, 1) // MHDIM
    lane = lax.broadcasted_iota(jnp.int32, row_ref.shape, 1)
    for j in range(2):
        head = 2 * pair + j
        steps = step_t_ref[pl.ds(head, 1), :]
        decay = decay_of(head, cum, cum_t)
        own = jnp.where(side == j, grads, 0.0).astype(BRAIN)
        mixing = cross[...] * decay
        total = total + matmul_tn((mixing * steps).astype(BRAIN), own)
        dmix = matmul_nt(own, values_low)
        dcross[...] += dmix * decay * steps
        weighed = dmix * mixing
        column_ref[pl.ds(head, 1), :] = jnp.sum(weighed, axis=0, keepdims=True)
        row_sum = jnp.sum(weighed * steps, axis=1, keepdims=True)
        row_ref[...] += jnp.where(lane == head, row_sum, 0.0)
    dx_ref[...] = total

    @pl.when(pair == pl.num_programs(0) - 1)
    def _():
        dc_ref[...] = jnp.dot(dcross[...], b_ref[...], precision=HIGH, preferred_element_type=FLOAT)
        db_ref[...] = lax.dot_general(
            dcross[...], c_ref[...], (((0,), (0,)), ((), ())), precision=HIGH, preferred_element_type=FLOAT
        )


def state_backward(conv_out, step_size, decay_rate, skip_gain, grad_mixed):
    length = conv_out.shape[0]
    pair_block = pl.BlockSpec((length, 2 * MHDIM), lambda i: (0, i))
    dx, db, dc, row_sums, column_sums = pl.pallas_call(
        state_backward_kernel,
        grid=(MHEADS // 2,),
        out_shape=[
            jax.ShapeDtypeStruct((length, DI), FLOAT),
            jax.ShapeDtypeStruct((length, NSTATE), FLOAT),
            jax.ShapeDtypeStruct((length, NSTATE), FLOAT),
            jax.ShapeDtypeStruct((length, MHEADS), FLOAT),
            jax.ShapeDtypeStruct((MHEADS, length), FLOAT),
        ],
        in_specs=state_specs(length) + [pair_block],
        out_specs=[
            pair_block,
            pl.BlockSpec((length, NSTATE), lambda i: (0, 0)),
            pl.BlockSpec((length, NSTATE), lambda i: (0, 0)),
            pl.BlockSpec((length, MHEADS), lambda i: (0, 0)),
            pl.BlockSpec((MHEADS, length), lambda i: (0, 0)),
        ],
        scratch_shapes=[
            pltpu.VMEM((length, MHEADS), FLOAT),
            pltpu.VMEM((MHEADS, length), FLOAT),
            pltpu.VMEM((length, length), FLOAT),
            pltpu.VMEM((length, length), FLOAT),
        ],
        compiler_params=pltpu.CompilerParams(vmem_limit_bytes=32 * MIB),
        name="state_backward",
    )(*state_operands(conv_out, step_size, decay_rate, skip_gain), grad_mixed)
    column_sums = column_sums.T
    dcum = row_sums - column_sums * step_size
    places = jnp.arange(length)
    upper = (places[:, None] <= places[None, :]).astype(FLOAT)
    drate_step = jnp.dot(upper, dcum, precision=HIGH, preferred_element_type=FLOAT)
    grad_step = column_sums + drate_step * decay_rate
    grad_decay_log = jnp.sum(drate_step * step_size, axis=0) * decay_rate
    return dx, db, dc, grad_step, grad_decay_log


def convolve(conv_in, conv_weight, conv_bias):
    length = conv_in.shape[0]
    padded = jnp.pad(conv_in, ((KCONV - 1, 0), (0, 0)))
    total = conv_bias + padded[0:length] * conv_weight[0]
    for tap in range(1, KCONV):
        total = total + padded[tap : tap + length] * conv_weight[tap]
    return silu_of(total)


def gated_norm(mixed, gate_z, mixer_gain):
    return rms_norm(mixed * silu_of(gate_z), mixer_gain)


def step_of(step_raw, step_bias):
    return softplus_of(step_raw + step_bias)


def mixer_forward(hidden, norm_gain, mixer_in, mixer_out, small):
    normed, norm_back = jax.vjp(rms_norm, hidden, norm_gain)
    normed_low = normed.astype(BRAIN)
    projected = matmul(normed_low, mixer_in)
    gate_z = projected[:, :DI]
    conv_in = projected[:, DI : DI + CONVCH]
    step_raw = projected[:, DI + CONVCH :]
    conv_out, conv_back = jax.vjp(convolve, conv_in, small["conv_weight"], small["conv_bias"])
    step_size, step_back = jax.vjp(step_of, step_raw, small["step_bias"])
    decay_rate = -jnp.exp(small["decay_log"])
    mixed = state_forward(conv_out, step_size, decay_rate, small["skip_gain"])
    mixer_norm, gated_back = jax.vjp(gated_norm, mixed, gate_z, small["mixer_gain"])
    mixer_low = mixer_norm.astype(BRAIN)
    output = hidden + matmul_nt(mixer_low, mixer_out)
    saved = (norm_back, normed_low, conv_out, conv_back, step_size, step_back, decay_rate, gated_back, mixer_low)
    return output, saved


def mixer_backward(grad_out, saved, mixer_in, mixer_out, small):
    norm_back, normed_low, conv_out, conv_back, step_size, step_back, decay_rate, gated_back, mixer_low = saved
    grad_low = grad_out.astype(BRAIN)
    grad_mixer_out = matmul_tn(grad_low, mixer_low).astype(BRAIN)
    grad_mixed, grad_gate, grad_mixer_gain = gated_back(matmul(grad_low, mixer_out))
    dx, db, dc, grad_step, grad_decay_log = state_backward(
        conv_out, step_size, decay_rate, small["skip_gain"], grad_mixed
    )
    grad_skip = jnp.sum(jnp.sum(grad_mixed * conv_out[:, :DI], axis=0).reshape(MHEADS, MHDIM), axis=1)
    grad_conv_in, grad_conv_weight, grad_conv_bias = conv_back(jnp.concatenate([dx, db, dc], axis=1))
    grad_step_raw, grad_step_bias = step_back(grad_step)
    grad_proj = jnp.concatenate([grad_gate, grad_conv_in, grad_step_raw], axis=1).astype(BRAIN)
    grad_mixer_in = matmul_tn(normed_low, grad_proj).astype(BRAIN)
    grad_hidden, grad_gain = norm_back(matmul_nt(grad_proj, mixer_in))
    grad_small = (
        grad_mixer_gain, grad_conv_weight, grad_conv_bias, grad_decay_log, grad_step_bias, grad_skip
    )
    return grad_out + grad_hidden, grad_gain, grad_mixer_in, grad_mixer_out, grad_small


def pick_rows(gates):
    tokens = gates.shape[1]
    down = lax.broadcasted_iota(jnp.int32, (tokens, tokens), 0)
    along = lax.broadcasted_iota(jnp.int32, (tokens, tokens), 1)
    upper = jnp.where(down <= along, 1.0, 0.0).astype(BRAIN)
    live = jnp.where(gates != 0.0, 1.0, 0.0)
    place = jnp.dot(
        jnp.broadcast_to(live, (8, tokens)).astype(BRAIN), upper, preferred_element_type=FLOAT
    )[0:1] - 1.0
    ranks = lax.broadcasted_iota(jnp.int32, (PICKED, tokens), 0).astype(FLOAT)
    return (ranks == place) & (live > 0.0)


def expert_forward_kernel(x_ref, g_ref, in_ref, out_ref, sin_ref, sout_ref, y_ref, xe_ref, gu_ref, sgu_ref):
    rows = x_ref[0]
    shared_gu = jnp.dot(rows, sin_ref[...], preferred_element_type=FLOAT)
    half = shared_gu.shape[1] // 2
    shared_mid = (silu_of(shared_gu[:, :half]) * shared_gu[:, half:]).astype(BRAIN)
    sgu_ref[0] = shared_gu.astype(sgu_ref.dtype)
    total = matmul_nt(shared_mid, sout_ref[...])
    for e in range(in_ref.shape[0]):
        gates = g_ref[0, e : e + 1, :]
        hit = pick_rows(gates)
        picked = jnp.dot(
            jnp.where(hit, 1.0, 0.0).astype(BRAIN), rows, preferred_element_type=FLOAT
        ).astype(BRAIN)
        gate_up = jnp.dot(picked, in_ref[e], preferred_element_type=FLOAT)
        width = gate_up.shape[1] // 2
        inner = (silu_of(gate_up[:, :width]) * gate_up[:, width:]).astype(BRAIN)
        result = matmul_nt(inner, out_ref[e]).astype(BRAIN)
        total = total + matmul_tn(jnp.where(hit, gates, 0.0).astype(BRAIN), result)
        xe_ref[e, 0] = picked
        gu_ref[e, 0] = gate_up.astype(gu_ref.dtype)
    y_ref[0] = total.astype(y_ref.dtype)


def expert_forward(rows, gates, expert_in, expert_out, shared_in, shared_out):
    group, tokens, width = rows.shape
    local = expert_in.shape[0]
    inner = expert_in.shape[2]
    by_slot = lambda *shape: pl.BlockSpec((1,) + shape, lambda s: (s,) + (0,) * len(shape))
    by_pair = lambda *shape: pl.BlockSpec((local, 1) + shape, lambda s: (0, s) + (0,) * len(shape))
    return pl.pallas_call(
        expert_forward_kernel,
        grid=(group,),
        out_shape=[
            jax.ShapeDtypeStruct(rows.shape, BRAIN),
            jax.ShapeDtypeStruct((local, group, PICKED, width), BRAIN),
            jax.ShapeDtypeStruct((local, group, PICKED, inner), BRAIN),
            jax.ShapeDtypeStruct((group, tokens, shared_in.shape[1]), BRAIN),
        ],
        in_specs=[
            by_slot(tokens, width),
            by_slot(local, tokens),
            whole_spec(expert_in.shape),
            whole_spec(expert_out.shape),
            whole_spec(shared_in.shape),
            whole_spec(shared_out.shape),
        ],
        out_specs=[
            by_slot(tokens, width),
            by_pair(PICKED, width),
            by_pair(PICKED, inner),
            by_slot(tokens, shared_in.shape[1]),
        ],
        compiler_params=pltpu.CompilerParams(vmem_limit_bytes=52 * MIB),
        name="expert_forward",
    )(rows, gates, expert_in, expert_out, shared_in, shared_out)


def swiglu_back(gate, up, grad):
    sig = jax.nn.sigmoid(gate)
    act = gate * sig
    return grad * up * (sig + act * (1.0 - sig)), grad * act, act * up


def expert_backward_kernel(
    d_ref, g_ref, gu_ref, sgu_ref, in_ref, out_ref, sin_ref, sout_ref,
    dx_ref, dg_ref, dgu_ref, dres_ref, mid_ref, dsgu_ref, smid_ref,
):
    grads = d_ref[0]
    shared_gu = sgu_ref[0].astype(FLOAT)
    half = shared_gu.shape[1] // 2
    dmid = jnp.dot(grads, sout_ref[...], preferred_element_type=FLOAT)
    dgate, dup, shared_mid = swiglu_back(shared_gu[:, :half], shared_gu[:, half:], dmid)
    shared_d = jnp.concatenate([dgate, dup], axis=1).astype(BRAIN)
    dsgu_ref[0] = shared_d
    smid_ref[0] = shared_mid.astype(BRAIN)
    total = matmul_nt(shared_d, sin_ref[...])
    for e in range(in_ref.shape[0]):
        gates = g_ref[0, e : e + 1, :]
        hit = pick_rows(gates)
        chosen = jnp.where(hit, 1.0, 0.0).astype(BRAIN)
        weight = jnp.sum(jnp.where(hit, gates, 0.0), axis=1, keepdims=True)
        picked = jnp.dot(chosen, grads, preferred_element_type=FLOAT)
        dres_ref[e, 0] = (picked * weight).astype(BRAIN)
        raw = jnp.dot(picked.astype(BRAIN), out_ref[e], preferred_element_type=FLOAT)
        gate_up = gu_ref[e, 0].astype(FLOAT)
        width = gate_up.shape[1] // 2
        dgate, dup, inner = swiglu_back(gate_up[:, :width], gate_up[:, width:], raw * weight)
        inner_low = inner.astype(BRAIN)
        mid_ref[e, 0] = inner_low
        dweight = jnp.sum(raw * inner_low.astype(FLOAT), axis=1, keepdims=True)
        dg_ref[0, e : e + 1, :] = jnp.sum(jnp.where(hit, dweight, 0.0), axis=0, keepdims=True)
        dgu = jnp.concatenate([dgate, dup], axis=1).astype(BRAIN)
        dgu_ref[e, 0] = dgu
        back = matmul_nt(dgu, in_ref[e]).astype(BRAIN)
        total = total + matmul_tn(chosen, back)
    dx_ref[0] = total.astype(dx_ref.dtype)


def expert_backward(grads, gates, gate_up, shared_gu, expert_in, expert_out, shared_in, shared_out):
    group, tokens, width = grads.shape
    local = expert_in.shape[0]
    inner = expert_in.shape[2]
    by_slot = lambda *shape: pl.BlockSpec((1,) + shape, lambda s: (s,) + (0,) * len(shape))
    by_pair = lambda *shape: pl.BlockSpec((local, 1) + shape, lambda s: (0, s) + (0,) * len(shape))
    return pl.pallas_call(
        expert_backward_kernel,
        grid=(group,),
        out_shape=[
            jax.ShapeDtypeStruct(grads.shape, BRAIN),
            jax.ShapeDtypeStruct((group, local, tokens), FLOAT),
            jax.ShapeDtypeStruct((local, group, PICKED, inner), BRAIN),
            jax.ShapeDtypeStruct((local, group, PICKED, width), BRAIN),
            jax.ShapeDtypeStruct((local, group, PICKED, inner // 2), BRAIN),
            jax.ShapeDtypeStruct(shared_gu.shape, BRAIN),
            jax.ShapeDtypeStruct(shared_gu.shape[:2] + (shared_gu.shape[2] // 2,), BRAIN),
        ],
        in_specs=[
            by_slot(tokens, width),
            by_slot(local, tokens),
            by_pair(PICKED, inner),
            by_slot(tokens, shared_gu.shape[2]),
            whole_spec(expert_in.shape),
            whole_spec(expert_out.shape),
            whole_spec(shared_in.shape),
            whole_spec(shared_out.shape),
        ],
        out_specs=[
            by_slot(tokens, width),
            by_slot(local, tokens),
            by_pair(PICKED, inner),
            by_pair(PICKED, width),
            by_pair(PICKED, inner // 2),
            by_slot(tokens, shared_gu.shape[2]),
            by_slot(tokens, shared_gu.shape[2] // 2),
        ],
        compiler_params=pltpu.CompilerParams(vmem_limit_bytes=52 * MIB),
        name="expert_backward",
    )(grads, gates, gate_up, shared_gu, expert_in, expert_out, shared_in, shared_out)


def moe_forward(hidden, routes, valid, norm_gain, weights):
    router, shared_in, shared_out, expert_in, expert_out = weights
    group = lax.axis_size("expert")
    local = expert_in.shape[0]
    normed, norm_back = jax.vjp(rms_norm, hidden, norm_gain)
    normed_low = normed.astype(BRAIN)
    logits = matmul(normed_low, router)
    chosen = jnp.any(routes[:, :, None] == jnp.arange(router.shape[1])[None, None, :], axis=1)
    largest = jnp.max(jnp.where(chosen, logits, -jnp.inf), axis=1, keepdims=True)
    raised = jnp.where(chosen, jnp.exp(jnp.where(chosen, logits - largest, 0.0)), 0.0)
    probs = raised / jnp.sum(raised, axis=1, keepdims=True)
    gates = probs * valid[:, None]
    rows_all, gates_all = spread([normed_low, gates.T], group, 1)
    own_gates = lax.dynamic_slice_in_dim(gates_all, lax.axis_index("expert") * local, local, axis=1)
    partial, picked, gate_up, shared_gu = expert_forward(
        rows_all, own_gates, expert_in, expert_out, shared_in, shared_out
    )
    output = hidden + gather_sum([partial], group, 2)[0]
    return output, (norm_back, normed_low, probs, rows_all, own_gates, picked, gate_up, shared_gu)


def moe_backward(grad_out, saved, valid, weights):
    norm_back, normed_low, probs, rows_all, own_gates, picked, gate_up, shared_gu = saved
    router, shared_in, shared_out, expert_in, expert_out = weights
    group = lax.axis_size("expert")
    local, width, inner = expert_in.shape
    grads_all = spread([grad_out.astype(BRAIN)], group, 3)[0]
    partial, dgates, dgate_up, dresult, middle, dshared, shared_mid = expert_backward(
        grads_all, own_gates, gate_up, shared_gu, expert_in, expert_out, shared_in, shared_out
    )
    placed = lax.dynamic_update_slice_in_dim(
        jnp.zeros((group, probs.shape[1], probs.shape[0]), FLOAT),
        dgates,
        lax.axis_index("expert") * local,
        axis=1,
    )
    grad_normed, grad_gates = gather_sum([partial, placed], group, 4)
    rows_of = lambda array: array.reshape(local, -1, array.shape[-1])
    by_expert = lambda left, right: lax.dot_general(
        rows_of(left), rows_of(right), (((1,), (1,)), ((0,), (0,))), preferred_element_type=FLOAT
    ).astype(BRAIN)
    grad_expert_in = by_expert(picked, dgate_up)
    grad_expert_out = by_expert(dresult, middle)
    flat = lambda array: array.reshape(-1, array.shape[-1])
    grad_shared_in = matmul_tn(flat(rows_all), flat(dshared)).astype(BRAIN)
    grad_shared_out = matmul_tn(flat(grads_all), flat(shared_mid)).astype(BRAIN)
    grad_probs = grad_gates.T * valid[:, None]
    grad_logits = probs * (grad_probs - jnp.sum(probs * grad_probs, axis=1, keepdims=True))
    logits_low = grad_logits.astype(BRAIN)
    grad_router = matmul_tn(normed_low, logits_low).astype(BRAIN)
    grad_hidden, grad_gain = norm_back(grad_normed + matmul_nt(logits_low, router))
    return (
        grad_out + grad_hidden,
        grad_gain,
        grad_router,
        grad_shared_in,
        grad_shared_out,
        grad_expert_in,
        grad_expert_out,
    )


def attend_scores(query, key_rows):
    length = query.shape[0]
    down = lax.broadcasted_iota(jnp.int32, (length, length), 0)
    along = lax.broadcasted_iota(jnp.int32, (length, length), 1)
    scores = jnp.where(down >= along, matmul_nt(query, key_rows) * AHDIM ** (-0.5), -1e30)
    raised = jnp.exp(scores - jnp.max(scores, axis=1, keepdims=True))
    return raised / jnp.sum(raised, axis=1, keepdims=True)


def attention_forward_kernel(q_ref, k_ref, v_ref, o_ref):
    for j in range(AHEADS // KVHEADS):
        part = slice(j * AHDIM, (j + 1) * AHDIM)
        probs = attend_scores(q_ref[:, part], k_ref[...])
        o_ref[:, part] = matmul(probs.astype(BRAIN), v_ref[...]).astype(BRAIN)


def attention_specs(length):
    queries = pl.BlockSpec((length, QD // KVHEADS), lambda h: (0, h))
    keys = pl.BlockSpec((length, AHDIM), lambda h: (0, QD // AHDIM + h))
    values = pl.BlockSpec((length, AHDIM), lambda h: (0, (QD + KVD) // AHDIM + h))
    return [queries, keys, values]


def attention_core(qkv):
    length = qkv.shape[0]
    specs = attention_specs(length)
    return pl.pallas_call(
        attention_forward_kernel,
        grid=(KVHEADS,),
        out_shape=jax.ShapeDtypeStruct((length, QD), BRAIN),
        in_specs=specs,
        out_specs=specs[0],
        compiler_params=pltpu.CompilerParams(vmem_limit_bytes=32 * MIB),
        name="attention_forward",
    )(qkv, qkv, qkv)


def attention_backward_kernel(q_ref, k_ref, v_ref, d_ref, dq_ref, dk_ref, dv_ref):
    keys = k_ref[...]
    values = v_ref[...]
    dkeys = jnp.zeros(keys.shape, FLOAT)
    dvalues = jnp.zeros(keys.shape, FLOAT)
    for j in range(AHEADS // KVHEADS):
        part = slice(j * AHDIM, (j + 1) * AHDIM)
        query = q_ref[:, part]
        grads = d_ref[:, part]
        probs = attend_scores(query, keys)
        dprobs = matmul_nt(grads, values)
        dvalues = dvalues + matmul_tn(probs.astype(BRAIN), grads)
        inner = jnp.sum(probs * dprobs, axis=1, keepdims=True)
        draw = (probs * (dprobs - inner) * AHDIM ** (-0.5)).astype(BRAIN)
        dq_ref[:, part] = matmul(draw, keys).astype(BRAIN)
        dkeys = dkeys + matmul_tn(draw, query)
    dk_ref[...] = dkeys.astype(BRAIN)
    dv_ref[...] = dvalues.astype(BRAIN)


def attention_core_back(qkv, grads):
    length = qkv.shape[0]
    specs = attention_specs(length)
    head_block = pl.BlockSpec((length, AHDIM), lambda h: (0, h))
    return pl.pallas_call(
        attention_backward_kernel,
        grid=(KVHEADS,),
        out_shape=[
            jax.ShapeDtypeStruct((length, QD), BRAIN),
            jax.ShapeDtypeStruct((length, KVD), BRAIN),
            jax.ShapeDtypeStruct((length, KVD), BRAIN),
        ],
        in_specs=specs + [specs[0]],
        out_specs=[specs[0], head_block, head_block],
        compiler_params=pltpu.CompilerParams(vmem_limit_bytes=32 * MIB),
        name="attention_backward",
    )(qkv, qkv, qkv, grads)


def attention_forward(hidden, norm_gain, attn_qkv, attn_out):
    normed, norm_back = jax.vjp(rms_norm, hidden, norm_gain)
    normed_low = normed.astype(BRAIN)
    qkv = matmul(normed_low, attn_qkv).astype(BRAIN)
    attended = attention_core(qkv)
    output = hidden + matmul_nt(attended, attn_out)
    return output, (norm_back, normed_low, qkv, attended)


def attention_backward(grad_out, saved, attn_qkv, attn_out):
    norm_back, normed_low, qkv, attended = saved
    grad_low = grad_out.astype(BRAIN)
    grad_attn_out = matmul_tn(grad_low, attended).astype(BRAIN)
    grad_attended = matmul(grad_low, attn_out).astype(BRAIN)
    grad_qkv = jnp.concatenate(attention_core_back(qkv, grad_attended), axis=1)
    grad_attn_qkv = matmul_tn(normed_low, grad_qkv).astype(BRAIN)
    grad_hidden, grad_gain = norm_back(matmul_nt(grad_qkv, attn_qkv))
    return grad_out + grad_hidden, grad_gain, grad_attn_qkv, grad_attn_out


def gather_dense(array):
    return lax.all_gather(array, BOTH, axis=0, tiled=True)


def gather_expert(array):
    return lax.all_gather(array, "dp", axis=1, tiled=True)


def scatter_dense(array):
    return lax.psum_scatter(array, BOTH, scatter_dimension=0, tiled=True).astype(FLOAT)


def scatter_expert(array):
    return lax.psum_scatter(array, "dp", scatter_dimension=1, tiled=True).astype(FLOAT)


def shared_columns(shared):
    group = lax.axis_size("expert")
    rows = shared[0].shape[0]
    pieces = []
    for shared_in, shared_out in zip(shared[0::2], shared[1::2]):
        half = shared_in.shape[1] // 2
        pieces += [shared_in[:, :half], shared_in[:, half:], shared_out]
    cut = [piece.reshape(rows, group, -1) for piece in pieces]
    return jnp.transpose(jnp.concatenate(cut, axis=2), (1, 0, 2))


def gather_shared(shared):
    group = lax.axis_size("expert")
    mine = lax.all_to_all(shared_columns(shared), "expert", split_axis=0, concat_axis=0, tiled=True)
    mine = mine.reshape(-1, mine.shape[2])
    whole = lax.all_gather(mine, "dp", axis=0, tiled=True)
    part = shared[1].shape[1] // group
    return [
        whole[:, 0 : 2 * part],
        whole[:, 2 * part : 3 * part],
        whole[:, 3 * part : 5 * part],
        whole[:, 5 * part :],
    ]


def scatter_shared(grads):
    group = lax.axis_size("expert")
    rows = lax.psum_scatter(jnp.concatenate(grads, axis=1), "dp", scatter_dimension=0, tiled=True)
    rows = rows.reshape(group, -1, rows.shape[1])
    own = lax.all_to_all(rows, "expert", split_axis=0, concat_axis=0, tiled=True).astype(FLOAT)
    part = own.shape[2] // 6

    def columns(index):
        piece = jnp.transpose(own[:, :, index * part : (index + 1) * part], (1, 0, 2))
        return piece.reshape(piece.shape[0], -1)

    return [
        jnp.concatenate([columns(0), columns(1)], axis=1),
        columns(2),
        jnp.concatenate([columns(3), columns(4)], axis=1),
        columns(5),
    ]


def per_device(
    layer_input, cotangent, lengths, routes_a, routes_b,
    mixer_in, mixer_out, router_a, shared_in_a, shared_out_a, expert_in_a, expert_out_a,
    attn_qkv, attn_out, router_b, shared_in_b, shared_out_b, expert_in_b, expert_out_b,
    norm_gains, mixer_gain, conv_weight, conv_bias, decay_log, step_bias, skip_gain,
):
    small = {
        "conv_weight": conv_weight,
        "conv_bias": conv_bias,
        "decay_log": decay_log,
        "step_bias": step_bias,
        "skip_gain": skip_gain,
        "mixer_gain": mixer_gain,
    }
    assert lengths.shape[0] == 1 and layer_input.shape[0] == SLOT_LEN
    valid = (jnp.arange(SLOT_LEN) < lengths[0]).astype(FLOAT)
    w_mixer_in = gather_dense(mixer_in)
    w_mixer_out = gather_dense(mixer_out)
    w_routers = gather_dense(jnp.concatenate([router_a, router_b], axis=1))
    experts = router_a.shape[1]
    w_shared = gather_shared([shared_in_a, shared_out_a, shared_in_b, shared_out_b])
    weights_a = (
        w_routers[:, :experts], w_shared[0], w_shared[1], gather_expert(expert_in_a), gather_expert(expert_out_a)
    )
    w_qkv = gather_dense(attn_qkv)
    w_attn_out = gather_dense(attn_out)
    weights_b = (
        w_routers[:, experts:], w_shared[2], w_shared[3], gather_expert(expert_in_b), gather_expert(expert_out_b)
    )
    hidden = layer_input.astype(FLOAT)
    hidden, saved_mix = mixer_forward(hidden, norm_gains[0], w_mixer_in, w_mixer_out, small)
    hidden, saved_a = moe_forward(hidden, routes_a, valid, norm_gains[1], weights_a)
    hidden, saved_attn = attention_forward(hidden, norm_gains[2], w_qkv, w_attn_out)
    layer_output, saved_b = moe_forward(hidden, routes_b, valid, norm_gains[3], weights_b)
    grad = cotangent * valid[:, None]
    grad, gain_four, d_router_b, d_shared_in_b, d_shared_out_b, d_in_b, d_out_b = moe_backward(
        grad, saved_b, valid, weights_b
    )
    d_in_b, d_out_b = scatter_expert(d_in_b), scatter_expert(d_out_b)
    grad, gain_three, d_qkv, d_attn_out = attention_backward(grad, saved_attn, w_qkv, w_attn_out)
    d_qkv, d_attn_out = scatter_dense(d_qkv), scatter_dense(d_attn_out)
    grad, gain_two, d_router_a, d_shared_in_a, d_shared_out_a, d_in_a, d_out_a = moe_backward(
        grad, saved_a, valid, weights_a
    )
    d_in_a, d_out_a = scatter_expert(d_in_a), scatter_expert(d_out_a)
    d_shared = scatter_shared([d_shared_in_a, d_shared_out_a, d_shared_in_b, d_shared_out_b])
    d_routers = scatter_dense(jnp.concatenate([d_router_a, d_router_b], axis=1))
    grad, gain_one, d_mixer_in, d_mixer_out, grad_small = mixer_backward(
        grad, saved_mix, w_mixer_in, w_mixer_out, small
    )
    d_mixer_out = scatter_dense(d_mixer_out)
    d_mixer_in = scatter_dense(d_mixer_in)
    parts = [jnp.stack([gain_one, gain_two, gain_three, gain_four])] + list(grad_small)
    flat = jnp.concatenate([part.reshape(-1) for part in parts])
    padded = jnp.pad(flat, (0, -flat.shape[0] % 1024)).reshape(-1, 128)
    summed = swap_sum(padded, 5).reshape(-1)
    sums = []
    place = 0
    for part in parts:
        sums.append(summed[place : place + part.size].reshape(part.shape))
        place += part.size
    return (
        layer_output, grad,
        d_mixer_in, d_mixer_out, d_routers[:, :experts], d_shared[0], d_shared[1], d_in_a, d_out_a,
        d_qkv, d_attn_out, d_routers[:, experts:], d_shared[2], d_shared[3], d_in_b, d_out_b,
        *sums,
    )


def solution(mesh):
    rows = P(BOTH, None)
    expert = P("expert", "dp", None)
    first = (rows, rows, rows, rows, rows, expert, expert)
    second = (rows, rows, rows, rows, rows, expert, expert)
    return jax.shard_map(
        per_device,
        mesh=mesh,
        in_specs=(rows, rows, P(BOTH), rows, rows) + first + second + (P(),) * 7,
        out_specs=(rows, rows) + first + second + (P(),) * 7,
        check_vma=False,
    )
```

```python
import functools

import jax
import jax.numpy as jnp
from jax import lax
from jax.experimental import pallas as pl
from jax.experimental.pallas import tpu as pltpu
from jax.sharding import PartitionSpec as P

MHEADS = 48
MHDIM = 64
NSTATE = 128
KCONV = 4
AHEADS = 12
KVHEADS = 4
AHDIM = 128
SLOT_LEN = 256
HALF = 128
CAP = 60
DI = 3072
CONVCH = 3328
QD = 1536
KVD = 512
QKV = 2560

EPS = 1e-05
HIGH = lax.Precision.HIGHEST
FLOAT = jnp.float32
BRAIN = jnp.bfloat16
MESH = pl.DeviceIdType.MESH
BOTH = ("dp", "expert")
PICKED = SLOT_LEN // HALF * 64
MIB = 2**20


def matmul(left, right):
    return jnp.dot(left, right, preferred_element_type=FLOAT)


def matmul_nt(left, right):
    return lax.dot_general(left, right, (((1,), (1,)), ((), ())), preferred_element_type=FLOAT)


def matmul_tn(left, right):
    return lax.dot_general(left, right, (((0,), (0,)), ((), ())), preferred_element_type=FLOAT)


def silu_of(values):
    return values * jax.nn.sigmoid(values)


def softplus_of(values):
    return jnp.log1p(jnp.exp(values))


def rms_norm(values, norm_gain):
    return values * lax.rsqrt(jnp.mean(values * values, axis=-1, keepdims=True) + EPS) * norm_gain


def whole_spec(shape):
    return pl.BlockSpec(shape, lambda *at: (0,) * len(shape), pipeline_mode=pl.Buffered(1))


def places(group):
    q = lax.axis_index("dp")
    e = lax.axis_index("expert")
    return q // 2, lax.rem(q, 2), e // 2, lax.rem(e, 2)


def greet(peers):
    barrier = pltpu.get_barrier_semaphore()
    count = 0
    for condition, device in peers:

        def hello():
            pl.semaphore_signal(barrier, inc=1, device_id=device, device_id_type=MESH)

        if condition is None:
            hello()
            count = count + 1
        else:
            pl.when(condition)(hello)
            count = count + jnp.where(condition, 1, 0)
    pl.semaphore_wait(barrier, count)


def line_peers(z, x, line):
    return [
        (None, {"expert": 2 * z + 1 - x}),
        (z > 0, {"expert": 2 * (z - 1) + x}),
        (z < line - 1, {"expert": 2 * (z + 1) + x}),
    ]


def remote(src, dst, send_sem, recv_sem, device):
    return pltpu.make_async_remote_copy(
        src_ref=src, dst_ref=dst, send_sem=send_sem, recv_sem=recv_sem, device_id=device, device_id_type=MESH
    )


def spread_kernel(count, wide, group, *refs):
    total = count + wide
    ins, outs = refs[:total], refs[total : 2 * total]
    sems = refs[2 * total :]
    up_sems, down_sems, cross_sems, recv_sems, own_sems = sems[:5]
    line = group // 2
    y, c, z, x = places(group)
    sibling, opposite = {"dp": 2 * y + 1 - c}, {"dp": 2 * (1 - y) + c}
    greet(line_peers(z, x, line) + ([(None, sibling), (None, opposite)] if wide else []))

    def copy(i, src, place, sem, device):
        return remote(src, outs[i].at[place], sem, recv_sems.at[i, place], {"expert": device})

    def moves(i, s, rising):
        zz = z - s if rising else z + s
        place = 2 * zz + x
        src = ins[i] if s == 0 else outs[i].at[place]
        up = functools.partial(copy, i, src, place, up_sems.at[i, s], 2 * (z + 1) + x)
        down = functools.partial(copy, i, src, place, down_sems.at[i, s], 2 * (z - 1) + x)
        cross = functools.partial(copy, i, src, place, cross_sems.at[i, zz], 2 * z + 1 - x)
        return up, down, cross

    def steps(act):
        for s in range(line):
            for rising in (True, False) if s else (True,):
                valid = (z - s >= 0) if rising else (z + s < line)

                @pl.when(valid)
                def _():
                    for i in range(count):
                        act(i, s, rising, *moves(i, s, rising))

    def block(i, q):
        rows = ins[i].shape[1]
        return outs[i].at[:, pl.ds(pl.multiple_of(q * rows, rows), rows), :]

    def wide_copy(i, kind):
        wide_send, wide_recv = sems[5:]
        own, other = 2 * y + c, 2 * (1 - y) + c
        k = i - count
        if kind == 0:
            return remote(ins[i], block(i, own), wide_send.at[k, 0], wide_recv.at[k, 0], sibling)
        if kind == 1:
            return remote(ins[i], block(i, own), wide_send.at[k, 1], wide_recv.at[k, 1], opposite)
        return remote(block(i, other), block(i, other), wide_send.at[k, 2], wide_recv.at[k, 2], sibling)

    def own_copy(i):
        place = outs[i].at[2 * z + x] if i < count else block(i, 2 * y + c)
        return pltpu.make_async_copy(ins[i], place, own_sems.at[i])

    def forward(i, s, rising, up, down, cross):
        if s:
            cross().wait_recv()
        if rising:
            pl.when(z < line - 1)(lambda: up().start())
        if not rising or s == 0:
            pl.when(z > 0)(lambda: down().start())
        cross().start()

    def settle(i, s, rising, up, down, cross):
        if rising:
            pl.when(z < line - 1)(lambda: up().wait_send())
        if not rising or s == 0:
            pl.when(z > 0)(lambda: down().wait_send())
        cross().wait_send()

    for i in range(count, total):
        wide_copy(i, 1).start()
        wide_copy(i, 0).start()
    for i in range(total):
        own_copy(i).start()
    steps(forward)
    for i in range(count, total):
        wide_copy(i, 1).wait_recv()
        wide_copy(i, 2).start()
    for i in range(count):
        for zz in range(line):
            place = 2 * zz + 1 - x
            copy(i, ins[i], place, own_sems.at[i], 2 * z + 1 - x).wait_recv()
    steps(settle)
    for i in range(count, total):
        wide_copy(i, 0).wait()
        wide_copy(i, 1).wait_send()
        wide_copy(i, 2).wait()
    for i in range(total):
        own_copy(i).wait()


def spread(arrays, wide, group, number):
    n, w, line = len(arrays), len(wide), group // 2
    split = lax.axis_size("dp")
    dma = pltpu.SemaphoreType.DMA
    any_spec = pl.BlockSpec(memory_space=pl.ANY)
    shapes = [jax.ShapeDtypeStruct((group,) + a.shape, a.dtype) for a in arrays]
    shapes += [jax.ShapeDtypeStruct((a.shape[0], split * a.shape[1], a.shape[2]), a.dtype) for a in wide]
    return pl.pallas_call(
        functools.partial(spread_kernel, n, w, group),
        out_shape=shapes,
        in_specs=[any_spec] * (n + w),
        out_specs=[any_spec] * (n + w),
        scratch_shapes=[dma((n, line)), dma((n, line)), dma((n, line)), dma((n, group)), dma((n + w,))]
        + ([dma((w, 3)), dma((w, 3))] if w else []),
        compiler_params=pltpu.CompilerParams(collective_id=number, has_side_effects=True),
        name="spread%d" % number,
    )(*arrays, *wide)


def add_blocks(target, sources, rows):
    step = min(rows, 16)

    def body(j, carry):
        at = pl.ds(pl.multiple_of(j * step, step), step)

        def view(item):
            ref, lead, columns = item
            return ref, tuple(lead) + (at,) + (() if columns is None else (columns,))

        total = None
        for item in sources:
            ref, index = view(item)
            value = ref[index].astype(FLOAT)
            total = value if total is None else total + value
        ref, index = view(target)
        ref[index] = total.astype(ref.dtype)
        return carry

    lax.fori_loop(0, rows // step, body, 0)


def gather_sum_kernel(count, wide, group, *refs):
    total = count + wide
    ins, outs = refs[:total], refs[total : 2 * total]
    bufs = refs[2 * total : 2 * total + 4 * count + 3 * wide]
    own_sems, cross_send, cross_recv, up_send, up_recv, down_send, down_recv = refs[2 * total + 4 * count + 3 * wide :][:7]
    line = group // 2
    held = [bufs[4 * i] for i in range(count)]
    crossed = [bufs[4 * i + 1] for i in range(count)]
    below = [bufs[4 * i + 2] for i in range(count)]
    above = [bufs[4 * i + 3] for i in range(count)]
    y, c, z, x = places(group)
    sibling, opposite = {"dp": 2 * y + 1 - c}, {"dp": 2 * (1 - y) + c}
    greet(line_peers(z, x, line) + ([(None, sibling), (None, opposite)] if wide else []))

    def own(i, d):
        return pltpu.make_async_copy(ins[i].at[2 * d + x], held[i].at[d], own_sems.at[i, d])

    def cross(i, d):
        return remote(
            ins[i].at[2 * d + 1 - x], crossed[i].at[d], cross_send.at[i, d], cross_recv.at[i, d],
            {"expert": 2 * z + 1 - x},
        )

    def rise(i, d):
        return remote(held[i].at[d], below[i].at[d], up_send.at[i, d], up_recv.at[i, d], {"expert": 2 * (z + 1) + x})

    def fall(i, d):
        return remote(held[i].at[d], above[i].at[d], down_send.at[i, d], down_recv.at[i, d], {"expert": 2 * (z - 1) + x})

    def order(act):
        for k in range(line):
            pl.when(line - 1 - k > z)(functools.partial(act, line - 1 - k))
            pl.when(k < z)(functools.partial(act, k))
        for k in range(line):
            pl.when(k == z)(functools.partial(act, k))

    def start_all(d):
        for i in range(count):
            cross(i, d).start()
            own(i, d).start()

    order(start_all)

    def wide_parts(i):
        k = i - count
        kept, landed, arrived = bufs[4 * count + 3 * k : 4 * count + 3 * k + 3]
        wide_own, core_send, core_recv, side_send, side_recv = refs[-5:]
        rows = ins[i].shape[1] // 4

        def block(q):
            return ins[i].at[:, pl.ds(pl.multiple_of(q * rows, rows), rows), :]

        def load(h):
            return pltpu.make_async_copy(block(2 * h + c), kept.at[h], wide_own.at[k, h])

        def to_sibling(h):
            return remote(block(2 * h + 1 - c), landed.at[h], core_send.at[k, h], core_recv.at[k, h], sibling)

        def to_opposite():
            return remote(kept.at[1 - y], arrived, side_send.at[k], side_recv.at[k], opposite)

        return kept, landed, arrived, load, to_sibling, to_opposite, rows

    for i in range(count, total):
        load, to_sibling = wide_parts(i)[3:5]
        for h in (1 - y, y):
            to_sibling(h).start()
            load(h).start()
    for i in range(count, total):
        kept, landed, arrived, load, to_sibling, to_opposite, rows = wide_parts(i)
        h = 1 - y
        load(h).wait()
        to_sibling(h).wait_recv()
        for e in range(ins[i].shape[0]):
            add_blocks((kept, (h, e), None), [(kept, (h, e), None), (landed, (h, e), None)], rows)
        to_opposite().start()

    def add(i, d, final, sources):
        target = (outs[i], (), None) if final else (held[i], (d,), None)
        add_blocks(target, [(held[i], (d,), None)] + [(s[i], (d,), None) for s in sources], held[i].shape[1])

    def ready(i, d):
        own(i, d).wait()
        cross(i, d).wait_recv()

    for k in range(line - 1):
        d = line - 1 - k

        @pl.when(d > z)
        def _():
            for i in range(count):
                ready(i, d)

                @pl.when(z > 0)
                def _():
                    rise(i, d).wait_recv()
                    add(i, d, False, [crossed, below])

                @pl.when(z == 0)
                def _():
                    add(i, d, False, [crossed])

                rise(i, d).start()

        d = k

        @pl.when(d < z)
        def _():
            for i in range(count):
                ready(i, d)

                @pl.when(z < line - 1)
                def _():
                    fall(i, d).wait_recv()
                    add(i, d, False, [crossed, above])

                @pl.when(z == line - 1)
                def _():
                    add(i, d, False, [crossed])

                fall(i, d).start()

    for i in range(count, total):
        kept, landed, arrived, load, to_sibling, to_opposite, rows = wide_parts(i)
        load(y).wait()
        to_sibling(y).wait_recv()
        to_opposite().wait_recv()
        for e in range(ins[i].shape[0]):
            add_blocks(
                (outs[i], (e,), None), [(kept, (y, e), None), (landed, (y, e), None), (arrived, (e,), None)], rows
            )
    for d in range(line):

        @pl.when(d == z)
        def _():
            for i in range(count):
                ready(i, d)
                if d < line - 1:
                    fall(i, d).wait_recv()
                if d > 0:
                    rise(i, d).wait_recv()
                add(i, d, True, [crossed] + ([below] if d > 0 else []) + ([above] if d < line - 1 else []))

    for d in range(line):
        for i in range(count):
            cross(i, d).wait_send()
            pl.when(d > z)(lambda: rise(i, d).wait_send())
            pl.when(d < z)(lambda: fall(i, d).wait_send())
    for i in range(count, total):
        to_sibling, to_opposite = wide_parts(i)[4:6]
        for h in range(2):
            to_sibling(h).wait_send()
        to_opposite().wait_send()


def gather_sum(arrays, wide, group, number):
    n, w, line = len(arrays), len(wide), group // 2
    dma = pltpu.SemaphoreType.DMA
    scratch = []
    for a in arrays:
        scratch += [pltpu.VMEM((line,) + a.shape[1:], a.dtype)] * 4
    shapes = [jax.ShapeDtypeStruct(a.shape[1:], FLOAT) for a in arrays]
    for a in wide:
        part = (a.shape[0], a.shape[1] // 4, a.shape[2])
        scratch += [pltpu.VMEM((2,) + part, a.dtype)] * 2 + [pltpu.VMEM(part, a.dtype)]
        shapes.append(jax.ShapeDtypeStruct(part, FLOAT))
    scratch += [dma((n, line))] * 7
    if w:
        scratch += [dma((w, 2))] * 3 + [dma((w,))] * 2
    return pl.pallas_call(
        functools.partial(gather_sum_kernel, n, w, group),
        out_shape=shapes,
        in_specs=[pl.BlockSpec(memory_space=pl.ANY)] * (n + w),
        out_specs=[pl.BlockSpec(memory_space=pltpu.VMEM)] * (n + w),
        scratch_shapes=scratch,
        compiler_params=pltpu.CompilerParams(collective_id=number, has_side_effects=True, vmem_limit_bytes=52 * MIB),
        name="gather_sum%d" % number,
    )(*arrays, *wide)


def head_kernel(group, cut, mix_ref, router_ref, shared_ref, mix_out, router_out, shared_out, own_sems, send_sems, recv_sems, swap_send, swap_recv):
    line = group // 2
    y, c, z, x = places(group)
    sibling, opposite = {"dp": 2 * y + 1 - c}, {"dp": 2 * (1 - y) + c}
    rising, falling, across = {"expert": 2 * (z + 1) + x}, {"expert": 2 * (z - 1) + x}, {"expert": 2 * z + 1 - x}
    me = 2 * z + x
    peers = [(None, {"expert": lax.rem(me + k, group)}) for k in range(1, group)]
    greet(peers + [(None, sibling), (None, opposite)])
    width = mix_ref.shape[1]
    pieces = [
        (mix_ref, mix_out, pl.ds(0, cut)),
        (mix_ref, mix_out, pl.ds(cut, width - cut)),
        (router_ref, router_out, pl.ds(0, router_ref.shape[1])),
    ]
    first = (0, 2)
    second = (1,)

    def copy(p, yy, cc, zz, xx, way, device, own=False):
        ref, out, columns = pieces[p]
        place = (2 * yy + cc) * group + 2 * zz + xx
        dst = out.at[place, :, columns]
        src = ref.at[:, columns] if own else dst
        slot = yy * group + 2 * zz + xx
        return remote(src, dst, send_sems.at[p, slot, way], recv_sems.at[p, place], device)

    def swap(k):
        to = lax.rem(me + k, group)
        return remote(shared_ref.at[to], shared_out.at[me], swap_send.at[k], swap_recv.at[me], {"expert": to})

    def own_copy(i, ref, out):
        return pltpu.make_async_copy(ref, out, own_sems.at[i])

    owns = [
        (mix_ref, mix_out.at[(2 * y + c) * group + me]),
        (router_ref, router_out.at[(2 * y + c) * group + me]),
        (shared_ref.at[me], shared_out.at[me]),
    ]

    def steps(act):
        for s in range(line):
            for up in (True, False) if s else (True,):
                zz = z - s if up else z + s
                valid = (z - s >= 0) if up else (z + s < line)

                @pl.when(valid)
                def _():
                    act(s, up, zz)

    def column_moves(p, s, up, zz):
        own = s == 0
        moves = []
        if up:
            moves.append((z < line - 1, functools.partial(copy, p, y, c, zz, x, 0, rising, own)))
        if not up or own:
            moves.append((z > 0, functools.partial(copy, p, y, c, zz, x, 1, falling, own)))
        moves.append((None, functools.partial(copy, p, y, c, zz, x, 2, across, own)))
        moves.append((None, functools.partial(copy, p, y, c, zz, x, 3, opposite, own)))
        moves.append((None, functools.partial(copy, p, y, c, zz, x, 4, sibling, own)))
        return moves

    def later_moves(p, zz):
        if p in first:
            return [
                ((y, x, 0), [(3, opposite), (4, sibling)], (y, 1 - x)),
                ((y, x, 1), [(4, sibling)], (1 - y, x)),
                ((y, x, 1), [(4, sibling)], (1 - y, 1 - x)),
            ]
        return [
            ((y, x, 0), [(2, across), (4, sibling)], (1 - y, x)),
            ((y, x, 1), [(4, sibling)], (y, 1 - x)),
            ((y, x, 1), [(4, sibling)], (1 - y, 1 - x)),
        ]

    for p in range(3):
        for condition, move in column_moves(p, 0, True, z):
            if condition is None:
                move().start()
            else:
                pl.when(condition)(lambda: move().start())
    for k in range(1, group):
        swap(k).start()
    for i, (ref, out) in enumerate(owns):
        own_copy(i, ref, out).start()

    def column(s, up, zz):
        if s == 0:
            return
        for p in range(3):
            copy(p, y, c, zz, x, 4, sibling).wait_recv()
            for condition, move in column_moves(p, s, up, zz):
                if condition is None:
                    move().start()
                else:
                    pl.when(condition)(lambda: move().start())

    def later(phase, start):
        def act(s, up, zz):
            for p in range(3):
                for (_, _, when), sends, (yy, xx) in later_moves(p, zz):
                    if when != phase:
                        continue
                    if start:
                        copy(p, yy, c, zz, xx, 4, sibling).wait_recv()
                    for way, device in sends:
                        item = copy(p, yy, c, zz, xx, way, device)
                        if start:
                            item.start()
                        else:
                            item.wait_send()

        return act

    steps(column)
    steps(later(0, True))
    steps(later(1, True))

    def finish(s, up, zz):
        for p in range(3):
            for yy in range(2):
                for xx in range(2):
                    copy(p, yy, 1 - c, zz, xx, 4, sibling).wait_recv()

    steps(finish)

    def settle(s, up, zz):
        for p in range(3):
            for condition, move in column_moves(p, s, up, zz):
                if condition is None:
                    move().wait_send()
                else:
                    pl.when(condition)(lambda: move().wait_send())

    steps(settle)
    steps(later(0, False))
    steps(later(1, False))
    for k in range(1, group):
        source = lax.rem(me + k, group)
        remote(shared_ref.at[source], shared_out.at[source], swap_send.at[k], swap_recv.at[source], across).wait_recv()
        swap(k).wait_send()
    for i, (ref, out) in enumerate(owns):
        own_copy(i, ref, out).wait()


def half_columns(width):
    return width // 256 * 128


def head_exchange(mix, routers, shared, number):
    group = lax.axis_size("expert")
    total = 4 * group
    dma = pltpu.SemaphoreType.DMA
    any_spec = pl.BlockSpec(memory_space=pl.ANY)
    return pl.pallas_call(
        functools.partial(head_kernel, group, half_columns(mix.shape[1])),
        out_shape=[
            jax.ShapeDtypeStruct((total,) + mix.shape, mix.dtype),
            jax.ShapeDtypeStruct((total,) + routers.shape, routers.dtype),
            jax.ShapeDtypeStruct(shared.shape, shared.dtype),
        ],
        in_specs=[any_spec] * 3,
        out_specs=[any_spec] * 3,
        scratch_shapes=[dma((3,)), dma((3, 2 * group, 5)), dma((3, total)), dma((group,)), dma((group,))],
        compiler_params=pltpu.CompilerParams(collective_id=number, has_side_effects=True),
        name="head_exchange",
    )(mix, routers, shared)


def tail_kernel(group, cut, steps, *refs):
    (mix_ref, router_ref, shared_ref, small_ref, mix_out, router_out, shared_out, small_out) = refs[:8]
    bufs = refs[8:20]
    totals, small_landed = refs[20:22]
    (own_sems, core_send, core_recv, one_send, one_recv, two_send, two_recv, line_send, line_recv,
     swap_send, swap_recv, small_send, small_recv, keep_sem) = refs[22:]
    line = group // 2
    y, c, z, x = places(group)
    sibling, opposite = {"dp": 2 * y + 1 - c}, {"dp": 2 * (1 - y) + c}
    rising, falling, across = {"expert": 2 * (z + 1) + x}, {"expert": 2 * (z - 1) + x}, {"expert": 2 * z + 1 - x}
    me = 2 * z + x

    def partner(axis, bit):
        here = lax.axis_index(axis)
        return {axis: here + bit * (1 - 2 * lax.rem(here // bit, 2))}

    peers = [(None, {"expert": lax.rem(me + k, group)}) for k in range(1, group)]
    greet(peers + [(None, sibling), (None, opposite)])

    ins, outs = (mix_ref, router_ref), (mix_out, router_out)
    held, landed, one, two, below, above = (bufs[0:2], bufs[2:4], bufs[4:6], bufs[6:8], bufs[8:10], bufs[10:12])
    rows = mix_ref.shape[1]
    width = mix_ref.shape[2]
    pieces = [(0, pl.ds(0, cut), True), (0, pl.ds(cut, width - cut), False), (1, pl.ds(0, router_ref.shape[2]), True)]

    def slot(yy, zz, xx):
        return yy * group + 2 * zz + xx

    def load(a, yy, zz, xx):
        s = slot(yy, zz, xx)
        return pltpu.make_async_copy(ins[a].at[(2 * yy + c) * group + 2 * zz + xx], held[a].at[s], own_sems.at[a, s])

    def to_sibling(a, yy, zz, xx):
        s = slot(yy, zz, xx)
        return remote(
            ins[a].at[(2 * yy + 1 - c) * group + 2 * zz + xx], landed[a].at[s], core_send.at[a, s], core_recv.at[a, s], sibling
        )

    def stage_one(p, zz, k):
        a, columns, over_y = pieces[p]
        s = slot(1 - y, zz, k) if over_y else slot(k, zz, 1 - x)
        return remote(
            held[a].at[s, :, columns], one[a].at[2 * zz + k, :, columns], one_send.at[p, 2 * zz + k],
            one_recv.at[p, 2 * zz + k], opposite if over_y else across,
        )

    def stage_two(p, zz):
        a, columns, over_y = pieces[p]
        s = slot(y, zz, 1 - x) if over_y else slot(1 - y, zz, x)
        return remote(
            held[a].at[s, :, columns], two[a].at[zz, :, columns], two_send.at[p, zz], two_recv.at[p, zz],
            across if over_y else opposite,
        )

    def rise(a, zz):
        return remote(held[a].at[slot(y, zz, x)], below[a].at[zz], line_send.at[a, 0, zz], line_recv.at[a, 0, zz], rising)

    def fall(a, zz):
        return remote(held[a].at[slot(y, zz, x)], above[a].at[zz], line_send.at[a, 1, zz], line_recv.at[a, 1, zz], falling)

    table = [sorted(range(line), key=lambda d: (-abs(d - k), d)) for k in range(line)]

    def target(j):
        return sum(jnp.where(z == k, table[k][j], 0) for k in range(line))

    def swap(k):
        to = lax.rem(me + k, group)
        return remote(shared_ref.at[to], shared_out.at[me], swap_send.at[k], swap_recv.at[me], {"expert": to})

    def small(step):
        axis, bit = steps[step]
        return remote(
            totals.at[step], small_landed.at[step], small_send.at[step], small_recv.at[step], partner(axis, bit)
        )

    keep = pltpu.make_async_copy(shared_ref.at[me], shared_out.at[me], keep_sem)
    keep.start()
    corners = [(yy, xx) for yy in range(2) for xx in range(2)]
    for j in range(line):
        for a in range(2):
            for yy, xx in corners:
                to_sibling(a, yy, target(j), xx).start()
                load(a, yy, target(j), xx).start()
    for k in range(1, group):
        swap(k).start()
    totals[0] = small_ref[...]
    small(0).start()

    def advance(step):
        if step < len(steps):
            small(step).wait()
            totals[step + 1] = totals[step] + small_landed[step]
            if step + 1 < len(steps):
                small(step + 1).start()

    def phase_a(zz):
        for a in range(2):
            for yy, xx in corners:
                s = slot(yy, zz, xx)
                load(a, yy, zz, xx).wait()
                to_sibling(a, yy, zz, xx).wait_recv()
                add_blocks((held[a], (s,), None), [(held[a], (s,), None), (landed[a], (s,), None)], rows)
        for p in range(3):
            for k in range(2):
                stage_one(p, zz, k).start()

    def phase_b(zz):
        for p, (a, columns, over_y) in enumerate(pieces):
            for k in (1 - x, x) if over_y else (1 - y, y):
                s = slot(y, zz, k) if over_y else slot(k, zz, x)
                stage_one(p, zz, k).wait_recv()
                add_blocks(
                    (held[a], (s,), columns), [(held[a], (s,), columns), (one[a], (2 * zz + k,), columns)], rows
                )
            stage_two(p, zz).start()

    def phase_c(zz):
        s = slot(y, zz, x)
        for p in range(3):
            stage_two(p, zz).wait_recv()
        for a in range(2):
            base = [(held[a], (s,), None), (two[a], (zz,), None)]
            low = (below[a], (zz,), None)
            high = (above[a], (zz,), None)
            kept = (held[a], (s,), None)

            @pl.when(zz > z)
            def _():
                @pl.when(z > 0)
                def _():
                    rise(a, zz).wait_recv()
                    add_blocks(kept, base + [low], rows)

                @pl.when(z == 0)
                def _():
                    add_blocks(kept, base, rows)

                rise(a, zz).start()

            @pl.when(zz < z)
            def _():
                @pl.when(z < line - 1)
                def _():
                    fall(a, zz).wait_recv()
                    add_blocks(kept, base + [high], rows)

                @pl.when(z == line - 1)
                def _():
                    add_blocks(kept, base, rows)

                fall(a, zz).start()

    def phase_last():
        s = slot(y, z, x)
        for p in range(3):
            stage_two(p, z).wait_recv()
        for a in range(2):
            base = [(held[a], (s,), None), (two[a], (z,), None)]
            low = (below[a], (z,), None)
            high = (above[a], (z,), None)
            final = (outs[a], (), None)

            @pl.when(z == 0)
            def _():
                fall(a, z).wait_recv()
                add_blocks(final, base + [high], rows)

            @pl.when(z == line - 1)
            def _():
                rise(a, z).wait_recv()
                add_blocks(final, base + [low], rows)

            @pl.when((z > 0) & (z < line - 1))
            def _():
                fall(a, z).wait_recv()
                rise(a, z).wait_recv()
                add_blocks(final, base + [low, high], rows)

    for t in range(line + 2):
        if t < line:
            phase_a(target(t))
        if 0 <= t - 1 < line:
            phase_b(target(t - 1))
        if 0 <= t - 2 < line - 1:
            phase_c(target(t - 2))
        if t - 2 == line - 1:
            phase_last()
        advance(t)
    for step in range(line + 2, len(steps)):
        advance(step)
    small_out[...] = totals[len(steps)]
    for k in range(1, group):
        source = lax.rem(me + k, group)
        remote(shared_ref.at[source], shared_out.at[source], swap_send.at[k], swap_recv.at[source], across).wait_recv()
        swap(k).wait_send()
    keep.wait()
    for zz in range(line):
        for a in range(2):
            for yy, xx in corners:
                to_sibling(a, yy, zz, xx).wait_send()
            pl.when(zz > z)(lambda: rise(a, zz).wait_send())
            pl.when(zz < z)(lambda: fall(a, zz).wait_send())
        for p in range(3):
            for k in range(2):
                stage_one(p, zz, k).wait_send()
            stage_two(p, zz).wait_send()


def tail_exchange(mix, routers, shared, small, number):
    group = lax.axis_size("expert")
    line = group // 2
    steps = []
    for axis in BOTH:
        bit = 1
        while bit < lax.axis_size(axis):
            steps.append((axis, bit))
            bit *= 2
    dma = pltpu.SemaphoreType.DMA
    vmem = pl.BlockSpec(memory_space=pltpu.VMEM)
    any_spec = pl.BlockSpec(memory_space=pl.ANY)
    scratch = []
    for blocks in (2 * group, 2 * group, group, line, line, line):
        scratch += [pltpu.VMEM((blocks,) + a.shape[1:], a.dtype) for a in (mix, routers)]
    scratch += [pltpu.VMEM((len(steps) + 1,) + small.shape, FLOAT), pltpu.VMEM((len(steps),) + small.shape, FLOAT)]
    scratch += [dma((2, 2 * group))] * 3 + [dma((3, group))] * 2 + [dma((3, line))] * 2 + [dma((2, 2, line))] * 2
    scratch += [dma((group,))] * 2 + [dma((len(steps),))] * 2 + [dma]
    return pl.pallas_call(
        functools.partial(tail_kernel, group, half_columns(mix.shape[2]), steps),
        out_shape=[
            jax.ShapeDtypeStruct(mix.shape[1:], FLOAT),
            jax.ShapeDtypeStruct(routers.shape[1:], FLOAT),
            jax.ShapeDtypeStruct(shared.shape, shared.dtype),
            jax.ShapeDtypeStruct(small.shape, FLOAT),
        ],
        in_specs=[any_spec, any_spec, any_spec, vmem],
        out_specs=[vmem, vmem, any_spec, vmem],
        scratch_shapes=scratch,
        compiler_params=pltpu.CompilerParams(collective_id=number, has_side_effects=True, vmem_limit_bytes=56 * MIB),
        name="tail_exchange",
    )(mix, routers, shared, small)


def state_setup(step_ref, rate_ref, step_t_ref, rate_t_ref, b_ref, c_ref, cum, cum_t, cross):
    length = step_ref.shape[0]
    down = lax.broadcasted_iota(jnp.int32, (length, length), 0)
    along = lax.broadcasted_iota(jnp.int32, (length, length), 1)
    lower = jnp.where(down >= along, 1.0, 0.0)
    upper = jnp.where(down <= along, 1.0, 0.0)
    cum[...] = jnp.dot(
        lower, step_ref[...] * rate_ref[...], precision=HIGH, preferred_element_type=FLOAT
    )
    cum_t[...] = jnp.dot(
        step_t_ref[...] * rate_t_ref[...], upper, precision=HIGH, preferred_element_type=FLOAT
    )
    cross[...] = lax.dot_general(
        c_ref[...], b_ref[...], (((1,), (1,)), ((), ())), precision=HIGH, preferred_element_type=FLOAT
    )


def decay_of(head, cum, cum_t):
    length, heads = cum.shape
    lane = lax.broadcasted_iota(jnp.int32, (length, heads), 1)
    column = jnp.sum(jnp.where(lane == head, cum[...], 0.0), axis=1, keepdims=True)
    spread_out = column - cum_t[pl.ds(head, 1), :]
    down = lax.broadcasted_iota(jnp.int32, (length, length), 0)
    along = lax.broadcasted_iota(jnp.int32, (length, length), 1)
    return jnp.exp(jnp.where(down >= along, spread_out, -1e30))


def state_forward_kernel(
    x_ref, b_ref, c_ref, step_ref, rate_ref, step_t_ref, rate_t_ref, skip_ref, y_ref, cum, cum_t, cross
):
    pair = pl.program_id(0)

    @pl.when(pair == 0)
    def _():
        state_setup(step_ref, rate_ref, step_t_ref, rate_t_ref, b_ref, c_ref, cum, cum_t, cross)

    values = x_ref[...]
    values_low = values.astype(BRAIN)
    total = values * skip_ref[...]
    side = lax.broadcasted_iota(jnp.int32, values.shape, 1) // MHDIM
    for j in range(2):
        head = 2 * pair + j
        mixing = cross[...] * decay_of(head, cum, cum_t) * step_t_ref[pl.ds(head, 1), :]
        part = jnp.dot(mixing.astype(BRAIN), values_low, preferred_element_type=FLOAT)
        total = total + jnp.where(side == j, part, 0.0)
    y_ref[...] = total


def state_specs(length):
    column = lambda place: pl.BlockSpec((length, NSTATE), place)
    return [
        column(lambda i: (0, i)),
        column(lambda i: (0, DI // NSTATE)),
        column(lambda i: (0, DI // NSTATE + 1)),
        whole_spec((length, MHEADS)),
        whole_spec((1, MHEADS)),
        whole_spec((MHEADS, length)),
        whole_spec((MHEADS, 1)),
        pl.BlockSpec((1, 2 * MHDIM), lambda i: (0, i)),
    ]


def state_operands(conv_out, step_size, decay_rate, skip_gain):
    return (
        conv_out,
        conv_out,
        conv_out,
        step_size,
        decay_rate[None, :],
        step_size.T,
        decay_rate[:, None],
        jnp.repeat(skip_gain, MHDIM)[None, :],
    )


def state_forward(conv_out, step_size, decay_rate, skip_gain):
    length = conv_out.shape[0]
    return pl.pallas_call(
        state_forward_kernel,
        grid=(MHEADS // 2,),
        out_shape=jax.ShapeDtypeStruct((length, DI), FLOAT),
        in_specs=state_specs(length),
        out_specs=pl.BlockSpec((length, 2 * MHDIM), lambda i: (0, i)),
        scratch_shapes=[
            pltpu.VMEM((length, MHEADS), FLOAT),
            pltpu.VMEM((MHEADS, length), FLOAT),
            pltpu.VMEM((length, length), FLOAT),
        ],
        compiler_params=pltpu.CompilerParams(vmem_limit_bytes=32 * MIB),
        name="state_forward",
    )(*state_operands(conv_out, step_size, decay_rate, skip_gain))


def state_backward_kernel(
    x_ref, b_ref, c_ref, step_ref, rate_ref, step_t_ref, rate_t_ref, skip_ref, dy_ref,
    dx_ref, db_ref, dc_ref, row_ref, column_ref, cum, cum_t, cross, dcross,
):
    pair = pl.program_id(0)

    @pl.when(pair == 0)
    def _():
        state_setup(step_ref, rate_ref, step_t_ref, rate_t_ref, b_ref, c_ref, cum, cum_t, cross)
        dcross[...] = jnp.zeros_like(dcross)
        row_ref[...] = jnp.zeros_like(row_ref)

    values_low = x_ref[...].astype(BRAIN)
    grads = dy_ref[...]
    total = grads * skip_ref[...]
    side = lax.broadcasted_iota(jnp.int32, grads.shape, 1) // MHDIM
    lane = lax.broadcasted_iota(jnp.int32, row_ref.shape, 1)
    for j in range(2):
        head = 2 * pair + j
        steps = step_t_ref[pl.ds(head, 1), :]
        decay = decay_of(head, cum, cum_t)
        own = jnp.where(side == j, grads, 0.0).astype(BRAIN)
        mixing = cross[...] * decay
        total = total + matmul_tn((mixing * steps).astype(BRAIN), own)
        dmix = matmul_nt(own, values_low)
        dcross[...] += dmix * decay * steps
        weighed = dmix * mixing
        column_ref[pl.ds(head, 1), :] = jnp.sum(weighed, axis=0, keepdims=True)
        row_sum = jnp.sum(weighed * steps, axis=1, keepdims=True)
        row_ref[...] += jnp.where(lane == head, row_sum, 0.0)
    dx_ref[...] = total

    @pl.when(pair == pl.num_programs(0) - 1)
    def _():
        dc_ref[...] = jnp.dot(dcross[...], b_ref[...], precision=HIGH, preferred_element_type=FLOAT)
        db_ref[...] = lax.dot_general(
            dcross[...], c_ref[...], (((0,), (0,)), ((), ())), precision=HIGH, preferred_element_type=FLOAT
        )


def state_backward(conv_out, step_size, decay_rate, skip_gain, grad_mixed):
    length = conv_out.shape[0]
    pair_block = pl.BlockSpec((length, 2 * MHDIM), lambda i: (0, i))
    dx, db, dc, row_sums, column_sums = pl.pallas_call(
        state_backward_kernel,
        grid=(MHEADS // 2,),
        out_shape=[
            jax.ShapeDtypeStruct((length, DI), FLOAT),
            jax.ShapeDtypeStruct((length, NSTATE), FLOAT),
            jax.ShapeDtypeStruct((length, NSTATE), FLOAT),
            jax.ShapeDtypeStruct((length, MHEADS), FLOAT),
            jax.ShapeDtypeStruct((MHEADS, length), FLOAT),
        ],
        in_specs=state_specs(length) + [pair_block],
        out_specs=[
            pair_block,
            pl.BlockSpec((length, NSTATE), lambda i: (0, 0)),
            pl.BlockSpec((length, NSTATE), lambda i: (0, 0)),
            pl.BlockSpec((length, MHEADS), lambda i: (0, 0)),
            pl.BlockSpec((MHEADS, length), lambda i: (0, 0)),
        ],
        scratch_shapes=[
            pltpu.VMEM((length, MHEADS), FLOAT),
            pltpu.VMEM((MHEADS, length), FLOAT),
            pltpu.VMEM((length, length), FLOAT),
            pltpu.VMEM((length, length), FLOAT),
        ],
        compiler_params=pltpu.CompilerParams(vmem_limit_bytes=32 * MIB),
        name="state_backward",
    )(*state_operands(conv_out, step_size, decay_rate, skip_gain), grad_mixed)
    column_sums = column_sums.T
    dcum = row_sums - column_sums * step_size
    places = jnp.arange(length)
    upper = (places[:, None] <= places[None, :]).astype(FLOAT)
    drate_step = jnp.dot(upper, dcum, precision=HIGH, preferred_element_type=FLOAT)
    grad_step = column_sums + drate_step * decay_rate
    grad_decay_log = jnp.sum(drate_step * step_size, axis=0) * decay_rate
    return dx, db, dc, grad_step, grad_decay_log


def convolve(conv_in, conv_weight, conv_bias):
    length = conv_in.shape[0]
    padded = jnp.pad(conv_in, ((KCONV - 1, 0), (0, 0)))
    total = conv_bias + padded[0:length] * conv_weight[0]
    for tap in range(1, KCONV):
        total = total + padded[tap : tap + length] * conv_weight[tap]
    return silu_of(total)


def gated_norm(mixed, gate_z, mixer_gain):
    return rms_norm(mixed * silu_of(gate_z), mixer_gain)


def step_of(step_raw, step_bias):
    return softplus_of(step_raw + step_bias)


def mixer_forward(hidden, norm_gain, mixer_in, mixer_out, small):
    normed, norm_back = jax.vjp(rms_norm, hidden, norm_gain)
    normed_low = normed.astype(BRAIN)
    projected = matmul(normed_low, mixer_in)
    gate_z = projected[:, :DI]
    conv_in = projected[:, DI : DI + CONVCH]
    step_raw = projected[:, DI + CONVCH :]
    conv_out, conv_back = jax.vjp(convolve, conv_in, small["conv_weight"], small["conv_bias"])
    step_size, step_back = jax.vjp(step_of, step_raw, small["step_bias"])
    decay_rate = -jnp.exp(small["decay_log"])
    mixed = state_forward(conv_out, step_size, decay_rate, small["skip_gain"])
    mixer_norm, gated_back = jax.vjp(gated_norm, mixed, gate_z, small["mixer_gain"])
    mixer_low = mixer_norm.astype(BRAIN)
    output = hidden + matmul_nt(mixer_low, mixer_out)
    saved = (norm_back, normed_low, conv_out, conv_back, step_size, step_back, decay_rate, gated_back, mixer_low)
    return output, saved


def mixer_backward(grad_out, saved, mixer_in, mixer_out, small):
    norm_back, normed_low, conv_out, conv_back, step_size, step_back, decay_rate, gated_back, mixer_low = saved
    grad_low = grad_out.astype(BRAIN)
    grad_mixer_out = matmul_tn(grad_low, mixer_low).astype(BRAIN)
    grad_norm, grad_mixer_out = lax.optimization_barrier((matmul(grad_low, mixer_out), grad_mixer_out))
    grad_mixed, grad_gate, grad_mixer_gain = gated_back(grad_norm)
    dx, db, dc, grad_step, grad_decay_log = state_backward(
        conv_out, step_size, decay_rate, small["skip_gain"], grad_mixed
    )
    grad_skip = jnp.sum(jnp.sum(grad_mixed * conv_out[:, :DI], axis=0).reshape(MHEADS, MHDIM), axis=1)
    grad_conv_in, grad_conv_weight, grad_conv_bias = conv_back(jnp.concatenate([dx, db, dc], axis=1))
    grad_step_raw, grad_step_bias = step_back(grad_step)
    grad_proj = jnp.concatenate([grad_gate, grad_conv_in, grad_step_raw], axis=1).astype(BRAIN)
    grad_mixer_in = matmul_tn(normed_low, grad_proj).astype(BRAIN)
    grad_hidden, grad_gain = norm_back(matmul_nt(grad_proj, mixer_in))
    grad_small = (
        grad_mixer_gain, grad_conv_weight, grad_conv_bias, grad_decay_log, grad_step_bias, grad_skip
    )
    return grad_out + grad_hidden, grad_gain, grad_mixer_in, grad_mixer_out, grad_small


def pick_rows(gates):
    tokens = gates.shape[1]
    down = lax.broadcasted_iota(jnp.int32, (tokens, tokens), 0)
    along = lax.broadcasted_iota(jnp.int32, (tokens, tokens), 1)
    upper = jnp.where(down <= along, 1.0, 0.0).astype(BRAIN)
    live = jnp.where(gates != 0.0, 1.0, 0.0)
    place = jnp.dot(
        jnp.broadcast_to(live, (8, tokens)).astype(BRAIN), upper, preferred_element_type=FLOAT
    )[0:1] - 1.0
    ranks = lax.broadcasted_iota(jnp.int32, (PICKED, tokens), 0).astype(FLOAT)
    return (ranks == place) & (live > 0.0)


def expert_forward_kernel(x_ref, g_ref, in_ref, out_ref, sin_ref, sout_ref, y_ref, xe_ref, gu_ref, sgu_ref):
    rows = x_ref[0]
    shared_gu = jnp.dot(rows, sin_ref[...], preferred_element_type=FLOAT)
    half = shared_gu.shape[1] // 2
    shared_mid = (silu_of(shared_gu[:, :half]) * shared_gu[:, half:]).astype(BRAIN)
    sgu_ref[0] = shared_gu.astype(sgu_ref.dtype)
    total = matmul_nt(shared_mid, sout_ref[...])
    for e in range(in_ref.shape[0]):
        gates = g_ref[0, e : e + 1, :]
        hit = pick_rows(gates)
        picked = jnp.dot(
            jnp.where(hit, 1.0, 0.0).astype(BRAIN), rows, preferred_element_type=FLOAT
        ).astype(BRAIN)
        gate_up = jnp.dot(picked, in_ref[e], preferred_element_type=FLOAT)
        width = gate_up.shape[1] // 2
        inner = (silu_of(gate_up[:, :width]) * gate_up[:, width:]).astype(BRAIN)
        result = matmul_nt(inner, out_ref[e]).astype(BRAIN)
        total = total + matmul_tn(jnp.where(hit, gates, 0.0).astype(BRAIN), result)
        xe_ref[e, 0] = picked
        gu_ref[e, 0] = gate_up.astype(gu_ref.dtype)
    y_ref[0] = total.astype(y_ref.dtype)


def expert_forward(rows, gates, expert_in, expert_out, shared_in, shared_out):
    group, tokens, width = rows.shape
    local = expert_in.shape[0]
    inner = expert_in.shape[2]
    by_slot = lambda *shape: pl.BlockSpec((1,) + shape, lambda s: (s,) + (0,) * len(shape))
    by_pair = lambda *shape: pl.BlockSpec((local, 1) + shape, lambda s: (0, s) + (0,) * len(shape))
    return pl.pallas_call(
        expert_forward_kernel,
        grid=(group,),
        out_shape=[
            jax.ShapeDtypeStruct(rows.shape, BRAIN),
            jax.ShapeDtypeStruct((local, group, PICKED, width), BRAIN),
            jax.ShapeDtypeStruct((local, group, PICKED, inner), BRAIN),
            jax.ShapeDtypeStruct((group, tokens, shared_in.shape[1]), BRAIN),
        ],
        in_specs=[
            by_slot(tokens, width),
            by_slot(local, tokens),
            whole_spec(expert_in.shape),
            whole_spec(expert_out.shape),
            whole_spec(shared_in.shape),
            whole_spec(shared_out.shape),
        ],
        out_specs=[
            by_slot(tokens, width),
            by_pair(PICKED, width),
            by_pair(PICKED, inner),
            by_slot(tokens, shared_in.shape[1]),
        ],
        compiler_params=pltpu.CompilerParams(vmem_limit_bytes=52 * MIB),
        name="expert_forward",
    )(rows, gates, expert_in, expert_out, shared_in, shared_out)


def swiglu_back(gate, up, grad):
    sig = jax.nn.sigmoid(gate)
    act = gate * sig
    return grad * up * (sig + act * (1.0 - sig)), grad * act, act * up


def expert_backward_kernel(
    d_ref, g_ref, gu_ref, sgu_ref, in_ref, out_ref, sin_ref, sout_ref,
    dx_ref, dg_ref, dgu_ref, dres_ref, mid_ref, dsgu_ref, smid_ref,
):
    grads = d_ref[0]
    shared_gu = sgu_ref[0].astype(FLOAT)
    half = shared_gu.shape[1] // 2
    dmid = jnp.dot(grads, sout_ref[...], preferred_element_type=FLOAT)
    dgate, dup, shared_mid = swiglu_back(shared_gu[:, :half], shared_gu[:, half:], dmid)
    shared_d = jnp.concatenate([dgate, dup], axis=1).astype(BRAIN)
    dsgu_ref[0] = shared_d
    smid_ref[0] = shared_mid.astype(BRAIN)
    total = matmul_nt(shared_d, sin_ref[...])
    for e in range(in_ref.shape[0]):
        gates = g_ref[0, e : e + 1, :]
        hit = pick_rows(gates)
        chosen = jnp.where(hit, 1.0, 0.0).astype(BRAIN)
        weight = jnp.sum(jnp.where(hit, gates, 0.0), axis=1, keepdims=True)
        picked = jnp.dot(chosen, grads, preferred_element_type=FLOAT)
        dres_ref[e, 0] = (picked * weight).astype(BRAIN)
        raw = jnp.dot(picked.astype(BRAIN), out_ref[e], preferred_element_type=FLOAT)
        gate_up = gu_ref[e, 0].astype(FLOAT)
        width = gate_up.shape[1] // 2
        dgate, dup, inner = swiglu_back(gate_up[:, :width], gate_up[:, width:], raw * weight)
        inner_low = inner.astype(BRAIN)
        mid_ref[e, 0] = inner_low
        dweight = jnp.sum(raw * inner_low.astype(FLOAT), axis=1, keepdims=True)
        dg_ref[0, e : e + 1, :] = jnp.sum(jnp.where(hit, dweight, 0.0), axis=0, keepdims=True)
        dgu = jnp.concatenate([dgate, dup], axis=1).astype(BRAIN)
        dgu_ref[e, 0] = dgu
        back = matmul_nt(dgu, in_ref[e]).astype(BRAIN)
        total = total + matmul_tn(chosen, back)
    dx_ref[0] = total.astype(dx_ref.dtype)


def expert_backward(grads, gates, gate_up, shared_gu, expert_in, expert_out, shared_in, shared_out):
    group, tokens, width = grads.shape
    local = expert_in.shape[0]
    inner = expert_in.shape[2]
    by_slot = lambda *shape: pl.BlockSpec((1,) + shape, lambda s: (s,) + (0,) * len(shape))
    by_pair = lambda *shape: pl.BlockSpec((local, 1) + shape, lambda s: (0, s) + (0,) * len(shape))
    return pl.pallas_call(
        expert_backward_kernel,
        grid=(group,),
        out_shape=[
            jax.ShapeDtypeStruct(grads.shape, BRAIN),
            jax.ShapeDtypeStruct((group, local, tokens), FLOAT),
            jax.ShapeDtypeStruct((local, group, PICKED, inner), BRAIN),
            jax.ShapeDtypeStruct((local, group, PICKED, width), BRAIN),
            jax.ShapeDtypeStruct((local, group, PICKED, inner // 2), BRAIN),
            jax.ShapeDtypeStruct(shared_gu.shape, BRAIN),
            jax.ShapeDtypeStruct(shared_gu.shape[:2] + (shared_gu.shape[2] // 2,), BRAIN),
        ],
        in_specs=[
            by_slot(tokens, width),
            by_slot(local, tokens),
            by_pair(PICKED, inner),
            by_slot(tokens, shared_gu.shape[2]),
            whole_spec(expert_in.shape),
            whole_spec(expert_out.shape),
            whole_spec(shared_in.shape),
            whole_spec(shared_out.shape),
        ],
        out_specs=[
            by_slot(tokens, width),
            by_slot(local, tokens),
            by_pair(PICKED, inner),
            by_pair(PICKED, width),
            by_pair(PICKED, inner // 2),
            by_slot(tokens, shared_gu.shape[2]),
            by_slot(tokens, shared_gu.shape[2] // 2),
        ],
        compiler_params=pltpu.CompilerParams(vmem_limit_bytes=52 * MIB),
        name="expert_backward",
    )(grads, gates, gate_up, shared_gu, expert_in, expert_out, shared_in, shared_out)


def moe_forward(hidden, routes, valid, norm_gain, router, pieces):
    group = lax.axis_size("expert")
    local = pieces[0].shape[0]
    normed, norm_back = jax.vjp(rms_norm, hidden, norm_gain)
    normed_low = normed.astype(BRAIN)
    logits = matmul(normed_low, router)
    chosen = jnp.any(routes[:, :, None] == jnp.arange(router.shape[1])[None, None, :], axis=1)
    largest = jnp.max(jnp.where(chosen, logits, -jnp.inf), axis=1, keepdims=True)
    raised = jnp.where(chosen, jnp.exp(jnp.where(chosen, logits - largest, 0.0)), 0.0)
    probs = raised / jnp.sum(raised, axis=1, keepdims=True)
    gates = probs * valid[:, None]
    if lax.axis_size("dp") == 4:
        rows_all, gates_all, expert_in, expert_out, shared = spread([normed_low, gates.T], pieces, group, 1)
    else:
        rows_all, gates_all = spread([normed_low, gates.T], [], group, 1)
        expert_in, expert_out, shared = [lax.all_gather(p, "dp", axis=1, tiled=True) for p in pieces]
    part = shared.shape[2] // 3
    weights = (router, shared[0, :, : 2 * part], shared[0, :, 2 * part :], expert_in, expert_out)
    own_gates = lax.dynamic_slice_in_dim(gates_all, lax.axis_index("expert") * local, local, axis=1)
    partial, picked, gate_up, shared_gu = expert_forward(rows_all, own_gates, expert_in, expert_out, *weights[1:3])
    output = hidden + gather_sum([partial], [], group, 2)[0]
    return output, (norm_back, normed_low, probs, rows_all, own_gates, picked, gate_up, shared_gu, weights)


def moe_backward(grad_out, saved, valid):
    norm_back, normed_low, probs, rows_all, own_gates, picked, gate_up, shared_gu, weights = saved
    router, shared_in, shared_out, expert_in, expert_out = weights
    group = lax.axis_size("expert")
    local, width, inner = expert_in.shape
    grads_all = spread([grad_out.astype(BRAIN)], [], group, 3)[0]
    partial, dgates, dgate_up, dresult, middle, dshared, shared_mid = expert_backward(
        grads_all, own_gates, gate_up, shared_gu, expert_in, expert_out, shared_in, shared_out
    )
    placed = lax.dynamic_update_slice_in_dim(
        jnp.zeros((group, probs.shape[1], probs.shape[0]), FLOAT),
        dgates,
        lax.axis_index("expert") * local,
        axis=1,
    )
    rows_of = lambda array: array.reshape(local, -1, array.shape[-1])
    by_expert = lambda left, right: lax.dot_general(
        rows_of(left), rows_of(right), (((1,), (1,)), ((0,), (0,))), preferred_element_type=FLOAT
    ).astype(BRAIN)
    flat = lambda array: array.reshape(-1, array.shape[-1])
    shared_grads = [matmul_tn(flat(rows_all), flat(dshared)), matmul_tn(flat(grads_all), flat(shared_mid))]
    sums = [
        by_expert(picked, dgate_up),
        by_expert(dresult, middle),
        jnp.concatenate(shared_grads, axis=1).astype(BRAIN)[None],
    ]
    if lax.axis_size("dp") == 4:
        grad_normed, grad_gates, *sums = gather_sum([partial, placed], sums, group, 4)
    else:
        grad_normed, grad_gates = gather_sum([partial, placed], [], group, 4)
        sums = [lax.psum_scatter(s, "dp", scatter_dimension=1, tiled=True).astype(FLOAT) for s in sums]
    grad_probs = grad_gates.T * valid[:, None]
    grad_logits = probs * (grad_probs - jnp.sum(probs * grad_probs, axis=1, keepdims=True))
    logits_low = grad_logits.astype(BRAIN)
    grad_router = matmul_tn(normed_low, logits_low).astype(BRAIN)
    grad_hidden, grad_gain = norm_back(grad_normed + matmul_nt(logits_low, router))
    return grad_out + grad_hidden, grad_gain, grad_router, sums[2][0].astype(BRAIN), sums[0], sums[1]


def attend_scores(query, key_rows):
    length = query.shape[0]
    down = lax.broadcasted_iota(jnp.int32, (length, length), 0)
    along = lax.broadcasted_iota(jnp.int32, (length, length), 1)
    scores = jnp.where(down >= along, matmul_nt(query, key_rows) * AHDIM ** (-0.5), -1e30)
    raised = jnp.exp(scores - jnp.max(scores, axis=1, keepdims=True))
    return raised / jnp.sum(raised, axis=1, keepdims=True)


def attention_forward_kernel(q_ref, k_ref, v_ref, o_ref):
    for j in range(AHEADS // KVHEADS):
        part = slice(j * AHDIM, (j + 1) * AHDIM)
        probs = attend_scores(q_ref[:, part], k_ref[...])
        o_ref[:, part] = matmul(probs.astype(BRAIN), v_ref[...]).astype(BRAIN)


def attention_specs(length):
    queries = pl.BlockSpec((length, QD // KVHEADS), lambda h: (0, h))
    keys = pl.BlockSpec((length, AHDIM), lambda h: (0, QD // AHDIM + h))
    values = pl.BlockSpec((length, AHDIM), lambda h: (0, (QD + KVD) // AHDIM + h))
    return [queries, keys, values]


def attention_core(qkv):
    length = qkv.shape[0]
    specs = attention_specs(length)
    return pl.pallas_call(
        attention_forward_kernel,
        grid=(KVHEADS,),
        out_shape=jax.ShapeDtypeStruct((length, QD), BRAIN),
        in_specs=specs,
        out_specs=specs[0],
        compiler_params=pltpu.CompilerParams(vmem_limit_bytes=32 * MIB),
        name="attention_forward",
    )(qkv, qkv, qkv)


def attention_backward_kernel(q_ref, k_ref, v_ref, d_ref, dq_ref, dk_ref, dv_ref):
    keys = k_ref[...]
    values = v_ref[...]
    dkeys = jnp.zeros(keys.shape, FLOAT)
    dvalues = jnp.zeros(keys.shape, FLOAT)
    for j in range(AHEADS // KVHEADS):
        part = slice(j * AHDIM, (j + 1) * AHDIM)
        query = q_ref[:, part]
        grads = d_ref[:, part]
        probs = attend_scores(query, keys)
        dprobs = matmul_nt(grads, values)
        dvalues = dvalues + matmul_tn(probs.astype(BRAIN), grads)
        inner = jnp.sum(probs * dprobs, axis=1, keepdims=True)
        draw = (probs * (dprobs - inner) * AHDIM ** (-0.5)).astype(BRAIN)
        dq_ref[:, part] = matmul(draw, keys).astype(BRAIN)
        dkeys = dkeys + matmul_tn(draw, query)
    dk_ref[...] = dkeys.astype(BRAIN)
    dv_ref[...] = dvalues.astype(BRAIN)


def attention_core_back(qkv, grads):
    length = qkv.shape[0]
    specs = attention_specs(length)
    head_block = pl.BlockSpec((length, AHDIM), lambda h: (0, h))
    return pl.pallas_call(
        attention_backward_kernel,
        grid=(KVHEADS,),
        out_shape=[
            jax.ShapeDtypeStruct((length, QD), BRAIN),
            jax.ShapeDtypeStruct((length, KVD), BRAIN),
            jax.ShapeDtypeStruct((length, KVD), BRAIN),
        ],
        in_specs=specs + [specs[0]],
        out_specs=[specs[0], head_block, head_block],
        compiler_params=pltpu.CompilerParams(vmem_limit_bytes=32 * MIB),
        name="attention_backward",
    )(qkv, qkv, qkv, grads)


def attention_forward(hidden, norm_gain, attn_qkv, attn_out):
    normed, norm_back = jax.vjp(rms_norm, hidden, norm_gain)
    normed_low = normed.astype(BRAIN)
    qkv = matmul(normed_low, attn_qkv).astype(BRAIN)
    attended = attention_core(qkv)
    output = hidden + matmul_nt(attended, attn_out)
    return output, (norm_back, normed_low, qkv, attended)


def attention_backward(grad_out, saved, attn_qkv, attn_out):
    norm_back, normed_low, qkv, attended = saved
    grad_low = grad_out.astype(BRAIN)
    grad_attn_out = matmul_tn(grad_low, attended).astype(BRAIN)
    grad_attended = matmul(grad_low, attn_out).astype(BRAIN)
    grad_qkv = jnp.concatenate(attention_core_back(qkv, grad_attended), axis=1)
    grad_attn_qkv = matmul_tn(normed_low, grad_qkv).astype(BRAIN)
    grad_hidden, grad_gain = norm_back(matmul_nt(grad_qkv, attn_qkv))
    return grad_out + grad_hidden, grad_gain, grad_attn_qkv, grad_attn_out


def gather_dense(array):
    return lax.all_gather(array, BOTH, axis=0, tiled=True)


def scatter_dense(array):
    return lax.psum_scatter(array, BOTH, scatter_dimension=0, tiled=True).astype(FLOAT)


def shared_columns(shared):
    group = lax.axis_size("expert")
    rows = shared[0].shape[0]
    pieces = []
    for shared_in, shared_out in zip(shared[0::2], shared[1::2]):
        half = shared_in.shape[1] // 2
        pieces += [shared_in[:, :half], shared_in[:, half:], shared_out]
    cut = [piece.reshape(rows, group, -1) for piece in pieces]
    return jnp.transpose(jnp.concatenate(cut, axis=2), (1, 0, 2))


def shared_whole(own):
    part = own.shape[2] // 6

    def columns(index):
        piece = jnp.transpose(own[:, :, index * part : (index + 1) * part], (1, 0, 2))
        return piece.reshape(piece.shape[0], -1)

    return [
        jnp.concatenate([columns(0), columns(1)], axis=1),
        columns(2),
        jnp.concatenate([columns(3), columns(4)], axis=1),
        columns(5),
    ]


def exchange(blocks):
    return lax.all_to_all(blocks, "expert", split_axis=0, concat_axis=0, tiled=True)


def first_gather(mixer_in, routers, shared):
    if lax.axis_size("dp") == 4:
        mix, routers, shared = head_exchange(mixer_in, routers, shared, 5)
        return mix.reshape(-1, mix.shape[2]), routers.reshape(-1, routers.shape[2]), shared
    return gather_dense(mixer_in), gather_dense(routers), exchange(shared)


def last_sums(mix, routers, shared, small):
    if lax.axis_size("dp") == 4:
        cut = lambda array: array.reshape(4 * lax.axis_size("expert"), -1, array.shape[1])
        return tail_exchange(cut(mix), cut(routers), shared, small, 6)
    return scatter_dense(mix), scatter_dense(routers), exchange(shared), lax.psum(small, BOTH)


def per_device(
    layer_input, cotangent, lengths, routes_a, routes_b,
    mixer_in, mixer_out, router_a, shared_in_a, shared_out_a, expert_in_a, expert_out_a,
    attn_qkv, attn_out, router_b, shared_in_b, shared_out_b, expert_in_b, expert_out_b,
    norm_gains, mixer_gain, conv_weight, conv_bias, decay_log, step_bias, skip_gain,
):
    small = {
        "conv_weight": conv_weight,
        "conv_bias": conv_bias,
        "decay_log": decay_log,
        "step_bias": step_bias,
        "skip_gain": skip_gain,
        "mixer_gain": mixer_gain,
    }
    assert lengths.shape[0] == 1 and layer_input.shape[0] == SLOT_LEN
    group = lax.axis_size("expert")
    experts = router_a.shape[1]
    valid = (jnp.arange(SLOT_LEN) < lengths[0]).astype(FLOAT)
    w_mixer_in, w_routers, w_shared = first_gather(
        mixer_in,
        jnp.concatenate([router_a, router_b], axis=1),
        shared_columns([shared_in_a, shared_out_a, shared_in_b, shared_out_b]),
    )
    w_shared = w_shared.reshape(1, -1, w_shared.shape[2])
    half = w_shared.shape[2] // 2
    w_mixer_out = gather_dense(mixer_out)
    w_qkv = gather_dense(attn_qkv)
    w_attn_out = gather_dense(attn_out)
    hidden = layer_input.astype(FLOAT)
    hidden, saved_mix = mixer_forward(hidden, norm_gains[0], w_mixer_in, w_mixer_out, small)
    hidden, saved_a = moe_forward(
        hidden, routes_a, valid, norm_gains[1], w_routers[:, :experts], [expert_in_a, expert_out_a, w_shared[:, :, :half]]
    )
    hidden, saved_attn = attention_forward(hidden, norm_gains[2], w_qkv, w_attn_out)
    layer_output, saved_b = moe_forward(
        hidden, routes_b, valid, norm_gains[3], w_routers[:, experts:], [expert_in_b, expert_out_b, w_shared[:, :, half:]]
    )
    grad = cotangent * valid[:, None]
    grad, gain_four, d_router_b, d_shared_b, d_in_b, d_out_b = moe_backward(grad, saved_b, valid)
    grad, gain_three, d_qkv, d_attn_out = attention_backward(grad, saved_attn, w_qkv, w_attn_out)
    grad, d_qkv, d_attn_out = lax.optimization_barrier((grad, d_qkv, d_attn_out))
    d_qkv, d_attn_out = scatter_dense(d_qkv), scatter_dense(d_attn_out)
    grad, gain_two, d_router_a, d_shared_a, d_in_a, d_out_a = moe_backward(grad, saved_a, valid)
    grad, gain_one, d_mixer_in, d_mixer_out, grad_small = mixer_backward(
        grad, saved_mix, w_mixer_in, w_mixer_out, small
    )
    d_mixer_out = scatter_dense(d_mixer_out)
    parts = [jnp.stack([gain_one, gain_two, gain_three, gain_four])] + list(grad_small)
    flat = jnp.concatenate([part.reshape(-1) for part in parts])
    padded = jnp.pad(flat, (0, -flat.shape[0] % 1024)).reshape(-1, 128)
    d_shared = jnp.concatenate([d_shared_a, d_shared_b], axis=1)
    d_mixer_in, d_routers, d_shared, summed = last_sums(
        d_mixer_in,
        jnp.concatenate([d_router_a, d_router_b], axis=1),
        d_shared.reshape(group, -1, d_shared.shape[1]),
        padded,
    )
    d_shared = shared_whole(d_shared.astype(FLOAT))
    summed = summed.reshape(-1)
    sums = []
    place = 0
    for part in parts:
        sums.append(summed[place : place + part.size].reshape(part.shape))
        place += part.size
    return (
        layer_output, grad,
        d_mixer_in, d_mixer_out, d_routers[:, :experts], d_shared[0], d_shared[1], d_in_a, d_out_a,
        d_qkv, d_attn_out, d_routers[:, experts:], d_shared[2], d_shared[3], d_in_b, d_out_b,
        *sums,
    )


def solution(mesh):
    rows = P(BOTH, None)
    expert = P("expert", "dp", None)
    first = (rows, rows, rows, rows, rows, expert, expert)
    second = (rows, rows, rows, rows, rows, expert, expert)
    return jax.shard_map(
        per_device,
        mesh=mesh,
        in_specs=(rows, rows, P(BOTH), rows, rows) + first + second + (P(),) * 7,
        out_specs=(rows, rows) + first + second + (P(),) * 7,
        check_vma=False,
    )
```

```python
import functools

import jax
import jax.numpy as jnp
from jax import lax
from jax.experimental import pallas as pl
from jax.experimental.pallas import tpu as pltpu
from jax.sharding import PartitionSpec as P

MHEADS = 48
MHDIM = 64
NSTATE = 128
KCONV = 4
AHEADS = 12
KVHEADS = 4
AHDIM = 128
SLOT_LEN = 256
HALF = 128
CAP = 60
DI = 3072
CONVCH = 3328
QD = 1536
KVD = 512
QKV = 2560

EPS = 1e-05
HIGH = lax.Precision.HIGHEST
FLOAT = jnp.float32
BRAIN = jnp.bfloat16
MESH = pl.DeviceIdType.MESH
BOTH = ("dp", "expert")
PICKED = SLOT_LEN // HALF * 64
MIB = 2**20


def matmul(left, right):
    return jnp.dot(left, right, preferred_element_type=FLOAT)


def matmul_nt(left, right):
    return lax.dot_general(left, right, (((1,), (1,)), ((), ())), preferred_element_type=FLOAT)


def matmul_tn(left, right):
    return lax.dot_general(left, right, (((0,), (0,)), ((), ())), preferred_element_type=FLOAT)


def silu_of(values):
    return values * jax.nn.sigmoid(values)


def softplus_of(values):
    return jnp.log1p(jnp.exp(values))


def rms_norm(values, norm_gain):
    return values * lax.rsqrt(jnp.mean(values * values, axis=-1, keepdims=True) + EPS) * norm_gain


def whole_spec(shape):
    return pl.BlockSpec(shape, lambda *at: (0,) * len(shape), pipeline_mode=pl.Buffered(1))


def places(group):
    q = lax.axis_index("dp")
    e = lax.axis_index("expert")
    return q // 2, lax.rem(q, 2), e // 2, lax.rem(e, 2)


def greet(peers):
    barrier = pltpu.get_barrier_semaphore()
    count = 0
    for condition, device in peers:

        def hello():
            pl.semaphore_signal(barrier, inc=1, device_id=device, device_id_type=MESH)

        if condition is None:
            hello()
            count = count + 1
        else:
            pl.when(condition)(hello)
            count = count + jnp.where(condition, 1, 0)
    pl.semaphore_wait(barrier, count)


def line_peers(z, x, line):
    return [
        (None, {"expert": 2 * z + 1 - x}),
        (z > 0, {"expert": 2 * (z - 1) + x}),
        (z < line - 1, {"expert": 2 * (z + 1) + x}),
    ]


def remote(src, dst, send_sem, recv_sem, device):
    return pltpu.make_async_remote_copy(
        src_ref=src, dst_ref=dst, send_sem=send_sem, recv_sem=recv_sem, device_id=device, device_id_type=MESH
    )


def spread_kernel(count, wide, sums, group, *refs):
    total = count + wide
    every = total + sums
    ins, outs = refs[:every], refs[every : 2 * every]
    stages = refs[2 * every : 2 * every + wide]
    sum_bufs = refs[2 * every + wide : 2 * every + wide + 3 * sums]
    sems = refs[2 * every + wide + 3 * sums :]
    sum_sems = sems[-5:]
    up_sems, down_sems, cross_sems, recv_sems, own_sems = sems[:5]
    line = group // 2
    y, c, z, x = places(group)
    sibling, opposite = {"dp": 2 * y + 1 - c}, {"dp": 2 * (1 - y) + c}
    greet(line_peers(z, x, line) + ([(None, sibling), (None, opposite)] if wide or sums else []))

    def copy(i, src, place, sem, device):
        return remote(src, outs[i].at[place], sem, recv_sems.at[i, place], {"expert": device})

    def moves(i, s, rising):
        zz = z - s if rising else z + s
        place = 2 * zz + x
        src = ins[i] if s == 0 else outs[i].at[place]
        up = functools.partial(copy, i, src, place, up_sems.at[i, s], 2 * (z + 1) + x)
        down = functools.partial(copy, i, src, place, down_sems.at[i, s], 2 * (z - 1) + x)
        cross = functools.partial(copy, i, src, place, cross_sems.at[i, zz], 2 * z + 1 - x)
        return up, down, cross

    def steps(act):
        for s in range(line):
            for rising in (True, False) if s else (True,):
                valid = (z - s >= 0) if rising else (z + s < line)

                @pl.when(valid)
                def _():
                    for i in range(count):
                        act(i, s, rising, *moves(i, s, rising))

    def block(i, q):
        rows = ins[i].shape[1]
        return outs[i].at[:, pl.ds(pl.multiple_of(q * rows, rows), rows), :]

    def wide_copy(i, kind):
        wide_send, wide_recv = sems[5:7]
        own, other = 2 * y + c, 2 * (1 - y) + c
        k = i - count
        if kind == 0:
            return remote(ins[i], block(i, own), wide_send.at[k, 0], wide_recv.at[k, 0], sibling)
        if kind == 1:
            return remote(ins[i], block(i, own), wide_send.at[k, 1], wide_recv.at[k, 1], opposite)
        return remote(block(i, other), block(i, other), wide_send.at[k, 2], wide_recv.at[k, 2], sibling)

    def own_copy(i):
        if i < count:
            return pltpu.make_async_copy(ins[i], outs[i].at[2 * z + x], own_sems.at[i])
        return pltpu.make_async_copy(ins[i], stages[i - count], own_sems.at[i])

    def own_store(i):
        return pltpu.make_async_copy(stages[i - count], block(i, 2 * y + c), own_sems.at[i])

    def forward(i, s, rising, up, down, cross):
        if s:
            cross().wait_recv()
        if rising:
            pl.when(z < line - 1)(lambda: up().start())
        if not rising or s == 0:
            pl.when(z > 0)(lambda: down().start())
        cross().start()

    def settle(i, s, rising, up, down, cross):
        if rising:
            pl.when(z < line - 1)(lambda: up().wait_send())
        if not rising or s == 0:
            pl.when(z > 0)(lambda: down().wait_send())
        cross().wait_send()

    def sum_parts(k):
        kept, landed, arrived = sum_bufs[3 * k : 3 * k + 3]
        own, core_send, core_recv, side_send, side_recv = sum_sems
        source = ins[total + k]
        rows = source.shape[1] // 4

        def piece(q):
            return source.at[:, pl.ds(pl.multiple_of(q * rows, rows), rows), :]

        def load(h):
            return pltpu.make_async_copy(piece(2 * h + c), kept.at[h], own.at[k, h])

        def to_sibling(h):
            return remote(piece(2 * h + 1 - c), landed.at[h], core_send.at[k, h], core_recv.at[k, h], sibling)

        def to_opposite():
            return remote(kept.at[1 - y], arrived, side_send.at[k], side_recv.at[k], opposite)

        def add(target, lead, sources):
            for e in range(source.shape[0]):
                add_blocks((target, lead + (e,), None), [(ref, at + (e,), None) for ref, at in sources], rows)

        return kept, landed, arrived, load, to_sibling, to_opposite, add

    for k in range(sums):
        load, to_sibling = sum_parts(k)[3:5]
        for h in (1 - y, y):
            to_sibling(h).start()
            load(h).start()
    for i in range(count, total):
        wide_copy(i, 1).start()
        wide_copy(i, 0).start()
    for i in range(total):
        own_copy(i).start()
    for i in range(count, total):
        own_copy(i).wait()
        own_store(i).start()
    if sums:
        steps(lambda *move: forward(*move) if move[1] == 0 else None)
        for k in range(sums):
            kept, landed, arrived, load, to_sibling, to_opposite, add = sum_parts(k)
            load(1 - y).wait()
            to_sibling(1 - y).wait_recv()
            add(kept, (1 - y,), [(kept, (1 - y,)), (landed, (1 - y,))])
            to_opposite().start()
        steps(lambda *move: forward(*move) if move[1] else None)
    else:
        steps(forward)
    for i in range(count, total):
        wide_copy(i, 1).wait_recv()
        wide_copy(i, 2).start()
    for i in range(count):
        for zz in range(line):
            place = 2 * zz + 1 - x
            copy(i, ins[i], place, own_sems.at[i], 2 * z + 1 - x).wait_recv()
    steps(settle)
    for i in range(count, total):
        wide_copy(i, 0).wait()
        wide_copy(i, 1).wait_send()
        wide_copy(i, 2).wait()
    for i in range(count):
        own_copy(i).wait()
    for i in range(count, total):
        own_store(i).wait()
    for k in range(sums):
        kept, landed, arrived, load, to_sibling, to_opposite, add = sum_parts(k)
        load(y).wait()
        to_sibling(y).wait_recv()
        to_opposite().wait_recv()
        add(outs[total + k], (), [(kept, (y,)), (landed, (y,)), (arrived, ())])
        for h in range(2):
            to_sibling(h).wait_send()
        to_opposite().wait_send()


def spread(arrays, wide, sums, group, number):
    n, w, s, line = len(arrays), len(wide), len(sums), group // 2
    split = lax.axis_size("dp")
    dma = pltpu.SemaphoreType.DMA
    any_spec = pl.BlockSpec(memory_space=pl.ANY)
    vmem = pl.BlockSpec(memory_space=pltpu.VMEM)
    shapes = [jax.ShapeDtypeStruct((group,) + a.shape, a.dtype) for a in arrays]
    shapes += [jax.ShapeDtypeStruct((a.shape[0], split * a.shape[1], a.shape[2]), a.dtype) for a in wide]
    scratch = [pltpu.VMEM(a.shape, a.dtype) for a in wide]
    for a in sums:
        part = (a.shape[0], a.shape[1] // 4, a.shape[2])
        scratch += [pltpu.VMEM((2,) + part, a.dtype)] * 2 + [pltpu.VMEM(part, a.dtype)]
        shapes.append(jax.ShapeDtypeStruct(part, FLOAT))
    scratch += [dma((n, line)), dma((n, line)), dma((n, line)), dma((n, group)), dma((n + w,))]
    if w:
        scratch += [dma((w, 3)), dma((w, 3))]
    if s:
        scratch += [dma((s, 2))] * 3 + [dma((s,))] * 2
    return pl.pallas_call(
        functools.partial(spread_kernel, n, w, s, group),
        out_shape=shapes,
        in_specs=[any_spec] * (n + w + s),
        out_specs=[any_spec] * (n + w) + [vmem] * s,
        scratch_shapes=scratch,
        compiler_params=pltpu.CompilerParams(collective_id=number, has_side_effects=True, vmem_limit_bytes=40 * MIB),
        name="spread%d" % number,
    )(*arrays, *wide, *sums)


def add_blocks(target, sources, rows):
    step = min(rows, 16)

    def body(j, carry):
        at = pl.ds(pl.multiple_of(j * step, step), step)

        def view(item):
            ref, lead, columns = item
            return ref, tuple(lead) + (at,) + (() if columns is None else (columns,))

        total = None
        for item in sources:
            ref, index = view(item)
            value = ref[index].astype(FLOAT)
            total = value if total is None else total + value
        ref, index = view(target)
        ref[index] = total.astype(ref.dtype)
        return carry

    lax.fori_loop(0, rows // step, body, 0)


def head_kernel(group, cut, dense, *refs):
    ins, outs = refs[: dense + 2], refs[dense + 2 : 2 * dense + 4]
    own_sems, send_sems, recv_sems, swap_send, swap_recv, row_send, row_recv = refs[2 * dense + 4 :]
    shared_ref, shared_out = ins[dense], outs[dense]
    row_ref, row_out = ins[dense + 1], outs[dense + 1]
    line = group // 2
    y, c, z, x = places(group)
    sibling, opposite = {"dp": 2 * y + 1 - c}, {"dp": 2 * (1 - y) + c}
    rising, falling, across = {"expert": 2 * (z + 1) + x}, {"expert": 2 * (z - 1) + x}, {"expert": 2 * z + 1 - x}
    me = 2 * z + x
    peers = [(None, {"expert": lax.rem(me + k, group)}) for k in range(1, group)]
    greet(peers + [(None, sibling), (None, opposite)])
    width = ins[0].shape[1]
    pieces = [(0, pl.ds(0, cut), True), (0, pl.ds(cut, width - cut), False)]
    pieces += [(i, pl.ds(0, ins[i].shape[1]), True) for i in range(1, dense)]
    count = len(pieces)

    def copy(p, yy, cc, zz, xx, way, device, own=False):
        i, columns, _ = pieces[p]
        place = (2 * yy + cc) * group + 2 * zz + xx
        dst = outs[i].at[place, :, columns]
        src = ins[i].at[:, columns] if own else dst
        slot = yy * group + 2 * zz + xx
        return remote(src, dst, send_sems.at[p, slot, way], recv_sems.at[p, place], device)

    def row_copy(zz, xx, way, device, own=False):
        dst = row_out.at[2 * zz + xx]
        return remote(row_ref if own else dst, dst, row_send.at[zz, way], row_recv.at[2 * zz + xx], device)

    def swap(k):
        to = lax.rem(me + k, group)
        return remote(shared_ref.at[to], shared_out.at[me], swap_send.at[k], swap_recv.at[me], {"expert": to})

    def own_copy(i):
        if i < dense:
            return pltpu.make_async_copy(ins[i], outs[i].at[(2 * y + c) * group + me], own_sems.at[i])
        if i == dense:
            return pltpu.make_async_copy(shared_ref.at[me], shared_out.at[me], own_sems.at[i])
        return pltpu.make_async_copy(row_ref, row_out.at[me], own_sems.at[i])

    def steps(act):
        for s in range(line):
            for up in (True, False) if s else (True,):
                zz = z - s if up else z + s
                valid = (z - s >= 0) if up else (z + s < line)

                @pl.when(valid)
                def _():
                    act(s, up, zz)

    def column_moves(p, s, up, zz):
        own = s == 0
        make = functools.partial(row_copy, zz, x) if p is None else functools.partial(copy, p, y, c, zz, x)
        moves = []
        if up:
            moves.append((z < line - 1, functools.partial(make, 0, rising, own)))
        if not up or own:
            moves.append((z > 0, functools.partial(make, 1, falling, own)))
        moves.append((None, functools.partial(make, 2, across, own)))
        if p is not None:
            moves.append((None, functools.partial(make, 3, opposite, own)))
            moves.append((None, functools.partial(make, 4, sibling, own)))
        return moves

    def run(moves, act):
        for condition, move in moves:
            if condition is None:
                act(move())
            else:
                pl.when(condition)(lambda: act(move()))

    def later_moves(p):
        if pieces[p][2]:
            return [
                (0, [(3, opposite), (4, sibling)], (y, 1 - x)),
                (1, [(4, sibling)], (1 - y, x)),
                (1, [(4, sibling)], (1 - y, 1 - x)),
            ]
        return [
            (0, [(2, across), (4, sibling)], (1 - y, x)),
            (1, [(4, sibling)], (y, 1 - x)),
            (1, [(4, sibling)], (1 - y, 1 - x)),
        ]

    everything = list(range(count)) + [None]

    def column(s, up, zz):
        for p in everything:
            if s:
                if p is None:
                    row_copy(zz, x, 2, across).wait_recv()
                else:
                    copy(p, y, c, zz, x, 4, sibling).wait_recv()
            run(column_moves(p, s, up, zz), lambda item: item.start())
        if s == 0:
            for k in range(1, group):
                swap(k).start()
            for i in range(dense + 2):
                own_copy(i).start()

    def later(phase, start):
        def act(s, up, zz):
            for p in range(count):
                for when, sends, (yy, xx) in later_moves(p):
                    if when != phase:
                        continue
                    if start:
                        copy(p, yy, c, zz, xx, 4, sibling).wait_recv()
                    for way, device in sends:
                        item = copy(p, yy, c, zz, xx, way, device)
                        if start:
                            item.start()
                        else:
                            item.wait_send()

        return act

    def finish(s, up, zz):
        row_copy(zz, 1 - x, 2, across).wait_recv()
        for p in range(count):
            for yy in range(2):
                for xx in range(2):
                    copy(p, yy, 1 - c, zz, xx, 4, sibling).wait_recv()

    def settle(s, up, zz):
        for p in everything:
            run(column_moves(p, s, up, zz), lambda item: item.wait_send())

    only = lambda act, k: steps(lambda s, up, zz: act(s, up, zz) if s == k else None)
    for k in range(line + 2):
        if k < line:
            only(column, k)
        if 0 <= k - 1 < line:
            only(later(0, True), k - 1)
        if 0 <= k - 2 < line:
            only(later(1, True), k - 2)
    steps(finish)
    steps(settle)
    steps(later(0, False))
    steps(later(1, False))
    for k in range(1, group):
        source = lax.rem(me + k, group)
        remote(shared_ref.at[source], shared_out.at[source], swap_send.at[k], swap_recv.at[source], across).wait_recv()
        swap(k).wait_send()
    for i in range(dense + 2):
        own_copy(i).wait()


def head_exchange(dense, shared, rows, number):
    group = lax.axis_size("expert")
    total = 4 * group
    count = len(dense) + 1
    dma = pltpu.SemaphoreType.DMA
    any_spec = pl.BlockSpec(memory_space=pl.ANY)
    cut = dense[0].shape[1] * 9 // 10 // 128 * 128
    return pl.pallas_call(
        functools.partial(head_kernel, group, cut, len(dense)),
        out_shape=[jax.ShapeDtypeStruct((total,) + a.shape, a.dtype) for a in dense]
        + [
            jax.ShapeDtypeStruct(shared.shape, shared.dtype),
            jax.ShapeDtypeStruct((group,) + rows.shape, rows.dtype),
        ],
        in_specs=[any_spec] * (len(dense) + 2),
        out_specs=[any_spec] * (len(dense) + 2),
        scratch_shapes=[
            dma((len(dense) + 2,)),
            dma((count, 2 * group, 5)),
            dma((count, total)),
            dma((group,)),
            dma((group,)),
            dma((group // 2, 3)),
            dma((group,)),
        ],
        compiler_params=pltpu.CompilerParams(collective_id=number, has_side_effects=True),
        name="head_exchange",
    )(*dense, shared, rows)


def farthest(z, line, j):
    table = [sorted(range(line), key=lambda d: (-abs(d - k), d)) for k in range(line)]
    return sum(
        jnp.where((z == k) & (j == n), table[k][n], 0) for k in range(line) for n in range(line) if table[k][n]
    )


def tail_kernel(group, sums, steps, *refs):
    (left_ref, right_ref, router_ref, shared_ref, small_ref) = refs[:5]
    sum_ins, refs = refs[5 : 5 + sums], refs[5 + sums :]
    (mix_out, router_out, shared_out, small_out) = refs[:4]
    sum_outs, refs = refs[4 : 4 + sums], refs[4 + sums :]
    bufs = refs[:12]
    made, totals, small_landed = refs[12:15]
    sum_bufs, refs = refs[15 : 15 + 3 * sums], refs[15 + 3 * sums :]
    sum_own, sum_core_send, sum_core_recv, sum_side_send, sum_side_recv, sum_store, late_send, late_recv = refs[-8:]
    (own_sems, core_send, core_recv, one_send, one_recv, two_send, two_recv, line_send, line_recv,
     swap_send, swap_recv, small_send, small_recv, keep_sem) = refs[:-8]
    line = group // 2
    y, c, z, x = places(group)
    sibling, opposite = {"dp": 2 * y + 1 - c}, {"dp": 2 * (1 - y) + c}
    rising, falling, across = {"expert": 2 * (z + 1) + x}, {"expert": 2 * (z - 1) + x}, {"expert": 2 * z + 1 - x}
    me = 2 * z + x

    def partner(axis, bit):
        here = lax.axis_index(axis)
        return {axis: here + bit * (1 - 2 * lax.rem(here // bit, 2))}

    peers = [(None, {"expert": lax.rem(me + k, group)}) for k in range(1, group)]
    greet(peers + [(None, sibling), (None, opposite)])

    outs = (mix_out, router_out)
    held, landed, one, two, below, above = (bufs[0:2], bufs[2:4], bufs[4:6], bufs[6:8], bufs[8:10], bufs[10:12])
    rows, width = mix_out.shape
    pieces = [(0, pl.ds(0, width), False), (1, pl.ds(0, router_ref.shape[2]), True)]
    count = len(pieces)

    def slot(yy, zz, xx):
        return yy * group + 2 * zz + xx

    def load(yy, zz, xx):
        s = slot(yy, zz, xx)
        return pltpu.make_async_copy(router_ref.at[(2 * yy + c) * group + 2 * zz + xx], held[1].at[s], own_sems.at[s])

    def to_sibling(a, yy, zz, xx, turn=0):
        s = slot(yy, zz, xx)
        source = made.at[4 * turn + 2 * yy + xx] if a == 0 else router_ref.at[(2 * yy + 1 - c) * group + 2 * zz + xx]
        return remote(source, landed[a].at[s], core_send.at[a, s], core_recv.at[a, s], sibling)

    def make(cc, zz, target, place_of):
        lefts = []
        for yy in range(2):
            start = pl.multiple_of(((2 * yy + cc) * group + 2 * zz) * rows, 16)
            lefts.append(left_ref[pl.ds(start, 2 * rows)])
        lefts = jnp.concatenate(lefts, axis=0)
        step = 1664
        for start in range(0, width, step):
            columns = slice(start, min(start + step, width))
            product = jnp.dot(lefts, right_ref[:, columns], preferred_element_type=FLOAT).astype(BRAIN)
            for yy in range(2):
                for xx in range(2):
                    place = (2 * yy + xx) * rows
                    target[place_of(yy, xx), :, columns] = product[place : place + rows]

    def stage_one(p, zz, k):
        a, columns, over_y = pieces[p]
        s = slot(1 - y, zz, k) if over_y else slot(k, zz, 1 - x)
        return remote(
            held[a].at[s, :, columns], one[a].at[2 * zz + k, :, columns], one_send.at[p, 2 * zz + k],
            one_recv.at[p, 2 * zz + k], opposite if over_y else across,
        )

    def stage_two(p, zz):
        a, columns, over_y = pieces[p]
        s = slot(y, zz, 1 - x) if over_y else slot(1 - y, zz, x)
        return remote(
            held[a].at[s, :, columns], two[a].at[zz, :, columns], two_send.at[p, zz], two_recv.at[p, zz],
            across if over_y else opposite,
        )

    def rise(a, zz):
        return remote(held[a].at[slot(y, zz, x)], below[a].at[zz], line_send.at[a, 0, zz], line_recv.at[a, 0, zz], rising)

    def fall(a, zz):
        return remote(held[a].at[slot(y, zz, x)], above[a].at[zz], line_send.at[a, 1, zz], line_recv.at[a, 1, zz], falling)

    def swap(k):
        to = lax.rem(me + k, group)
        return remote(shared_ref.at[to], shared_out.at[me], swap_send.at[k], swap_recv.at[me], {"expert": to})

    def small(step):
        axis, bit = steps[step]
        return remote(
            totals.at[step], small_landed.at[step], small_send.at[step], small_recv.at[step], partner(axis, bit)
        )

    keep = pltpu.make_async_copy(shared_ref.at[me], shared_out.at[me], keep_sem)
    keep.start()
    corners = [(yy, xx) for yy in range(2) for xx in range(2)]
    for zz in range(line):
        for yy, xx in corners:
            to_sibling(1, yy, zz, xx).start()
            load(yy, zz, xx).start()
    for k in range(1, group):
        swap(k).start()
    totals[0] = small_ref[...]
    small(0).start()

    def advance(step):
        if step < len(steps):
            small(step).wait()
            totals[step + 1] = totals[step] + small_landed[step]
            if step + 1 < len(steps):
                small(step + 1).start()

    def phase_make(zz, t):
        turn = lax.rem(t, 2)

        @pl.when(t >= 2)
        def _():
            for yy, xx in corners:
                to_sibling(0, yy, farthest(z, line, t - 2), xx, turn).wait_send()

        make(1 - c, zz, made, lambda yy, xx: 4 * turn + 2 * yy + xx)
        for yy, xx in corners:
            to_sibling(0, yy, zz, xx, turn).start()
        make(c, zz, held[0], lambda yy, xx: slot(yy, zz, xx))

    def sum_parts(k):
        kept, landed, arrived = sum_bufs[3 * k : 3 * k + 3]
        source = sum_ins[k]
        height = source.shape[1] // 4

        def piece(q):
            return source.at[:, pl.ds(pl.multiple_of(q * height, height), height), :]

        def take(h):
            return pltpu.make_async_copy(piece(2 * h + c), kept.at[h], sum_own.at[k, h])

        def give(h):
            return remote(piece(2 * h + 1 - c), landed.at[h], sum_core_send.at[k, h], sum_core_recv.at[k, h], sibling)

        def pass_on():
            return remote(kept.at[1 - y], arrived, sum_side_send.at[k], sum_side_recv.at[k], opposite)

        def add(h, extra):
            for e in range(source.shape[0]):
                items = [(kept, (h, e), None), (landed, (h, e), None)] + ([(arrived, (e,), None)] if extra else [])
                add_blocks((kept, (h, e), None), items, height)

        def store():
            return pltpu.make_async_copy(kept.at[y], sum_outs[k], sum_store.at[k])

        return take, give, pass_on, add, store

    def sums_first():
        for k in range(sums):
            take, give, pass_on, add, store = sum_parts(k)
            take(1 - y).wait()
            give(1 - y).wait_recv()
            add(1 - y, False)
            pass_on().start()

    def late(k):
        to = lax.rem(me + k, group)
        height = sum_outs[0].shape[1]
        block = sum_bufs[0].at[y, 0, pl.ds(pl.multiple_of(to * height, 16), height)]
        if k == 0:
            return pltpu.make_async_copy(block, sum_outs[0].at[me], late_send.at[k])
        return remote(block, sum_outs[0].at[me], late_send.at[k], late_recv.at[me], {"expert": to})

    def sums_last(which):
        for k in which:
            take, give, pass_on, add, store = sum_parts(k)
            take(y).wait()
            give(y).wait_recv()
            pass_on().wait_recv()
            add(y, True)
            if k:
                store().start()
            else:
                for n in range(group):
                    late(n).start()

    def sums_settle():
        for k in range(sums):
            take, give, pass_on, add, store = sum_parts(k)
            give(y).wait_send()
            give(1 - y).wait_send()
            pass_on().wait_send()
            if k:
                store().wait()
        late(0).wait()
        for n in range(1, group):
            source = lax.rem(me + n, group)
            remote(
                shared_ref.at[source], sum_outs[0].at[source], late_send.at[n], late_recv.at[source], across
            ).wait_recv()
            late(n).wait_send()

    def phase_a(zz):
        for a in range(2):
            for yy, xx in corners:
                s = slot(yy, zz, xx)
                if a == 1:
                    load(yy, zz, xx).wait()
                to_sibling(a, yy, zz, xx).wait_recv()
                add_blocks((held[a], (s,), None), [(held[a], (s,), None), (landed[a], (s,), None)], rows)
        for p in range(count):
            for k in range(2):
                stage_one(p, zz, k).start()

    def phase_b(zz):
        for p, (a, columns, over_y) in enumerate(pieces):
            for k in (1 - x, x) if over_y else (1 - y, y):
                s = slot(y, zz, k) if over_y else slot(k, zz, x)
                stage_one(p, zz, k).wait_recv()
                add_blocks(
                    (held[a], (s,), columns), [(held[a], (s,), columns), (one[a], (2 * zz + k,), columns)], rows
                )
            stage_two(p, zz).start()

    def phase_c(zz):
        s = slot(y, zz, x)
        for p in range(count):
            stage_two(p, zz).wait_recv()
        for a in range(2):
            base = [(held[a], (s,), None), (two[a], (zz,), None)]
            low = (below[a], (zz,), None)
            high = (above[a], (zz,), None)
            kept = (held[a], (s,), None)

            @pl.when(zz > z)
            def _():
                @pl.when(z > 0)
                def _():
                    rise(a, zz).wait_recv()
                    add_blocks(kept, base + [low], rows)

                @pl.when(z == 0)
                def _():
                    add_blocks(kept, base, rows)

                rise(a, zz).start()

            @pl.when(zz < z)
            def _():
                @pl.when(z < line - 1)
                def _():
                    fall(a, zz).wait_recv()
                    add_blocks(kept, base + [high], rows)

                @pl.when(z == line - 1)
                def _():
                    add_blocks(kept, base, rows)

                fall(a, zz).start()

    def phase_last():
        s = slot(y, z, x)
        for p in range(count):
            stage_two(p, z).wait_recv()
        for a in range(2):
            base = [(held[a], (s,), None), (two[a], (z,), None)]
            low = (below[a], (z,), None)
            high = (above[a], (z,), None)
            final = (outs[a], (), None)

            @pl.when(z == 0)
            def _():
                fall(a, z).wait_recv()
                add_blocks(final, base + [high], rows)

            @pl.when(z == line - 1)
            def _():
                rise(a, z).wait_recv()
                add_blocks(final, base + [low], rows)

            @pl.when((z > 0) & (z < line - 1))
            def _():
                fall(a, z).wait_recv()
                rise(a, z).wait_recv()
                add_blocks(final, base + [low, high], rows)

    for k in range(sums):
        take, give = sum_parts(k)[:2]
        for h in (1 - y, y):
            take(h).start()
            give(h).start()

    def body(t, carry):
        for shift, phase, number in ((0, phase_make, line), (1, phase_a, line), (2, phase_b, line), (3, phase_c, line - 1)):

            @pl.when((t >= shift) & (t - shift < number))
            def _():
                phase(farthest(z, line, t - shift), *([t] if shift == 0 else []))

        pl.when(t == 0)(sums_first)
        pl.when(t == 4)(lambda: sums_last([0]))
        for step in range(len(steps)):
            pl.when(t == step + 1)(functools.partial(advance, step))
        return carry

    lax.fori_loop(0, max(line + 3, len(steps) + 1), body, 0)
    phase_last()
    sums_last(range(1, sums))
    sums_settle()
    for t in (line - 2, line - 1):
        for yy, xx in corners:
            to_sibling(0, yy, farthest(z, line, t), xx, t % 2).wait_send()
    small_out[...] = totals[len(steps)]
    for k in range(1, group):
        source = lax.rem(me + k, group)
        remote(shared_ref.at[source], shared_out.at[source], swap_send.at[k], swap_recv.at[source], across).wait_recv()
        swap(k).wait_send()
    keep.wait()
    for zz in range(line):
        for a in range(2):
            if a == 1:
                for yy, xx in corners:
                    to_sibling(a, yy, zz, xx).wait_send()
            pl.when(zz > z)(lambda: rise(a, zz).wait_send())
            pl.when(zz < z)(lambda: fall(a, zz).wait_send())
        for p in range(count):
            for k in range(2):
                stage_one(p, zz, k).wait_send()
            stage_two(p, zz).wait_send()


def tail_exchange(left, right, routers, shared, small, sums, number):
    group = lax.axis_size("expert")
    line = group // 2
    steps = []
    for axis in BOTH:
        bit = 1
        while bit < lax.axis_size(axis):
            steps.append((axis, bit))
            bit *= 2
    dma = pltpu.SemaphoreType.DMA
    vmem = pl.BlockSpec(memory_space=pltpu.VMEM)
    any_spec = pl.BlockSpec(memory_space=pl.ANY)
    mix = (left.shape[0] // (4 * group), right.shape[1])
    scratch = []
    for blocks in (2 * group, 2 * group, group, line, line, line):
        scratch += [pltpu.VMEM((blocks,) + shape, BRAIN) for shape in (mix, routers.shape[1:])]
    scratch += [pltpu.VMEM((8,) + mix, BRAIN)]
    scratch += [pltpu.VMEM((len(steps) + 1,) + small.shape, FLOAT), pltpu.VMEM((len(steps),) + small.shape, FLOAT)]
    parts = [(a.shape[0], a.shape[1] // 4, a.shape[2]) for a in sums]
    for part in parts:
        scratch += [pltpu.VMEM((2,) + part, BRAIN)] * 2 + [pltpu.VMEM(part, BRAIN)]
    scratch += [dma((2 * group,))] + [dma((2, 2 * group))] * 2
    scratch += [dma((2, group))] * 2 + [dma((2, line))] * 2 + [dma((2, 2, line))] * 2
    scratch += [dma((group,))] * 2 + [dma((len(steps),))] * 2 + [dma]
    scratch += [dma((len(sums), 2))] * 3 + [dma((len(sums),))] * 3 + [dma((group,))] * 2
    return pl.pallas_call(
        functools.partial(tail_kernel, group, len(sums), steps),
        out_shape=[
            jax.ShapeDtypeStruct(mix, FLOAT),
            jax.ShapeDtypeStruct(routers.shape[1:], FLOAT),
            jax.ShapeDtypeStruct(shared.shape, shared.dtype),
            jax.ShapeDtypeStruct(small.shape, FLOAT),
        ]
        + [jax.ShapeDtypeStruct(shared.shape, BRAIN)]
        + [jax.ShapeDtypeStruct(part, BRAIN) for part in parts[1:]],
        in_specs=[vmem, vmem, any_spec, any_spec, vmem] + [any_spec] * len(sums),
        out_specs=[vmem, vmem, any_spec, vmem] + [any_spec] * len(sums),
        scratch_shapes=scratch,
        compiler_params=pltpu.CompilerParams(collective_id=number, has_side_effects=True, vmem_limit_bytes=62 * MIB),
        name="tail_exchange",
    )(left, right, routers, shared, small, *sums)


def state_setup(step_ref, rate_ref, step_t_ref, rate_t_ref, b_ref, c_ref, cum, cum_t, cross):
    length = step_ref.shape[0]
    down = lax.broadcasted_iota(jnp.int32, (length, length), 0)
    along = lax.broadcasted_iota(jnp.int32, (length, length), 1)
    lower = jnp.where(down >= along, 1.0, 0.0)
    upper = jnp.where(down <= along, 1.0, 0.0)
    cum[...] = jnp.dot(
        lower, step_ref[...] * rate_ref[...], precision=HIGH, preferred_element_type=FLOAT
    )
    cum_t[...] = jnp.dot(
        step_t_ref[...] * rate_t_ref[...], upper, precision=HIGH, preferred_element_type=FLOAT
    )
    cross[...] = lax.dot_general(
        c_ref[...], b_ref[...], (((1,), (1,)), ((), ())), precision=HIGH, preferred_element_type=FLOAT
    )


def decay_of(head, cum, cum_t):
    length, heads = cum.shape
    lane = lax.broadcasted_iota(jnp.int32, (length, heads), 1)
    column = jnp.sum(jnp.where(lane == head, cum[...], 0.0), axis=1, keepdims=True)
    spread_out = column - cum_t[pl.ds(head, 1), :]
    down = lax.broadcasted_iota(jnp.int32, (length, length), 0)
    along = lax.broadcasted_iota(jnp.int32, (length, length), 1)
    return jnp.exp(jnp.where(down >= along, spread_out, -1e30))


def state_forward_kernel(
    x_ref, b_ref, c_ref, step_ref, rate_ref, step_t_ref, rate_t_ref, skip_ref, y_ref, cum, cum_t, cross
):
    pair = pl.program_id(0)

    @pl.when(pair == 0)
    def _():
        state_setup(step_ref, rate_ref, step_t_ref, rate_t_ref, b_ref, c_ref, cum, cum_t, cross)

    values = x_ref[...]
    values_low = values.astype(BRAIN)
    total = values * skip_ref[...]
    side = lax.broadcasted_iota(jnp.int32, values.shape, 1) // MHDIM
    for j in range(2):
        head = 2 * pair + j
        mixing = cross[...] * decay_of(head, cum, cum_t) * step_t_ref[pl.ds(head, 1), :]
        part = jnp.dot(mixing.astype(BRAIN), values_low, preferred_element_type=FLOAT)
        total = total + jnp.where(side == j, part, 0.0)
    y_ref[...] = total


def state_specs(length):
    column = lambda place: pl.BlockSpec((length, NSTATE), place)
    return [
        column(lambda i: (0, i)),
        column(lambda i: (0, DI // NSTATE)),
        column(lambda i: (0, DI // NSTATE + 1)),
        whole_spec((length, MHEADS)),
        whole_spec((1, MHEADS)),
        whole_spec((MHEADS, length)),
        whole_spec((MHEADS, 1)),
        pl.BlockSpec((1, 2 * MHDIM), lambda i: (0, i)),
    ]


def state_operands(conv_out, step_size, decay_rate, skip_gain):
    return (
        conv_out,
        conv_out,
        conv_out,
        step_size,
        decay_rate[None, :],
        step_size.T,
        decay_rate[:, None],
        jnp.repeat(skip_gain, MHDIM)[None, :],
    )


def state_forward(conv_out, step_size, decay_rate, skip_gain):
    length = conv_out.shape[0]
    return pl.pallas_call(
        state_forward_kernel,
        grid=(MHEADS // 2,),
        out_shape=jax.ShapeDtypeStruct((length, DI), FLOAT),
        in_specs=state_specs(length),
        out_specs=pl.BlockSpec((length, 2 * MHDIM), lambda i: (0, i)),
        scratch_shapes=[
            pltpu.VMEM((length, MHEADS), FLOAT),
            pltpu.VMEM((MHEADS, length), FLOAT),
            pltpu.VMEM((length, length), FLOAT),
        ],
        compiler_params=pltpu.CompilerParams(vmem_limit_bytes=32 * MIB),
        name="state_forward",
    )(*state_operands(conv_out, step_size, decay_rate, skip_gain))


def state_backward_kernel(
    x_ref, b_ref, c_ref, step_ref, rate_ref, step_t_ref, rate_t_ref, skip_ref, dy_ref,
    dx_ref, db_ref, dc_ref, row_ref, column_ref, cum, cum_t, cross, dcross,
):
    pair = pl.program_id(0)

    @pl.when(pair == 0)
    def _():
        state_setup(step_ref, rate_ref, step_t_ref, rate_t_ref, b_ref, c_ref, cum, cum_t, cross)
        dcross[...] = jnp.zeros_like(dcross)
        row_ref[...] = jnp.zeros_like(row_ref)

    values_low = x_ref[...].astype(BRAIN)
    grads = dy_ref[...]
    total = grads * skip_ref[...]
    side = lax.broadcasted_iota(jnp.int32, grads.shape, 1) // MHDIM
    lane = lax.broadcasted_iota(jnp.int32, row_ref.shape, 1)
    for j in range(2):
        head = 2 * pair + j
        steps = step_t_ref[pl.ds(head, 1), :]
        decay = decay_of(head, cum, cum_t)
        own = jnp.where(side == j, grads, 0.0).astype(BRAIN)
        mixing = cross[...] * decay
        total = total + matmul_tn((mixing * steps).astype(BRAIN), own)
        dmix = matmul_nt(own, values_low)
        dcross[...] += dmix * decay * steps
        weighed = dmix * mixing
        column_ref[pl.ds(head, 1), :] = jnp.sum(weighed, axis=0, keepdims=True)
        row_sum = jnp.sum(weighed * steps, axis=1, keepdims=True)
        row_ref[...] += jnp.where(lane == head, row_sum, 0.0)
    dx_ref[...] = total

    @pl.when(pair == pl.num_programs(0) - 1)
    def _():
        dc_ref[...] = jnp.dot(dcross[...], b_ref[...], precision=HIGH, preferred_element_type=FLOAT)
        db_ref[...] = lax.dot_general(
            dcross[...], c_ref[...], (((0,), (0,)), ((), ())), precision=HIGH, preferred_element_type=FLOAT
        )


def state_backward(conv_out, step_size, decay_rate, skip_gain, grad_mixed):
    length = conv_out.shape[0]
    pair_block = pl.BlockSpec((length, 2 * MHDIM), lambda i: (0, i))
    dx, db, dc, row_sums, column_sums = pl.pallas_call(
        state_backward_kernel,
        grid=(MHEADS // 2,),
        out_shape=[
            jax.ShapeDtypeStruct((length, DI), FLOAT),
            jax.ShapeDtypeStruct((length, NSTATE), FLOAT),
            jax.ShapeDtypeStruct((length, NSTATE), FLOAT),
            jax.ShapeDtypeStruct((length, MHEADS), FLOAT),
            jax.ShapeDtypeStruct((MHEADS, length), FLOAT),
        ],
        in_specs=state_specs(length) + [pair_block],
        out_specs=[
            pair_block,
            pl.BlockSpec((length, NSTATE), lambda i: (0, 0)),
            pl.BlockSpec((length, NSTATE), lambda i: (0, 0)),
            pl.BlockSpec((length, MHEADS), lambda i: (0, 0)),
            pl.BlockSpec((MHEADS, length), lambda i: (0, 0)),
        ],
        scratch_shapes=[
            pltpu.VMEM((length, MHEADS), FLOAT),
            pltpu.VMEM((MHEADS, length), FLOAT),
            pltpu.VMEM((length, length), FLOAT),
            pltpu.VMEM((length, length), FLOAT),
        ],
        compiler_params=pltpu.CompilerParams(vmem_limit_bytes=32 * MIB),
        name="state_backward",
    )(*state_operands(conv_out, step_size, decay_rate, skip_gain), grad_mixed)
    column_sums = column_sums.T
    dcum = row_sums - column_sums * step_size
    places = jnp.arange(length)
    upper = (places[:, None] <= places[None, :]).astype(FLOAT)
    drate_step = jnp.dot(upper, dcum, precision=HIGH, preferred_element_type=FLOAT)
    grad_step = column_sums + drate_step * decay_rate
    grad_decay_log = jnp.sum(drate_step * step_size, axis=0) * decay_rate
    return dx, db, dc, grad_step, grad_decay_log


def convolve(conv_in, conv_weight, conv_bias):
    length = conv_in.shape[0]
    padded = jnp.pad(conv_in, ((KCONV - 1, 0), (0, 0)))
    total = conv_bias + padded[0:length] * conv_weight[0]
    for tap in range(1, KCONV):
        total = total + padded[tap : tap + length] * conv_weight[tap]
    return silu_of(total)


def gated_norm(mixed, gate_z, mixer_gain):
    return rms_norm(mixed * silu_of(gate_z), mixer_gain)


def step_of(step_raw, step_bias):
    return softplus_of(step_raw + step_bias)


def mixer_forward(hidden, norm_gain, mixer_in, mixer_out, small):
    normed, norm_back = jax.vjp(rms_norm, hidden, norm_gain)
    normed_low = normed.astype(BRAIN)
    projected = matmul(normed_low, mixer_in)
    gate_z = projected[:, :DI]
    conv_in = projected[:, DI : DI + CONVCH]
    step_raw = projected[:, DI + CONVCH :]
    conv_out, conv_back = jax.vjp(convolve, conv_in, small["conv_weight"], small["conv_bias"])
    step_size, step_back = jax.vjp(step_of, step_raw, small["step_bias"])
    decay_rate = -jnp.exp(small["decay_log"])
    mixed = state_forward(conv_out, step_size, decay_rate, small["skip_gain"])
    mixer_norm, gated_back = jax.vjp(gated_norm, mixed, gate_z, small["mixer_gain"])
    mixer_low = mixer_norm.astype(BRAIN)
    output = hidden + matmul_nt(mixer_low, mixer_out)
    saved = (norm_back, normed_low, conv_out, conv_back, step_size, step_back, decay_rate, gated_back, mixer_low)
    return output, saved


def mixer_backward(grad_out, saved, mixer_in, mixer_out, small):
    norm_back, normed_low, conv_out, conv_back, step_size, step_back, decay_rate, gated_back, mixer_low = saved
    grad_low = grad_out.astype(BRAIN)
    grad_mixer_out = matmul_tn(grad_low, mixer_low).astype(BRAIN)
    grad_norm, grad_mixer_out = lax.optimization_barrier((matmul(grad_low, mixer_out), grad_mixer_out))
    grad_mixed, grad_gate, grad_mixer_gain = gated_back(grad_norm)
    dx, db, dc, grad_step, grad_decay_log = state_backward(
        conv_out, step_size, decay_rate, small["skip_gain"], grad_mixed
    )
    grad_skip = jnp.sum(jnp.sum(grad_mixed * conv_out[:, :DI], axis=0).reshape(MHEADS, MHDIM), axis=1)
    grad_conv_in, grad_conv_weight, grad_conv_bias = conv_back(jnp.concatenate([dx, db, dc], axis=1))
    grad_step_raw, grad_step_bias = step_back(grad_step)
    grad_proj = jnp.concatenate([grad_gate, grad_conv_in, grad_step_raw], axis=1).astype(BRAIN)
    grad_hidden, grad_gain = norm_back(matmul_nt(grad_proj, mixer_in))
    grad_small = (
        grad_mixer_gain, grad_conv_weight, grad_conv_bias, grad_decay_log, grad_step_bias, grad_skip
    )
    return grad_out + grad_hidden, grad_gain, normed_low, grad_proj, grad_mixer_out, grad_small


PARTS = 2


def fold(group, held, sent, crossed, below, above, out_ref, sems):
    cross_send, cross_recv, up_send, up_recv, down_send, down_recv = sems
    line = group // 2
    z, x = places(group)[2:]
    rows = held.shape[1] // PARTS

    def piece(ref, d, p):
        return ref.at[d, pl.ds(p * rows, rows)]

    def cross(d, p):
        return remote(
            piece(sent, d, p), piece(crossed, d, p), cross_send.at[d, p], cross_recv.at[d, p], {"expert": 2 * z + 1 - x}
        )

    def rise(d, p):
        return remote(
            piece(held, d, p), piece(below, d, p), up_send.at[d, p], up_recv.at[d, p], {"expert": 2 * (z + 1) + x}
        )

    def fall(d, p):
        return remote(
            piece(held, d, p), piece(above, d, p), down_send.at[d, p], down_recv.at[d, p], {"expert": 2 * (z - 1) + x}
        )

    def add(d, p, final, sources):
        def body(j, carry):
            at = pl.ds(pl.multiple_of(p * rows + j * 16, 16), 16)
            total = held[d, at].astype(FLOAT)
            for source in sources:
                total = total + source[d, at].astype(FLOAT)
            if final:
                out_ref[at] = total
            else:
                held[d, at] = total.astype(held.dtype)
            return carry

        lax.fori_loop(0, rows // 16, body, 0)

    def start_cross(d):
        for p in range(PARTS):
            cross(d, p).start()

    def chain(d):
        for p in range(PARTS):
            cross(d, p).wait_recv()

            @pl.when(d > z)
            def _():
                @pl.when(z > 0)
                def _():
                    rise(d, p).wait_recv()
                    add(d, p, False, [crossed, below])

                @pl.when(z == 0)
                def _():
                    add(d, p, False, [crossed])

                rise(d, p).start()

            @pl.when(d < z)
            def _():
                @pl.when(z < line - 1)
                def _():
                    fall(d, p).wait_recv()
                    add(d, p, False, [crossed, above])

                @pl.when(z == line - 1)
                def _():
                    add(d, p, False, [crossed])

                fall(d, p).start()

    def last():
        for p in range(PARTS):
            cross(z, p).wait_recv()

            @pl.when(z == 0)
            def _():
                fall(z, p).wait_recv()
                add(z, p, True, [crossed, above])

            @pl.when(z == line - 1)
            def _():
                rise(z, p).wait_recv()
                add(z, p, True, [crossed, below])

            @pl.when((z > 0) & (z < line - 1))
            def _():
                fall(z, p).wait_recv()
                rise(z, p).wait_recv()
                add(z, p, True, [crossed, below, above])

    def settle():
        for d in range(line):
            for p in range(PARTS):
                cross(d, p).wait_send()
                pl.when(d > z)(lambda: rise(d, p).wait_send())
                pl.when(d < z)(lambda: fall(d, p).wait_send())

    return start_cross, chain, last, settle


def fold_scratch(group, tokens, width):
    line = group // 2
    dma = pltpu.SemaphoreType.DMA
    return [pltpu.VMEM((line, tokens, width), BRAIN)] * 5 + [dma((line, PARTS))] * 6


def run_blocks(group, compute, held, sent, start_cross, chain, last):
    line = group // 2
    z, x = places(group)[2:]

    def body(j, carry):
        d = farthest(z, line, j // 2)
        crossing = lax.rem(j, 2) == 0

        @pl.when(j == group - 2)
        def _():
            chain(farthest(z, line, 0))

        total = compute(2 * d + jnp.where(crossing, 1 - x, x)).astype(BRAIN)

        @pl.when(crossing)
        def _():
            sent[d] = total
            start_cross(d)

        @pl.when(jnp.logical_not(crossing))
        def _():
            held[d] = total

        return carry

    lax.fori_loop(0, group, body, 0)
    for j in range(1, line - 1):
        chain(farthest(z, line, j))
    last()


def load_blocks(group, source, target, sems):
    z, x = places(group)[2:]

    def load(s):
        return pltpu.make_async_copy(source.at[s], target.at[s], sems.at[s])

    def body(j, carry):
        d = farthest(z, group // 2, j // 2)
        load(2 * d + jnp.where(lax.rem(j, 2) == 0, 1 - x, x)).start()
        return carry

    lax.fori_loop(0, group, body, 0)
    return lambda s: load(s).wait()


def pick_rows(gates):
    tokens = gates.shape[1]
    down = lax.broadcasted_iota(jnp.int32, (tokens, tokens), 0)
    along = lax.broadcasted_iota(jnp.int32, (tokens, tokens), 1)
    upper = jnp.where(down <= along, 1.0, 0.0).astype(BRAIN)
    live = jnp.where(gates != 0.0, 1.0, 0.0)
    place = jnp.dot(
        jnp.broadcast_to(live, (8, tokens)).astype(BRAIN), upper, preferred_element_type=FLOAT
    )[0:1] - 1.0
    ranks = lax.broadcasted_iota(jnp.int32, (PICKED, tokens), 0).astype(FLOAT)
    return (ranks == place) & (live > 0.0)


def expert_forward_kernel(
    group, x_hbm, g_ref, in_ref, out_ref, sin_ref, sout_ref, y_ref, xe_ref, gu_ref, sgu_ref,
    rows_ref, held, sent, crossed, below, above, *sems,
):
    z, x = places(group)[2:]
    wait_load = load_blocks(group, x_hbm, rows_ref, sems[6])
    greet(line_peers(z, x, group // 2))
    start_cross, chain, last, settle = fold(group, held, sent, crossed, below, above, y_ref, sems[:6])

    def compute(s):
        wait_load(s)
        rows = rows_ref[s]
        shared_gu = jnp.dot(rows, sin_ref[...], preferred_element_type=FLOAT)
        half = shared_gu.shape[1] // 2
        shared_mid = (silu_of(shared_gu[:, :half]) * shared_gu[:, half:]).astype(BRAIN)
        sgu_ref[s] = shared_gu.astype(sgu_ref.dtype)
        total = matmul_nt(shared_mid, sout_ref[...])
        for e in range(in_ref.shape[0]):
            gates = g_ref[s, e : e + 1, :]
            hit = pick_rows(gates)
            picked = jnp.dot(
                jnp.where(hit, 1.0, 0.0).astype(BRAIN), rows, preferred_element_type=FLOAT
            ).astype(BRAIN)
            gate_up = jnp.dot(picked, in_ref[e], preferred_element_type=FLOAT)
            width = gate_up.shape[1] // 2
            inner = (silu_of(gate_up[:, :width]) * gate_up[:, width:]).astype(BRAIN)
            result = matmul_nt(inner, out_ref[e]).astype(BRAIN)
            total = total + matmul_tn(jnp.where(hit, gates, 0.0).astype(BRAIN), result)
            xe_ref[e, s] = picked
            gu_ref[e, s] = gate_up.astype(gu_ref.dtype)
        return total

    run_blocks(group, compute, held, sent, start_cross, chain, last)
    settle()


def expert_forward(rows, gates, expert_in, expert_out, shared_in, shared_out, number):
    group, tokens, width = rows.shape
    local = expert_in.shape[0]
    inner = expert_in.shape[2]
    vmem = pl.BlockSpec(memory_space=pltpu.VMEM)
    dma = pltpu.SemaphoreType.DMA
    return pl.pallas_call(
        functools.partial(expert_forward_kernel, group),
        out_shape=[
            jax.ShapeDtypeStruct((tokens, width), FLOAT),
            jax.ShapeDtypeStruct((local, group, PICKED, width), BRAIN),
            jax.ShapeDtypeStruct((local, group, PICKED, inner), BRAIN),
            jax.ShapeDtypeStruct((group, tokens, shared_in.shape[1]), BRAIN),
        ],
        in_specs=[pl.BlockSpec(memory_space=pl.ANY)] + [vmem] * 5,
        out_specs=[vmem] * 4,
        scratch_shapes=[pltpu.VMEM(rows.shape, BRAIN)] + fold_scratch(group, tokens, width) + [dma((group,))],
        compiler_params=pltpu.CompilerParams(collective_id=number, has_side_effects=True, vmem_limit_bytes=60 * MIB),
        name="expert_forward",
    )(rows, gates, expert_in, expert_out, shared_in, shared_out)


def swiglu_back(gate, up, grad):
    sig = jax.nn.sigmoid(gate)
    act = gate * sig
    return grad * up * (sig + act * (1.0 - sig)), grad * act, act * up


def expert_backward_kernel(
    group, d_hbm, g_ref, gu_ref, sgu_ref, in_ref, out_ref, sin_ref, sout_ref,
    dx_ref, dg_ref, dgu_ref, dres_ref, mid_ref, dsgu_ref, smid_ref,
    rows_ref, dgates, held, sent, crossed, below, above, *sems,
):
    z, x = places(group)[2:]
    me = 2 * z + x
    gate_send, gate_recv = sems[7:9]
    wait_load = load_blocks(group, d_hbm, rows_ref, sems[6])
    greet([(None, {"expert": lax.rem(me + k, group)}) for k in range(1, group)])
    start_cross, chain, last, settle = fold(group, held, sent, crossed, below, above, dx_ref, sems[:6])

    def give(s):
        return remote(dgates.at[s], dg_ref.at[me], gate_send.at[s], gate_recv.at[me], {"expert": s})

    def compute(s):
        wait_load(s)
        grads = rows_ref[s]
        shared_gu = sgu_ref[s].astype(FLOAT)
        half = shared_gu.shape[1] // 2
        dmid = jnp.dot(grads, sout_ref[...], preferred_element_type=FLOAT)
        dgate, dup, shared_mid = swiglu_back(shared_gu[:, :half], shared_gu[:, half:], dmid)
        shared_d = jnp.concatenate([dgate, dup], axis=1).astype(BRAIN)
        dsgu_ref[s] = shared_d
        smid_ref[s] = shared_mid.astype(BRAIN)
        total = matmul_nt(shared_d, sin_ref[...])
        for e in range(in_ref.shape[0]):
            gates = g_ref[s, e : e + 1, :]
            hit = pick_rows(gates)
            chosen = jnp.where(hit, 1.0, 0.0).astype(BRAIN)
            weight = jnp.sum(jnp.where(hit, gates, 0.0), axis=1, keepdims=True)
            picked = jnp.dot(chosen, grads, preferred_element_type=FLOAT)
            dres_ref[e, s] = (picked * weight).astype(BRAIN)
            raw = jnp.dot(picked.astype(BRAIN), out_ref[e], preferred_element_type=FLOAT)
            gate_up = gu_ref[e, s].astype(FLOAT)
            width = gate_up.shape[1] // 2
            dgate, dup, inner = swiglu_back(gate_up[:, :width], gate_up[:, width:], raw * weight)
            inner_low = inner.astype(BRAIN)
            mid_ref[e, s] = inner_low
            dweight = jnp.sum(raw * inner_low.astype(FLOAT), axis=1, keepdims=True)
            dgates[s, e : e + 1, :] = jnp.sum(jnp.where(hit, dweight, 0.0), axis=0, keepdims=True)
            dgu = jnp.concatenate([dgate, dup], axis=1).astype(BRAIN)
            dgu_ref[e, s] = dgu
            back = matmul_nt(dgu, in_ref[e]).astype(BRAIN)
            total = total + matmul_tn(chosen, back)
        pl.when(s != me)(lambda: give(s).start())
        return total

    run_blocks(group, compute, held, sent, start_cross, chain, last)
    dg_ref[me] = dgates[me]
    for k in range(1, group):
        source = lax.rem(me + k, group)
        remote(dgates.at[source], dg_ref.at[source], gate_send.at[source], gate_recv.at[source], {"expert": source}).wait_recv()
        give(source).wait_send()
    settle()


def expert_backward(grads, gates, gate_up, shared_gu, expert_in, expert_out, shared_in, shared_out, number):
    group, tokens, width = grads.shape
    local = expert_in.shape[0]
    inner = expert_in.shape[2]
    vmem = pl.BlockSpec(memory_space=pltpu.VMEM)
    dma = pltpu.SemaphoreType.DMA
    return pl.pallas_call(
        functools.partial(expert_backward_kernel, group),
        out_shape=[
            jax.ShapeDtypeStruct((tokens, width), FLOAT),
            jax.ShapeDtypeStruct((group, local, tokens), FLOAT),
            jax.ShapeDtypeStruct((local, group, PICKED, inner), BRAIN),
            jax.ShapeDtypeStruct((local, group, PICKED, width), BRAIN),
            jax.ShapeDtypeStruct((local, group, PICKED, inner // 2), BRAIN),
            jax.ShapeDtypeStruct(shared_gu.shape, BRAIN),
            jax.ShapeDtypeStruct(shared_gu.shape[:2] + (shared_gu.shape[2] // 2,), BRAIN),
        ],
        in_specs=[pl.BlockSpec(memory_space=pl.ANY)] + [vmem] * 7,
        out_specs=[vmem] * 7,
        scratch_shapes=[pltpu.VMEM(grads.shape, BRAIN), pltpu.VMEM((group, local, tokens), FLOAT)]
        + fold_scratch(group, tokens, width)
        + [dma((group,))] * 3,
        compiler_params=pltpu.CompilerParams(collective_id=number, has_side_effects=True, vmem_limit_bytes=62 * MIB),
        name="expert_backward",
    )(grads, gates, gate_up, shared_gu, expert_in, expert_out, shared_in, shared_out)


def moe_forward(hidden, routes, valid, norm_gain, router, pieces):
    group = lax.axis_size("expert")
    local = pieces[0].shape[0]
    normed, norm_back = jax.vjp(rms_norm, hidden, norm_gain)
    normed_low = normed.astype(BRAIN)
    logits = matmul(normed_low, router)
    chosen = jnp.any(routes[:, :, None] == jnp.arange(router.shape[1])[None, None, :], axis=1)
    largest = jnp.max(jnp.where(chosen, logits, -jnp.inf), axis=1, keepdims=True)
    raised = jnp.where(chosen, jnp.exp(jnp.where(chosen, logits - largest, 0.0)), 0.0)
    probs = raised / jnp.sum(raised, axis=1, keepdims=True)
    gates = probs * valid[:, None]
    if lax.axis_size("dp") == 4:
        rows_all, gates_all, expert_in, expert_out, shared = spread([normed_low, gates.T], pieces, [], group, 1)
    else:
        rows_all, gates_all = spread([normed_low, gates.T], [], [], group, 1)
        expert_in, expert_out, shared = [lax.all_gather(p, "dp", axis=1, tiled=True) for p in pieces]
    part = shared.shape[2] // 3
    weights = (router, shared[0, :, : 2 * part], shared[0, :, 2 * part :], expert_in, expert_out)
    own_gates = lax.dynamic_slice_in_dim(gates_all, lax.axis_index("expert") * local, local, axis=1)
    routed, picked, gate_up, shared_gu = expert_forward(rows_all, own_gates, expert_in, expert_out, *weights[1:3], 2)
    return hidden + routed, (norm_back, normed_low, probs, rows_all, own_gates, picked, gate_up, shared_gu, weights)


def moe_backward(grad_out, saved, valid, grads_all, earlier):
    norm_back, normed_low, probs, rows_all, own_gates, picked, gate_up, shared_gu, weights = saved
    router, shared_in, shared_out, expert_in, expert_out = weights
    group = lax.axis_size("expert")
    local, width, inner = expert_in.shape
    if grads_all is None:
        if lax.axis_size("dp") == 4:
            grads_all, *earlier = spread([grad_out.astype(BRAIN)], [], earlier, group, 3)
        else:
            grads_all = spread([grad_out.astype(BRAIN)], [], [], group, 3)[0]
            earlier = [scatter_expert(s) for s in earlier]
    grad_normed, grad_gates, dgate_up, dresult, middle, dshared, shared_mid = expert_backward(
        grads_all, own_gates, gate_up, shared_gu, expert_in, expert_out, shared_in, shared_out, 4
    )
    rows_of = lambda array: array.reshape(local, -1, array.shape[-1])
    by_expert = lambda left, right: lax.dot_general(
        rows_of(left), rows_of(right), (((1,), (1,)), ((0,), (0,))), preferred_element_type=FLOAT
    ).astype(BRAIN)
    flat = lambda array: array.reshape(-1, array.shape[-1])
    shared_grads = [matmul_tn(flat(rows_all), flat(dshared)), matmul_tn(flat(grads_all), flat(shared_mid))]
    sums = [
        jnp.concatenate(shared_grads, axis=1).astype(BRAIN)[None],
        by_expert(picked, dgate_up),
        by_expert(dresult, middle),
    ]
    grad_probs = grad_gates.reshape(-1, grad_gates.shape[2]).T * valid[:, None]
    grad_logits = probs * (grad_probs - jnp.sum(probs * grad_probs, axis=1, keepdims=True))
    logits_low = grad_logits.astype(BRAIN)
    grad_router = matmul_tn(normed_low, logits_low).astype(BRAIN)
    grad_hidden, grad_gain = norm_back(grad_normed + matmul_nt(logits_low, router))
    return grad_out + grad_hidden, grad_gain, grad_router, sums, earlier


def attend_scores(query, key_rows):
    length = query.shape[0]
    down = lax.broadcasted_iota(jnp.int32, (length, length), 0)
    along = lax.broadcasted_iota(jnp.int32, (length, length), 1)
    scores = jnp.where(down >= along, matmul_nt(query, key_rows) * AHDIM ** (-0.5), -1e30)
    raised = jnp.exp(scores - jnp.max(scores, axis=1, keepdims=True))
    return raised / jnp.sum(raised, axis=1, keepdims=True)


def attention_forward_kernel(q_ref, k_ref, v_ref, o_ref):
    for j in range(AHEADS // KVHEADS):
        part = slice(j * AHDIM, (j + 1) * AHDIM)
        probs = attend_scores(q_ref[:, part], k_ref[...])
        o_ref[:, part] = matmul(probs.astype(BRAIN), v_ref[...]).astype(BRAIN)


def attention_specs(length):
    queries = pl.BlockSpec((length, QD // KVHEADS), lambda h: (0, h))
    keys = pl.BlockSpec((length, AHDIM), lambda h: (0, QD // AHDIM + h))
    values = pl.BlockSpec((length, AHDIM), lambda h: (0, (QD + KVD) // AHDIM + h))
    return [queries, keys, values]


def attention_core(qkv):
    length = qkv.shape[0]
    specs = attention_specs(length)
    return pl.pallas_call(
        attention_forward_kernel,
        grid=(KVHEADS,),
        out_shape=jax.ShapeDtypeStruct((length, QD), BRAIN),
        in_specs=specs,
        out_specs=specs[0],
        compiler_params=pltpu.CompilerParams(vmem_limit_bytes=32 * MIB),
        name="attention_forward",
    )(qkv, qkv, qkv)


def attention_backward_kernel(q_ref, k_ref, v_ref, d_ref, dq_ref, dk_ref, dv_ref):
    keys = k_ref[...]
    values = v_ref[...]
    dkeys = jnp.zeros(keys.shape, FLOAT)
    dvalues = jnp.zeros(keys.shape, FLOAT)
    for j in range(AHEADS // KVHEADS):
        part = slice(j * AHDIM, (j + 1) * AHDIM)
        query = q_ref[:, part]
        grads = d_ref[:, part]
        probs = attend_scores(query, keys)
        dprobs = matmul_nt(grads, values)
        dvalues = dvalues + matmul_tn(probs.astype(BRAIN), grads)
        inner = jnp.sum(probs * dprobs, axis=1, keepdims=True)
        draw = (probs * (dprobs - inner) * AHDIM ** (-0.5)).astype(BRAIN)
        dq_ref[:, part] = matmul(draw, keys).astype(BRAIN)
        dkeys = dkeys + matmul_tn(draw, query)
    dk_ref[...] = dkeys.astype(BRAIN)
    dv_ref[...] = dvalues.astype(BRAIN)


def attention_core_back(qkv, grads):
    length = qkv.shape[0]
    specs = attention_specs(length)
    head_block = pl.BlockSpec((length, AHDIM), lambda h: (0, h))
    return pl.pallas_call(
        attention_backward_kernel,
        grid=(KVHEADS,),
        out_shape=[
            jax.ShapeDtypeStruct((length, QD), BRAIN),
            jax.ShapeDtypeStruct((length, KVD), BRAIN),
            jax.ShapeDtypeStruct((length, KVD), BRAIN),
        ],
        in_specs=specs + [specs[0]],
        out_specs=[specs[0], head_block, head_block],
        compiler_params=pltpu.CompilerParams(vmem_limit_bytes=32 * MIB),
        name="attention_backward",
    )(qkv, qkv, qkv, grads)


def attention_forward(hidden, norm_gain, attn_qkv, attn_out):
    normed, norm_back = jax.vjp(rms_norm, hidden, norm_gain)
    normed_low = normed.astype(BRAIN)
    qkv = matmul(normed_low, attn_qkv).astype(BRAIN)
    attended = attention_core(qkv)
    output = hidden + matmul_nt(attended, attn_out)
    return output, (norm_back, normed_low, qkv, attended)


def attention_backward(grad_out, saved, attn_qkv, attn_out):
    norm_back, normed_low, qkv, attended = saved
    grad_low = grad_out.astype(BRAIN)
    grad_attn_out = matmul_tn(grad_low, attended).astype(BRAIN)
    grad_attended = matmul(grad_low, attn_out).astype(BRAIN)
    grad_qkv = jnp.concatenate(attention_core_back(qkv, grad_attended), axis=1)
    grad_attn_qkv = matmul_tn(normed_low, grad_qkv).astype(BRAIN)
    grad_hidden, grad_gain = norm_back(matmul_nt(grad_qkv, attn_qkv))
    return grad_out + grad_hidden, grad_gain, grad_attn_qkv, grad_attn_out


def gather_dense(array):
    return lax.all_gather(array, BOTH, axis=0, tiled=True)


def scatter_dense(array):
    return lax.psum_scatter(array, BOTH, scatter_dimension=0, tiled=True).astype(FLOAT)


def scatter_expert(array):
    return lax.psum_scatter(array, "dp", scatter_dimension=1, tiled=True).astype(FLOAT)


def shared_columns(shared):
    group = lax.axis_size("expert")
    rows = shared[0].shape[0]
    pieces = []
    for shared_in, shared_out in zip(shared[0::2], shared[1::2]):
        half = shared_in.shape[1] // 2
        pieces += [shared_in[:, :half], shared_in[:, half:], shared_out]
    cut = [piece.reshape(rows, group, -1) for piece in pieces]
    return jnp.transpose(jnp.concatenate(cut, axis=2), (1, 0, 2))


def shared_whole(own):
    part = own.shape[2] // 6

    def columns(index):
        piece = jnp.transpose(own[:, :, index * part : (index + 1) * part], (1, 0, 2))
        return piece.reshape(piece.shape[0], -1)

    return [
        jnp.concatenate([columns(0), columns(1)], axis=1),
        columns(2),
        jnp.concatenate([columns(3), columns(4)], axis=1),
        columns(5),
    ]


def exchange(blocks):
    return lax.all_to_all(blocks, "expert", split_axis=0, concat_axis=0, tiled=True)


def first_gather(dense, shared, rows):
    if lax.axis_size("dp") == 4:
        *dense, shared, rows = head_exchange(dense, shared, rows, 5)
        return [array.reshape(-1, array.shape[2]) for array in dense], shared, rows
    rows = spread([rows], [], [], lax.axis_size("expert"), 3)[0]
    return [gather_dense(array) for array in dense], exchange(shared), rows


def last_sums(left, right, routers, small, sums_a, shared_b):
    group = lax.axis_size("expert")
    cut = lambda array: array.reshape(group, -1, array.shape[-1])
    shared_b = cut(shared_b.astype(BRAIN))
    if lax.axis_size("dp") == 4:
        routers = routers.reshape(4 * group, -1, routers.shape[1])
        return tail_exchange(left.T, right, routers, shared_b, small, sums_a, 6)
    mix = matmul_tn(left, right).astype(BRAIN)
    shared_a, *sums_a = [scatter_expert(s) for s in sums_a]
    shared_a = exchange(cut(shared_a.astype(BRAIN)))
    return scatter_dense(mix), scatter_dense(routers), exchange(shared_b), lax.psum(small, BOTH), shared_a, *sums_a


def per_device(
    layer_input, cotangent, lengths, routes_a, routes_b,
    mixer_in, mixer_out, router_a, shared_in_a, shared_out_a, expert_in_a, expert_out_a,
    attn_qkv, attn_out, router_b, shared_in_b, shared_out_b, expert_in_b, expert_out_b,
    norm_gains, mixer_gain, conv_weight, conv_bias, decay_log, step_bias, skip_gain,
):
    small = {
        "conv_weight": conv_weight,
        "conv_bias": conv_bias,
        "decay_log": decay_log,
        "step_bias": step_bias,
        "skip_gain": skip_gain,
        "mixer_gain": mixer_gain,
    }
    assert lengths.shape[0] == 1 and layer_input.shape[0] == SLOT_LEN
    group = lax.axis_size("expert")
    experts = router_a.shape[1]
    valid = (jnp.arange(SLOT_LEN) < lengths[0]).astype(FLOAT)
    grad = cotangent * valid[:, None]
    (w_mixer_in, w_mixer_out, w_routers), w_shared, last_rows = first_gather(
        [mixer_in, mixer_out, jnp.concatenate([router_a, router_b], axis=1)],
        shared_columns([shared_in_a, shared_out_a, shared_in_b, shared_out_b]),
        grad.astype(BRAIN),
    )
    w_shared = w_shared.reshape(1, -1, w_shared.shape[2])
    half = w_shared.shape[2] // 2
    attn_qkv, attn_out, w_routers = lax.optimization_barrier((attn_qkv, attn_out, w_routers))
    w_qkv = gather_dense(attn_qkv)
    w_attn_out = gather_dense(attn_out)
    hidden = layer_input.astype(FLOAT)
    hidden, saved_mix = mixer_forward(hidden, norm_gains[0], w_mixer_in, w_mixer_out, small)
    hidden, saved_a = moe_forward(
        hidden, routes_a, valid, norm_gains[1], w_routers[:, :experts], [expert_in_a, expert_out_a, w_shared[:, :, :half]]
    )
    hidden, saved_attn = attention_forward(hidden, norm_gains[2], w_qkv, w_attn_out)
    layer_output, saved_b = moe_forward(
        hidden, routes_b, valid, norm_gains[3], w_routers[:, experts:], [expert_in_b, expert_out_b, w_shared[:, :, half:]]
    )
    grad, gain_four, d_router_b, sums_b, _ = moe_backward(grad, saved_b, valid, last_rows, [])
    grad, gain_three, d_qkv, d_attn_out = attention_backward(grad, saved_attn, w_qkv, w_attn_out)
    grad, d_qkv, d_attn_out = lax.optimization_barrier((grad, d_qkv, d_attn_out))
    d_qkv, d_attn_out = scatter_dense(d_qkv), scatter_dense(d_attn_out)
    grad, gain_two, d_router_a, sums_a, sums_b = moe_backward(grad, saved_a, valid, None, sums_b)
    d_shared_b, d_in_b, d_out_b = sums_b
    grad, gain_one, mix_left, mix_right, d_mixer_out, grad_small = mixer_backward(
        grad, saved_mix, w_mixer_in, w_mixer_out, small
    )
    d_mixer_out = scatter_dense(d_mixer_out)
    parts = [jnp.stack([gain_one, gain_two, gain_three, gain_four])] + list(grad_small)
    flat = jnp.concatenate([part.reshape(-1) for part in parts])
    padded = jnp.pad(flat, (0, -flat.shape[0] % 1024)).reshape(-1, 128)
    d_mixer_in, d_routers, d_shared_b, summed, d_shared_a, d_in_a, d_out_a = last_sums(
        mix_left, mix_right, jnp.concatenate([d_router_a, d_router_b], axis=1), padded, sums_a, d_shared_b
    )
    d_in_a, d_out_a = d_in_a.astype(FLOAT), d_out_a.astype(FLOAT)
    d_shared = shared_whole(jnp.concatenate([d_shared_a, d_shared_b], axis=2).astype(FLOAT))
    summed = summed.reshape(-1)
    sums = []
    place = 0
    for part in parts:
        sums.append(summed[place : place + part.size].reshape(part.shape))
        place += part.size
    return (
        layer_output, grad,
        d_mixer_in, d_mixer_out, d_routers[:, :experts], d_shared[0], d_shared[1], d_in_a, d_out_a,
        d_qkv, d_attn_out, d_routers[:, experts:], d_shared[2], d_shared[3], d_in_b, d_out_b,
        *sums,
    )


def solution(mesh):
    rows = P(BOTH, None)
    expert = P("expert", "dp", None)
    first = (rows, rows, rows, rows, rows, expert, expert)
    second = (rows, rows, rows, rows, rows, expert, expert)
    return jax.shard_map(
        per_device,
        mesh=mesh,
        in_specs=(rows, rows, P(BOTH), rows, rows) + first + second + (P(),) * 7,
        out_specs=(rows, rows) + first + second + (P(),) * 7,
        check_vma=False,
    )
```

```python
import functools

import jax
import jax.numpy as jnp
from jax import lax
from jax.experimental import pallas as pl
from jax.experimental.pallas import tpu as pltpu
from jax.sharding import PartitionSpec as P

MHEADS = 48
MHDIM = 64
NSTATE = 128
KCONV = 4
AHEADS = 12
KVHEADS = 4
AHDIM = 128
SLOT_LEN = 256
HALF = 128
CAP = 60
DI = 3072
CONVCH = 3328
QD = 1536
KVD = 512
QKV = 2560

EPS = 1e-05
HIGH = lax.Precision.HIGHEST
FLOAT = jnp.float32
BRAIN = jnp.bfloat16
MESH = pl.DeviceIdType.MESH
BOTH = ("dp", "expert")
PICKED = SLOT_LEN // HALF * 64
MIB = 2**20


def matmul(left, right):
    return jnp.dot(left, right, preferred_element_type=FLOAT)


def matmul_nt(left, right):
    return lax.dot_general(left, right, (((1,), (1,)), ((), ())), preferred_element_type=FLOAT)


def matmul_tn(left, right):
    return lax.dot_general(left, right, (((0,), (0,)), ((), ())), preferred_element_type=FLOAT)


def silu_of(values):
    return values * jax.nn.sigmoid(values)


def softplus_of(values):
    return jnp.log1p(jnp.exp(values))


def rms_norm(values, norm_gain):
    return values * lax.rsqrt(jnp.mean(values * values, axis=-1, keepdims=True) + EPS) * norm_gain


def whole_spec(shape):
    return pl.BlockSpec(shape, lambda *at: (0,) * len(shape), pipeline_mode=pl.Buffered(1))


def places(group):
    q = lax.axis_index("dp")
    e = lax.axis_index("expert")
    return q // 2, lax.rem(q, 2), e // 2, lax.rem(e, 2)


def greet(peers):
    barrier = pltpu.get_barrier_semaphore()
    count = 0
    for condition, device in peers:

        def hello():
            pl.semaphore_signal(barrier, inc=1, device_id=device, device_id_type=MESH)

        if condition is None:
            hello()
            count = count + 1
        else:
            pl.when(condition)(hello)
            count = count + jnp.where(condition, 1, 0)
    pl.semaphore_wait(barrier, count)


def line_peers(z, x, line):
    return [
        (None, {"expert": 2 * z + 1 - x}),
        (z > 0, {"expert": 2 * (z - 1) + x}),
        (z < line - 1, {"expert": 2 * (z + 1) + x}),
    ]


def remote(src, dst, send_sem, recv_sem, device):
    return pltpu.make_async_remote_copy(
        src_ref=src, dst_ref=dst, send_sem=send_sem, recv_sem=recv_sem, device_id=device, device_id_type=MESH
    )


def spread_kernel(count, wide, sums, group, *refs):
    total = count + wide
    every = total + sums
    ins, outs = refs[:every], refs[every : 2 * every]
    stages = refs[2 * every : 2 * every + wide]
    sum_bufs = refs[2 * every + wide : 2 * every + wide + 3 * sums]
    sems = refs[2 * every + wide + 3 * sums :]
    sum_sems = sems[-5:]
    up_sems, down_sems, cross_sems, recv_sems, own_sems = sems[:5]
    line = group // 2
    y, c, z, x = places(group)
    sibling, opposite = {"dp": 2 * y + 1 - c}, {"dp": 2 * (1 - y) + c}
    greet(line_peers(z, x, line) + ([(None, sibling), (None, opposite)] if wide or sums else []))

    def copy(i, src, place, sem, device):
        return remote(src, outs[i].at[place], sem, recv_sems.at[i, place], {"expert": device})

    def moves(i, s, rising):
        zz = z - s if rising else z + s
        place = 2 * zz + x
        src = ins[i] if s == 0 else outs[i].at[place]
        up = functools.partial(copy, i, src, place, up_sems.at[i, s], 2 * (z + 1) + x)
        down = functools.partial(copy, i, src, place, down_sems.at[i, s], 2 * (z - 1) + x)
        cross = functools.partial(copy, i, src, place, cross_sems.at[i, zz], 2 * z + 1 - x)
        return up, down, cross

    def steps(act):
        for s in range(line):
            for rising in (True, False) if s else (True,):
                valid = (z - s >= 0) if rising else (z + s < line)

                @pl.when(valid)
                def _():
                    for i in range(count):
                        act(i, s, rising, *moves(i, s, rising))

    def block(i, q):
        rows = ins[i].shape[1]
        return outs[i].at[:, pl.ds(pl.multiple_of(q * rows, rows), rows), :]

    def wide_copy(i, kind):
        wide_send, wide_recv = sems[5:7]
        own, other = 2 * y + c, 2 * (1 - y) + c
        k = i - count
        if kind == 0:
            return remote(ins[i], block(i, own), wide_send.at[k, 0], wide_recv.at[k, 0], sibling)
        if kind == 1:
            return remote(ins[i], block(i, own), wide_send.at[k, 1], wide_recv.at[k, 1], opposite)
        return remote(block(i, other), block(i, other), wide_send.at[k, 2], wide_recv.at[k, 2], sibling)

    def own_copy(i):
        if i < count:
            return pltpu.make_async_copy(ins[i], outs[i].at[2 * z + x], own_sems.at[i])
        return pltpu.make_async_copy(ins[i], stages[i - count], own_sems.at[i])

    def own_store(i):
        return pltpu.make_async_copy(stages[i - count], block(i, 2 * y + c), own_sems.at[i])

    def forward(i, s, rising, up, down, cross):
        if s:
            cross().wait_recv()
        if rising:
            pl.when(z < line - 1)(lambda: up().start())
        if not rising or s == 0:
            pl.when(z > 0)(lambda: down().start())
        cross().start()

    def settle(i, s, rising, up, down, cross):
        if rising:
            pl.when(z < line - 1)(lambda: up().wait_send())
        if not rising or s == 0:
            pl.when(z > 0)(lambda: down().wait_send())
        cross().wait_send()

    def sum_parts(k):
        kept, landed, arrived = sum_bufs[3 * k : 3 * k + 3]
        own, core_send, core_recv, side_send, side_recv = sum_sems
        source = ins[total + k]
        rows = source.shape[1] // 4

        def piece(q):
            return source.at[:, pl.ds(pl.multiple_of(q * rows, rows), rows), :]

        def load(h):
            return pltpu.make_async_copy(piece(2 * h + c), kept.at[h], own.at[k, h])

        def to_sibling(h):
            return remote(piece(2 * h + 1 - c), landed.at[h], core_send.at[k, h], core_recv.at[k, h], sibling)

        def to_opposite():
            return remote(kept.at[1 - y], arrived, side_send.at[k], side_recv.at[k], opposite)

        def add(target, lead, sources):
            for e in range(source.shape[0]):
                add_blocks((target, lead + (e,), None), [(ref, at + (e,), None) for ref, at in sources], rows)

        return kept, landed, arrived, load, to_sibling, to_opposite, add

    for k in range(sums):
        load, to_sibling = sum_parts(k)[3:5]
        for h in (1 - y, y):
            to_sibling(h).start()
            load(h).start()
    for i in range(count, total):
        wide_copy(i, 1).start()
        wide_copy(i, 0).start()
    for i in range(total):
        own_copy(i).start()
    for i in range(count, total):
        own_copy(i).wait()
        own_store(i).start()
    if sums:
        steps(lambda *move: forward(*move) if move[1] == 0 else None)
        for k in range(sums):
            kept, landed, arrived, load, to_sibling, to_opposite, add = sum_parts(k)
            load(1 - y).wait()
            to_sibling(1 - y).wait_recv()
            add(kept, (1 - y,), [(kept, (1 - y,)), (landed, (1 - y,))])
            to_opposite().start()
        steps(lambda *move: forward(*move) if move[1] else None)
    else:
        steps(forward)
    for i in range(count, total):
        wide_copy(i, 1).wait_recv()
        wide_copy(i, 2).start()
    for i in range(count):
        for zz in range(line):
            place = 2 * zz + 1 - x
            copy(i, ins[i], place, own_sems.at[i], 2 * z + 1 - x).wait_recv()
    steps(settle)
    for i in range(count, total):
        wide_copy(i, 0).wait()
        wide_copy(i, 1).wait_send()
        wide_copy(i, 2).wait()
    for i in range(count):
        own_copy(i).wait()
    for i in range(count, total):
        own_store(i).wait()
    for k in range(sums):
        kept, landed, arrived, load, to_sibling, to_opposite, add = sum_parts(k)
        load(y).wait()
        to_sibling(y).wait_recv()
        to_opposite().wait_recv()
        add(outs[total + k], (), [(kept, (y,)), (landed, (y,)), (arrived, ())])
        for h in range(2):
            to_sibling(h).wait_send()
        to_opposite().wait_send()


def spread(arrays, wide, sums, group, number):
    n, w, s, line = len(arrays), len(wide), len(sums), group // 2
    split = lax.axis_size("dp")
    dma = pltpu.SemaphoreType.DMA
    any_spec = pl.BlockSpec(memory_space=pl.ANY)
    vmem = pl.BlockSpec(memory_space=pltpu.VMEM)
    shapes = [jax.ShapeDtypeStruct((group,) + a.shape, a.dtype) for a in arrays]
    shapes += [jax.ShapeDtypeStruct((a.shape[0], split * a.shape[1], a.shape[2]), a.dtype) for a in wide]
    scratch = [pltpu.VMEM(a.shape, a.dtype) for a in wide]
    for a in sums:
        part = (a.shape[0], a.shape[1] // 4, a.shape[2])
        scratch += [pltpu.VMEM((2,) + part, a.dtype)] * 2 + [pltpu.VMEM(part, a.dtype)]
        shapes.append(jax.ShapeDtypeStruct(part, FLOAT))
    scratch += [dma((n, line)), dma((n, line)), dma((n, line)), dma((n, group)), dma((n + w,))]
    if w:
        scratch += [dma((w, 3)), dma((w, 3))]
    if s:
        scratch += [dma((s, 2))] * 3 + [dma((s,))] * 2
    return pl.pallas_call(
        functools.partial(spread_kernel, n, w, s, group),
        out_shape=shapes,
        in_specs=[any_spec] * (n + w + s),
        out_specs=[any_spec] * (n + w) + [vmem] * s,
        scratch_shapes=scratch,
        compiler_params=pltpu.CompilerParams(collective_id=number, has_side_effects=True, vmem_limit_bytes=40 * MIB),
        name="spread%d" % number,
    )(*arrays, *wide, *sums)


def add_blocks(target, sources, rows):
    step = min(rows, 16)

    def body(j, carry):
        at = pl.ds(pl.multiple_of(j * step, step), step)

        def view(item):
            ref, lead, columns = item
            return ref, tuple(lead) + (at,) + (() if columns is None else (columns,))

        total = None
        for item in sources:
            ref, index = view(item)
            value = ref[index].astype(FLOAT)
            total = value if total is None else total + value
        ref, index = view(target)
        ref[index] = total.astype(ref.dtype)
        return carry

    lax.fori_loop(0, rows // step, body, 0)


def head_kernel(group, cut, dense, *refs):
    ins, outs = refs[: dense + 2], refs[dense + 2 : 2 * dense + 4]
    own_sems, send_sems, recv_sems, swap_send, swap_recv, row_send, row_recv = refs[2 * dense + 4 :]
    shared_ref, shared_out = ins[dense], outs[dense]
    row_ref, row_out = ins[dense + 1], outs[dense + 1]
    line = group // 2
    y, c, z, x = places(group)
    sibling, opposite = {"dp": 2 * y + 1 - c}, {"dp": 2 * (1 - y) + c}
    rising, falling, across = {"expert": 2 * (z + 1) + x}, {"expert": 2 * (z - 1) + x}, {"expert": 2 * z + 1 - x}
    me = 2 * z + x
    peers = [(None, {"expert": lax.rem(me + k, group)}) for k in range(1, group)]
    greet(peers + [(None, sibling), (None, opposite)])
    width = ins[0].shape[1]
    pieces = [(0, pl.ds(0, cut), True), (0, pl.ds(cut, width - cut), False)]
    pieces += [(i, pl.ds(0, ins[i].shape[1]), True) for i in range(1, dense)]
    count = len(pieces)

    def copy(p, yy, cc, zz, xx, way, device, own=False):
        i, columns, _ = pieces[p]
        place = (2 * yy + cc) * group + 2 * zz + xx
        dst = outs[i].at[place, :, columns]
        src = ins[i].at[:, columns] if own else dst
        slot = yy * group + 2 * zz + xx
        return remote(src, dst, send_sems.at[p, slot, way], recv_sems.at[p, place], device)

    def row_copy(zz, xx, way, device, own=False):
        dst = row_out.at[2 * zz + xx]
        return remote(row_ref if own else dst, dst, row_send.at[zz, way], row_recv.at[2 * zz + xx], device)

    def swap(k):
        to = lax.rem(me + k, group)
        return remote(shared_ref.at[to], shared_out.at[me], swap_send.at[k], swap_recv.at[me], {"expert": to})

    def own_copy(i):
        if i < dense:
            return pltpu.make_async_copy(ins[i], outs[i].at[(2 * y + c) * group + me], own_sems.at[i])
        if i == dense:
            return pltpu.make_async_copy(shared_ref.at[me], shared_out.at[me], own_sems.at[i])
        return pltpu.make_async_copy(row_ref, row_out.at[me], own_sems.at[i])

    def steps(act):
        for s in range(line):
            for up in (True, False) if s else (True,):
                zz = z - s if up else z + s
                valid = (z - s >= 0) if up else (z + s < line)

                @pl.when(valid)
                def _():
                    act(s, up, zz)

    def column_moves(p, s, up, zz):
        own = s == 0
        make = functools.partial(row_copy, zz, x) if p is None else functools.partial(copy, p, y, c, zz, x)
        moves = []
        if up:
            moves.append((z < line - 1, functools.partial(make, 0, rising, own)))
        if not up or own:
            moves.append((z > 0, functools.partial(make, 1, falling, own)))
        moves.append((None, functools.partial(make, 2, across, own)))
        if p is not None:
            moves.append((None, functools.partial(make, 3, opposite, own)))
            moves.append((None, functools.partial(make, 4, sibling, own)))
        return moves

    def run(moves, act):
        for condition, move in moves:
            if condition is None:
                act(move())
            else:
                pl.when(condition)(lambda: act(move()))

    def later_moves(p):
        if pieces[p][2]:
            return [
                (0, [(3, opposite), (4, sibling)], (y, 1 - x)),
                (1, [(4, sibling)], (1 - y, x)),
                (1, [(4, sibling)], (1 - y, 1 - x)),
            ]
        return [
            (0, [(2, across), (4, sibling)], (1 - y, x)),
            (1, [(4, sibling)], (y, 1 - x)),
            (1, [(4, sibling)], (1 - y, 1 - x)),
        ]

    everything = list(range(count)) + [None]

    def column(s, up, zz):
        for p in range(count):
            if s:
                copy(p, y, c, zz, x, 4, sibling).wait_recv()
            run(column_moves(p, s, up, zz), lambda item: item.start())
        if s == 0:
            for k in range(1, group):
                swap(k).start()
            for i in range(dense + 2):
                own_copy(i).start()

    def rows(s, up, zz):
        if s:
            row_copy(zz, x, 2, across).wait_recv()
        run(column_moves(None, s, up, zz), lambda item: item.start())

    def later(phase, start):
        def act(s, up, zz):
            for p in range(count):
                for when, sends, (yy, xx) in later_moves(p):
                    if when != phase:
                        continue
                    if start:
                        copy(p, yy, c, zz, xx, 4, sibling).wait_recv()
                    for way, device in sends:
                        item = copy(p, yy, c, zz, xx, way, device)
                        if start:
                            item.start()
                        else:
                            item.wait_send()

        return act

    def finish(s, up, zz):
        row_copy(zz, 1 - x, 2, across).wait_recv()
        for p in range(count):
            for yy in range(2):
                for xx in range(2):
                    copy(p, yy, 1 - c, zz, xx, 4, sibling).wait_recv()

    def settle(s, up, zz):
        for p in everything:
            run(column_moves(p, s, up, zz), lambda item: item.wait_send())

    only = lambda act, k: steps(lambda s, up, zz: act(s, up, zz) if s == k else None)
    for k in range(line + 2):
        if k < line:
            only(column, k)
            only(rows, k)
        if 0 <= k - 1 < line:
            only(later(0, True), k - 1)
        if 0 <= k - 2 < line:
            only(later(1, True), k - 2)
    steps(finish)
    steps(settle)
    steps(later(0, False))
    steps(later(1, False))
    for k in range(1, group):
        source = lax.rem(me + k, group)
        remote(shared_ref.at[source], shared_out.at[source], swap_send.at[k], swap_recv.at[source], across).wait_recv()
        swap(k).wait_send()
    for i in range(dense + 2):
        own_copy(i).wait()


def head_exchange(dense, shared, rows, number):
    group = lax.axis_size("expert")
    total = 4 * group
    count = len(dense) + 1
    dma = pltpu.SemaphoreType.DMA
    any_spec = pl.BlockSpec(memory_space=pl.ANY)
    cut = dense[0].shape[1] * 9 // 10 // 128 * 128
    return pl.pallas_call(
        functools.partial(head_kernel, group, cut, len(dense)),
        out_shape=[jax.ShapeDtypeStruct((total,) + a.shape, a.dtype) for a in dense]
        + [
            jax.ShapeDtypeStruct(shared.shape, shared.dtype),
            jax.ShapeDtypeStruct((group,) + rows.shape, rows.dtype),
        ],
        in_specs=[any_spec] * (len(dense) + 2),
        out_specs=[any_spec] * (len(dense) + 2),
        scratch_shapes=[
            dma((len(dense) + 2,)),
            dma((count, 2 * group, 5)),
            dma((count, total)),
            dma((group,)),
            dma((group,)),
            dma((group // 2, 3)),
            dma((group,)),
        ],
        compiler_params=pltpu.CompilerParams(collective_id=number, has_side_effects=True),
        name="head_exchange",
    )(*dense, shared, rows)


def farthest(z, line, j):
    table = [sorted(range(line), key=lambda d: (-abs(d - k), d)) for k in range(line)]
    return sum(
        jnp.where((z == k) & (j == n), table[k][n], 0) for k in range(line) for n in range(line) if table[k][n]
    )


def tail_kernel(group, sums, steps, *refs):
    (left_ref, right_ref, router_ref, shared_ref, small_ref) = refs[:5]
    sum_ins, refs = refs[5 : 5 + sums], refs[5 + sums :]
    (mix_out, router_out, shared_out, small_out) = refs[:4]
    sum_outs, refs = refs[4 : 4 + sums], refs[4 + sums :]
    bufs = refs[:12]
    made, totals, small_landed = refs[12:15]
    sum_bufs, refs = refs[15 : 15 + 3 * sums], refs[15 + 3 * sums :]
    sum_own, sum_core_send, sum_core_recv, sum_side_send, sum_side_recv, sum_store, late_send, late_recv = refs[-8:]
    (own_sems, core_send, core_recv, one_send, one_recv, two_send, two_recv, line_send, line_recv,
     swap_send, swap_recv, small_send, small_recv, keep_sem) = refs[:-8]
    line = group // 2
    y, c, z, x = places(group)
    sibling, opposite = {"dp": 2 * y + 1 - c}, {"dp": 2 * (1 - y) + c}
    rising, falling, across = {"expert": 2 * (z + 1) + x}, {"expert": 2 * (z - 1) + x}, {"expert": 2 * z + 1 - x}
    me = 2 * z + x

    def partner(axis, bit):
        here = lax.axis_index(axis)
        return {axis: here + bit * (1 - 2 * lax.rem(here // bit, 2))}

    peers = [(None, {"expert": lax.rem(me + k, group)}) for k in range(1, group)]
    greet(peers + [(None, sibling), (None, opposite)])

    outs = (mix_out, router_out)
    held, landed, one, two, below, above = (bufs[0:2], bufs[2:4], bufs[4:6], bufs[6:8], bufs[8:10], bufs[10:12])
    rows, width = mix_out.shape
    pieces = [(0, pl.ds(0, width), False), (1, pl.ds(0, router_ref.shape[2]), True)]
    count = len(pieces)

    def slot(yy, zz, xx):
        return yy * group + 2 * zz + xx

    def load(yy, zz, xx):
        s = slot(yy, zz, xx)
        return pltpu.make_async_copy(router_ref.at[(2 * yy + c) * group + 2 * zz + xx], held[1].at[s], own_sems.at[s])

    def to_sibling(a, yy, zz, xx, turn=0):
        s = slot(yy, zz, xx)
        source = made.at[4 * turn + 2 * yy + xx] if a == 0 else router_ref.at[(2 * yy + 1 - c) * group + 2 * zz + xx]
        return remote(source, landed[a].at[s], core_send.at[a, s], core_recv.at[a, s], sibling)

    def make(cc, zz, target, place_of):
        lefts = []
        for yy in range(2):
            start = pl.multiple_of(((2 * yy + cc) * group + 2 * zz) * rows, 16)
            lefts.append(left_ref[pl.ds(start, 2 * rows)])
        lefts = jnp.concatenate(lefts, axis=0)
        step = 1664
        for start in range(0, width, step):
            columns = slice(start, min(start + step, width))
            product = jnp.dot(lefts, right_ref[:, columns], preferred_element_type=FLOAT).astype(BRAIN)
            for yy in range(2):
                for xx in range(2):
                    place = (2 * yy + xx) * rows
                    target[place_of(yy, xx), :, columns] = product[place : place + rows]

    def stage_one(p, zz, k):
        a, columns, over_y = pieces[p]
        s = slot(1 - y, zz, k) if over_y else slot(k, zz, 1 - x)
        return remote(
            held[a].at[s, :, columns], one[a].at[2 * zz + k, :, columns], one_send.at[p, 2 * zz + k],
            one_recv.at[p, 2 * zz + k], opposite if over_y else across,
        )

    def stage_two(p, zz):
        a, columns, over_y = pieces[p]
        s = slot(y, zz, 1 - x) if over_y else slot(1 - y, zz, x)
        return remote(
            held[a].at[s, :, columns], two[a].at[zz, :, columns], two_send.at[p, zz], two_recv.at[p, zz],
            across if over_y else opposite,
        )

    def rise(a, zz):
        return remote(held[a].at[slot(y, zz, x)], below[a].at[zz], line_send.at[a, 0, zz], line_recv.at[a, 0, zz], rising)

    def fall(a, zz):
        return remote(held[a].at[slot(y, zz, x)], above[a].at[zz], line_send.at[a, 1, zz], line_recv.at[a, 1, zz], falling)

    def swap(k):
        to = lax.rem(me + k, group)
        return remote(shared_ref.at[to], shared_out.at[me], swap_send.at[k], swap_recv.at[me], {"expert": to})

    def small(step):
        axis, bit = steps[step]
        return remote(
            totals.at[step], small_landed.at[step], small_send.at[step], small_recv.at[step], partner(axis, bit)
        )

    keep = pltpu.make_async_copy(shared_ref.at[me], shared_out.at[me], keep_sem)
    keep.start()
    corners = [(yy, xx) for yy in range(2) for xx in range(2)]
    for zz in range(line):
        for yy, xx in corners:
            to_sibling(1, yy, zz, xx).start()
            load(yy, zz, xx).start()
    for k in range(1, group):
        swap(k).start()
    totals[0] = small_ref[...]
    small(0).start()

    def advance(step):
        if step < len(steps):
            small(step).wait()
            totals[step + 1] = totals[step] + small_landed[step]
            if step + 1 < len(steps):
                small(step + 1).start()

    def phase_make(zz, t):
        turn = lax.rem(t, 2)

        @pl.when(t >= 2)
        def _():
            for yy, xx in corners:
                to_sibling(0, yy, farthest(z, line, t - 2), xx, turn).wait_send()

        make(1 - c, zz, made, lambda yy, xx: 4 * turn + 2 * yy + xx)
        for yy, xx in corners:
            to_sibling(0, yy, zz, xx, turn).start()
        make(c, zz, held[0], lambda yy, xx: slot(yy, zz, xx))

    def sum_parts(k):
        kept, landed, arrived = sum_bufs[3 * k : 3 * k + 3]
        source = sum_ins[k]
        height = source.shape[1] // 4

        def piece(q):
            return source.at[:, pl.ds(pl.multiple_of(q * height, height), height), :]

        def take(h):
            return pltpu.make_async_copy(piece(2 * h + c), kept.at[h], sum_own.at[k, h])

        def give(h):
            return remote(piece(2 * h + 1 - c), landed.at[h], sum_core_send.at[k, h], sum_core_recv.at[k, h], sibling)

        def pass_on():
            return remote(kept.at[1 - y], arrived, sum_side_send.at[k], sum_side_recv.at[k], opposite)

        def add(h, extra):
            for e in range(source.shape[0]):
                items = [(kept, (h, e), None), (landed, (h, e), None)] + ([(arrived, (e,), None)] if extra else [])
                add_blocks((kept, (h, e), None), items, height)

        def store():
            return pltpu.make_async_copy(kept.at[y], sum_outs[k], sum_store.at[k])

        return take, give, pass_on, add, store

    def sums_first():
        for k in range(sums):
            take, give, pass_on, add, store = sum_parts(k)
            take(1 - y).wait()
            give(1 - y).wait_recv()
            add(1 - y, False)
            pass_on().start()

    def late(k):
        to = lax.rem(me + k, group)
        height = sum_outs[0].shape[1]
        block = sum_bufs[0].at[y, 0, pl.ds(pl.multiple_of(to * height, 16), height)]
        if k == 0:
            return pltpu.make_async_copy(block, sum_outs[0].at[me], late_send.at[k])
        return remote(block, sum_outs[0].at[me], late_send.at[k], late_recv.at[me], {"expert": to})

    def sums_last(which):
        for k in which:
            take, give, pass_on, add, store = sum_parts(k)
            take(y).wait()
            give(y).wait_recv()
            pass_on().wait_recv()
            add(y, True)
            if k:
                store().start()
            else:
                for n in range(group):
                    late(n).start()

    def sums_settle():
        for k in range(sums):
            take, give, pass_on, add, store = sum_parts(k)
            give(y).wait_send()
            give(1 - y).wait_send()
            pass_on().wait_send()
            if k:
                store().wait()
        late(0).wait()
        for n in range(1, group):
            source = lax.rem(me + n, group)
            remote(
                shared_ref.at[source], sum_outs[0].at[source], late_send.at[n], late_recv.at[source], across
            ).wait_recv()
            late(n).wait_send()

    def phase_a(zz):
        for a in range(2):
            for yy, xx in corners:
                s = slot(yy, zz, xx)
                if a == 1:
                    load(yy, zz, xx).wait()
                to_sibling(a, yy, zz, xx).wait_recv()
                add_blocks((held[a], (s,), None), [(held[a], (s,), None), (landed[a], (s,), None)], rows)
        for p in range(count):
            for k in range(2):
                stage_one(p, zz, k).start()

    def phase_b(zz):
        for p, (a, columns, over_y) in enumerate(pieces):
            for k in (1 - x, x) if over_y else (1 - y, y):
                s = slot(y, zz, k) if over_y else slot(k, zz, x)
                stage_one(p, zz, k).wait_recv()
                add_blocks(
                    (held[a], (s,), columns), [(held[a], (s,), columns), (one[a], (2 * zz + k,), columns)], rows
                )
            stage_two(p, zz).start()

    def phase_c(zz):
        s = slot(y, zz, x)
        for p in range(count):
            stage_two(p, zz).wait_recv()
        for a in range(2):
            base = [(held[a], (s,), None), (two[a], (zz,), None)]
            low = (below[a], (zz,), None)
            high = (above[a], (zz,), None)
            kept = (held[a], (s,), None)

            @pl.when(zz > z)
            def _():
                @pl.when(z > 0)
                def _():
                    rise(a, zz).wait_recv()
                    add_blocks(kept, base + [low], rows)

                @pl.when(z == 0)
                def _():
                    add_blocks(kept, base, rows)

                rise(a, zz).start()

            @pl.when(zz < z)
            def _():
                @pl.when(z < line - 1)
                def _():
                    fall(a, zz).wait_recv()
                    add_blocks(kept, base + [high], rows)

                @pl.when(z == line - 1)
                def _():
                    add_blocks(kept, base, rows)

                fall(a, zz).start()

    def phase_last():
        s = slot(y, z, x)
        for p in range(count):
            stage_two(p, z).wait_recv()
        for a in range(2):
            base = [(held[a], (s,), None), (two[a], (z,), None)]
            low = (below[a], (z,), None)
            high = (above[a], (z,), None)
            final = (outs[a], (), None)

            @pl.when(z == 0)
            def _():
                fall(a, z).wait_recv()
                add_blocks(final, base + [high], rows)

            @pl.when(z == line - 1)
            def _():
                rise(a, z).wait_recv()
                add_blocks(final, base + [low], rows)

            @pl.when((z > 0) & (z < line - 1))
            def _():
                fall(a, z).wait_recv()
                rise(a, z).wait_recv()
                add_blocks(final, base + [low, high], rows)

    for k in range(sums):
        take, give = sum_parts(k)[:2]
        for h in (1 - y, y):
            take(h).start()
            give(h).start()

    def body(t, carry):
        for shift, phase, number in ((0, phase_make, line), (1, phase_a, line), (2, phase_b, line), (3, phase_c, line - 1)):

            @pl.when((t >= shift) & (t - shift < number))
            def _():
                phase(farthest(z, line, t - shift), *([t] if shift == 0 else []))

        pl.when(t == 0)(sums_first)
        pl.when(t == 4)(lambda: sums_last([0]))
        for step in range(len(steps)):
            pl.when(t == step + 1)(functools.partial(advance, step))
        return carry

    lax.fori_loop(0, max(line + 3, len(steps) + 1), body, 0)
    phase_last()
    sums_last(range(1, sums))
    sums_settle()
    for t in (line - 2, line - 1):
        for yy, xx in corners:
            to_sibling(0, yy, farthest(z, line, t), xx, t % 2).wait_send()
    small_out[...] = totals[len(steps)]
    for k in range(1, group):
        source = lax.rem(me + k, group)
        remote(shared_ref.at[source], shared_out.at[source], swap_send.at[k], swap_recv.at[source], across).wait_recv()
        swap(k).wait_send()
    keep.wait()
    for zz in range(line):
        for a in range(2):
            if a == 1:
                for yy, xx in corners:
                    to_sibling(a, yy, zz, xx).wait_send()
            pl.when(zz > z)(lambda: rise(a, zz).wait_send())
            pl.when(zz < z)(lambda: fall(a, zz).wait_send())
        for p in range(count):
            for k in range(2):
                stage_one(p, zz, k).wait_send()
            stage_two(p, zz).wait_send()


def tail_exchange(left, right, routers, shared, small, sums, number):
    group = lax.axis_size("expert")
    line = group // 2
    steps = []
    for axis in BOTH:
        bit = 1
        while bit < lax.axis_size(axis):
            steps.append((axis, bit))
            bit *= 2
    dma = pltpu.SemaphoreType.DMA
    vmem = pl.BlockSpec(memory_space=pltpu.VMEM)
    any_spec = pl.BlockSpec(memory_space=pl.ANY)
    mix = (left.shape[0] // (4 * group), right.shape[1])
    scratch = []
    for blocks in (2 * group, 2 * group, group, line, line, line):
        scratch += [pltpu.VMEM((blocks,) + shape, BRAIN) for shape in (mix, routers.shape[1:])]
    scratch += [pltpu.VMEM((8,) + mix, BRAIN)]
    scratch += [pltpu.VMEM((len(steps) + 1,) + small.shape, FLOAT), pltpu.VMEM((len(steps),) + small.shape, FLOAT)]
    parts = [(a.shape[0], a.shape[1] // 4, a.shape[2]) for a in sums]
    for part in parts:
        scratch += [pltpu.VMEM((2,) + part, BRAIN)] * 2 + [pltpu.VMEM(part, BRAIN)]
    scratch += [dma((2 * group,))] + [dma((2, 2 * group))] * 2
    scratch += [dma((2, group))] * 2 + [dma((2, line))] * 2 + [dma((2, 2, line))] * 2
    scratch += [dma((group,))] * 2 + [dma((len(steps),))] * 2 + [dma]
    scratch += [dma((len(sums), 2))] * 3 + [dma((len(sums),))] * 3 + [dma((group,))] * 2
    return pl.pallas_call(
        functools.partial(tail_kernel, group, len(sums), steps),
        out_shape=[
            jax.ShapeDtypeStruct(mix, FLOAT),
            jax.ShapeDtypeStruct(routers.shape[1:], FLOAT),
            jax.ShapeDtypeStruct(shared.shape, shared.dtype),
            jax.ShapeDtypeStruct(small.shape, FLOAT),
        ]
        + [jax.ShapeDtypeStruct(shared.shape, BRAIN)]
        + [jax.ShapeDtypeStruct(part, BRAIN) for part in parts[1:]],
        in_specs=[vmem, vmem, any_spec, any_spec, vmem] + [any_spec] * len(sums),
        out_specs=[vmem, vmem, any_spec, vmem] + [any_spec] * len(sums),
        scratch_shapes=scratch,
        compiler_params=pltpu.CompilerParams(collective_id=number, has_side_effects=True, vmem_limit_bytes=62 * MIB),
        name="tail_exchange",
    )(left, right, routers, shared, small, *sums)


def state_setup(step_ref, rate_ref, step_t_ref, rate_t_ref, b_ref, c_ref, cum, cum_t, cross):
    length = step_ref.shape[0]
    down = lax.broadcasted_iota(jnp.int32, (length, length), 0)
    along = lax.broadcasted_iota(jnp.int32, (length, length), 1)
    lower = jnp.where(down >= along, 1.0, 0.0)
    upper = jnp.where(down <= along, 1.0, 0.0)
    cum[...] = jnp.dot(
        lower, step_ref[...] * rate_ref[...], precision=HIGH, preferred_element_type=FLOAT
    )
    cum_t[...] = jnp.dot(
        step_t_ref[...] * rate_t_ref[...], upper, precision=HIGH, preferred_element_type=FLOAT
    )
    cross[...] = lax.dot_general(
        c_ref[...], b_ref[...], (((1,), (1,)), ((), ())), precision=HIGH, preferred_element_type=FLOAT
    )


def decay_of(head, cum, cum_t):
    length, heads = cum.shape
    lane = lax.broadcasted_iota(jnp.int32, (length, heads), 1)
    column = jnp.sum(jnp.where(lane == head, cum[...], 0.0), axis=1, keepdims=True)
    spread_out = column - cum_t[pl.ds(head, 1), :]
    down = lax.broadcasted_iota(jnp.int32, (length, length), 0)
    along = lax.broadcasted_iota(jnp.int32, (length, length), 1)
    return jnp.exp(jnp.where(down >= along, spread_out, -1e30))


def state_forward_kernel(
    x_ref, b_ref, c_ref, step_ref, rate_ref, step_t_ref, rate_t_ref, skip_ref, y_ref, cum, cum_t, cross
):
    pair = pl.program_id(0)

    @pl.when(pair == 0)
    def _():
        state_setup(step_ref, rate_ref, step_t_ref, rate_t_ref, b_ref, c_ref, cum, cum_t, cross)

    values = x_ref[...]
    values_low = values.astype(BRAIN)
    total = values * skip_ref[...]
    side = lax.broadcasted_iota(jnp.int32, values.shape, 1) // MHDIM
    for j in range(2):
        head = 2 * pair + j
        mixing = cross[...] * decay_of(head, cum, cum_t) * step_t_ref[pl.ds(head, 1), :]
        part = jnp.dot(mixing.astype(BRAIN), values_low, preferred_element_type=FLOAT)
        total = total + jnp.where(side == j, part, 0.0)
    y_ref[...] = total


def state_specs(length):
    column = lambda place: pl.BlockSpec((length, NSTATE), place)
    return [
        column(lambda i: (0, i)),
        column(lambda i: (0, DI // NSTATE)),
        column(lambda i: (0, DI // NSTATE + 1)),
        whole_spec((length, MHEADS)),
        whole_spec((1, MHEADS)),
        whole_spec((MHEADS, length)),
        whole_spec((MHEADS, 1)),
        pl.BlockSpec((1, 2 * MHDIM), lambda i: (0, i)),
    ]


def state_operands(conv_out, step_size, decay_rate, skip_gain):
    return (
        conv_out,
        conv_out,
        conv_out,
        step_size,
        decay_rate[None, :],
        step_size.T,
        decay_rate[:, None],
        jnp.repeat(skip_gain, MHDIM)[None, :],
    )


def state_forward(conv_out, step_size, decay_rate, skip_gain):
    length = conv_out.shape[0]
    return pl.pallas_call(
        state_forward_kernel,
        grid=(MHEADS // 2,),
        out_shape=jax.ShapeDtypeStruct((length, DI), FLOAT),
        in_specs=state_specs(length),
        out_specs=pl.BlockSpec((length, 2 * MHDIM), lambda i: (0, i)),
        scratch_shapes=[
            pltpu.VMEM((length, MHEADS), FLOAT),
            pltpu.VMEM((MHEADS, length), FLOAT),
            pltpu.VMEM((length, length), FLOAT),
        ],
        compiler_params=pltpu.CompilerParams(vmem_limit_bytes=32 * MIB),
        name="state_forward",
    )(*state_operands(conv_out, step_size, decay_rate, skip_gain))


def state_backward_kernel(
    x_ref, b_ref, c_ref, step_ref, rate_ref, step_t_ref, rate_t_ref, skip_ref, dy_ref,
    dx_ref, db_ref, dc_ref, row_ref, column_ref, cum, cum_t, cross, dcross,
):
    pair = pl.program_id(0)

    @pl.when(pair == 0)
    def _():
        state_setup(step_ref, rate_ref, step_t_ref, rate_t_ref, b_ref, c_ref, cum, cum_t, cross)
        dcross[...] = jnp.zeros_like(dcross)
        row_ref[...] = jnp.zeros_like(row_ref)

    values_low = x_ref[...].astype(BRAIN)
    grads = dy_ref[...]
    total = grads * skip_ref[...]
    side = lax.broadcasted_iota(jnp.int32, grads.shape, 1) // MHDIM
    lane = lax.broadcasted_iota(jnp.int32, row_ref.shape, 1)
    for j in range(2):
        head = 2 * pair + j
        steps = step_t_ref[pl.ds(head, 1), :]
        decay = decay_of(head, cum, cum_t)
        own = jnp.where(side == j, grads, 0.0).astype(BRAIN)
        mixing = cross[...] * decay
        total = total + matmul_tn((mixing * steps).astype(BRAIN), own)
        dmix = matmul_nt(own, values_low)
        dcross[...] += dmix * decay * steps
        weighed = dmix * mixing
        column_ref[pl.ds(head, 1), :] = jnp.sum(weighed, axis=0, keepdims=True)
        row_sum = jnp.sum(weighed * steps, axis=1, keepdims=True)
        row_ref[...] += jnp.where(lane == head, row_sum, 0.0)
    dx_ref[...] = total

    @pl.when(pair == pl.num_programs(0) - 1)
    def _():
        dc_ref[...] = jnp.dot(dcross[...], b_ref[...], precision=HIGH, preferred_element_type=FLOAT)
        db_ref[...] = lax.dot_general(
            dcross[...], c_ref[...], (((0,), (0,)), ((), ())), precision=HIGH, preferred_element_type=FLOAT
        )


def state_backward(conv_out, step_size, decay_rate, skip_gain, grad_mixed):
    length = conv_out.shape[0]
    pair_block = pl.BlockSpec((length, 2 * MHDIM), lambda i: (0, i))
    dx, db, dc, row_sums, column_sums = pl.pallas_call(
        state_backward_kernel,
        grid=(MHEADS // 2,),
        out_shape=[
            jax.ShapeDtypeStruct((length, DI), FLOAT),
            jax.ShapeDtypeStruct((length, NSTATE), FLOAT),
            jax.ShapeDtypeStruct((length, NSTATE), FLOAT),
            jax.ShapeDtypeStruct((length, MHEADS), FLOAT),
            jax.ShapeDtypeStruct((MHEADS, length), FLOAT),
        ],
        in_specs=state_specs(length) + [pair_block],
        out_specs=[
            pair_block,
            pl.BlockSpec((length, NSTATE), lambda i: (0, 0)),
            pl.BlockSpec((length, NSTATE), lambda i: (0, 0)),
            pl.BlockSpec((length, MHEADS), lambda i: (0, 0)),
            pl.BlockSpec((MHEADS, length), lambda i: (0, 0)),
        ],
        scratch_shapes=[
            pltpu.VMEM((length, MHEADS), FLOAT),
            pltpu.VMEM((MHEADS, length), FLOAT),
            pltpu.VMEM((length, length), FLOAT),
            pltpu.VMEM((length, length), FLOAT),
        ],
        compiler_params=pltpu.CompilerParams(vmem_limit_bytes=32 * MIB),
        name="state_backward",
    )(*state_operands(conv_out, step_size, decay_rate, skip_gain), grad_mixed)
    column_sums = column_sums.T
    dcum = row_sums - column_sums * step_size
    places = jnp.arange(length)
    upper = (places[:, None] <= places[None, :]).astype(FLOAT)
    drate_step = jnp.dot(upper, dcum, precision=HIGH, preferred_element_type=FLOAT)
    grad_step = column_sums + drate_step * decay_rate
    grad_decay_log = jnp.sum(drate_step * step_size, axis=0) * decay_rate
    return dx, db, dc, grad_step, grad_decay_log


def convolve(conv_in, conv_weight, conv_bias):
    length = conv_in.shape[0]
    padded = jnp.pad(conv_in, ((KCONV - 1, 0), (0, 0)))
    total = conv_bias + padded[0:length] * conv_weight[0]
    for tap in range(1, KCONV):
        total = total + padded[tap : tap + length] * conv_weight[tap]
    return silu_of(total)


def gated_norm(mixed, gate_z, mixer_gain):
    return rms_norm(mixed * silu_of(gate_z), mixer_gain)


def step_of(step_raw, step_bias):
    return softplus_of(step_raw + step_bias)


def mixer_forward(hidden, norm_gain, mixer_in, mixer_out, small):
    normed, norm_back = jax.vjp(rms_norm, hidden, norm_gain)
    normed_low = normed.astype(BRAIN)
    projected = matmul(normed_low, mixer_in)
    gate_z = projected[:, :DI]
    conv_in = projected[:, DI : DI + CONVCH]
    step_raw = projected[:, DI + CONVCH :]
    conv_out, conv_back = jax.vjp(convolve, conv_in, small["conv_weight"], small["conv_bias"])
    step_size, step_back = jax.vjp(step_of, step_raw, small["step_bias"])
    decay_rate = -jnp.exp(small["decay_log"])
    mixed = state_forward(conv_out, step_size, decay_rate, small["skip_gain"])
    mixer_norm, gated_back = jax.vjp(gated_norm, mixed, gate_z, small["mixer_gain"])
    mixer_low = mixer_norm.astype(BRAIN)
    output = hidden + matmul_nt(mixer_low, mixer_out)
    saved = (norm_back, normed_low, conv_out, conv_back, step_size, step_back, decay_rate, gated_back, mixer_low)
    return output, saved


def mixer_backward(grad_out, saved, mixer_in, mixer_out, small):
    norm_back, normed_low, conv_out, conv_back, step_size, step_back, decay_rate, gated_back, mixer_low = saved
    grad_low = grad_out.astype(BRAIN)
    grad_mixer_out = matmul_tn(grad_low, mixer_low).astype(BRAIN)
    grad_norm, grad_mixer_out = lax.optimization_barrier((matmul(grad_low, mixer_out), grad_mixer_out))
    grad_mixed, grad_gate, grad_mixer_gain = gated_back(grad_norm)
    dx, db, dc, grad_step, grad_decay_log = state_backward(
        conv_out, step_size, decay_rate, small["skip_gain"], grad_mixed
    )
    grad_skip = jnp.sum(jnp.sum(grad_mixed * conv_out[:, :DI], axis=0).reshape(MHEADS, MHDIM), axis=1)
    grad_conv_in, grad_conv_weight, grad_conv_bias = conv_back(jnp.concatenate([dx, db, dc], axis=1))
    grad_step_raw, grad_step_bias = step_back(grad_step)
    grad_proj = jnp.concatenate([grad_gate, grad_conv_in, grad_step_raw], axis=1).astype(BRAIN)
    grad_hidden, grad_gain = norm_back(matmul_nt(grad_proj, mixer_in))
    grad_small = (
        grad_mixer_gain, grad_conv_weight, grad_conv_bias, grad_decay_log, grad_step_bias, grad_skip
    )
    return grad_out + grad_hidden, grad_gain, normed_low, grad_proj, grad_mixer_out, grad_small


PARTS = 2


def fold(group, held, sent, crossed, below, above, out_ref, sems):
    cross_send, cross_recv, up_send, up_recv, down_send, down_recv = sems
    line = group // 2
    z, x = places(group)[2:]
    rows = held.shape[1] // PARTS

    def piece(ref, d, p):
        return ref.at[d, pl.ds(p * rows, rows)]

    def cross(d, p):
        return remote(
            piece(sent, d, p), piece(crossed, d, p), cross_send.at[d, p], cross_recv.at[d, p], {"expert": 2 * z + 1 - x}
        )

    def rise(d, p):
        return remote(
            piece(held, d, p), piece(below, d, p), up_send.at[d, p], up_recv.at[d, p], {"expert": 2 * (z + 1) + x}
        )

    def fall(d, p):
        return remote(
            piece(held, d, p), piece(above, d, p), down_send.at[d, p], down_recv.at[d, p], {"expert": 2 * (z - 1) + x}
        )

    def add(d, p, final, sources):
        def body(j, carry):
            at = pl.ds(pl.multiple_of(p * rows + j * 16, 16), 16)
            total = held[d, at].astype(FLOAT)
            for source in sources:
                total = total + source[d, at].astype(FLOAT)
            if final:
                out_ref[at] = total
            else:
                held[d, at] = total.astype(held.dtype)
            return carry

        lax.fori_loop(0, rows // 16, body, 0)

    def start_cross(d):
        for p in range(PARTS):
            cross(d, p).start()

    def chain(d):
        for p in range(PARTS):
            cross(d, p).wait_recv()

            @pl.when(d > z)
            def _():
                @pl.when(z > 0)
                def _():
                    rise(d, p).wait_recv()
                    add(d, p, False, [crossed, below])

                @pl.when(z == 0)
                def _():
                    add(d, p, False, [crossed])

                rise(d, p).start()

            @pl.when(d < z)
            def _():
                @pl.when(z < line - 1)
                def _():
                    fall(d, p).wait_recv()
                    add(d, p, False, [crossed, above])

                @pl.when(z == line - 1)
                def _():
                    add(d, p, False, [crossed])

                fall(d, p).start()

    def last():
        for p in range(PARTS):
            cross(z, p).wait_recv()

            @pl.when(z == 0)
            def _():
                fall(z, p).wait_recv()
                add(z, p, True, [crossed, above])

            @pl.when(z == line - 1)
            def _():
                rise(z, p).wait_recv()
                add(z, p, True, [crossed, below])

            @pl.when((z > 0) & (z < line - 1))
            def _():
                fall(z, p).wait_recv()
                rise(z, p).wait_recv()
                add(z, p, True, [crossed, below, above])

    def settle():
        for d in range(line):
            for p in range(PARTS):
                cross(d, p).wait_send()
                pl.when(d > z)(lambda: rise(d, p).wait_send())
                pl.when(d < z)(lambda: fall(d, p).wait_send())

    return start_cross, chain, last, settle


def fold_scratch(group, tokens, width):
    line = group // 2
    dma = pltpu.SemaphoreType.DMA
    return [pltpu.VMEM((line, tokens, width), BRAIN)] * 5 + [dma((line, PARTS))] * 6


def run_blocks(group, compute, held, sent, start_cross, chain, last, between=None):
    line = group // 2
    z, x = places(group)[2:]

    def body(j, carry):
        d = farthest(z, line, j // 2)
        crossing = lax.rem(j, 2) == 0

        @pl.when(j == group - 2)
        def _():
            chain(farthest(z, line, 0))

        total = compute(2 * d + jnp.where(crossing, 1 - x, x)).astype(BRAIN)

        @pl.when(crossing)
        def _():
            sent[d] = total
            start_cross(d)

        @pl.when(jnp.logical_not(crossing))
        def _():
            held[d] = total

        return carry

    lax.fori_loop(0, group, body, 0)
    for j in range(1, line - 1):
        chain(farthest(z, line, j))
        if between is not None:
            between(j - 1, line - 2)
    last()


def load_blocks(group, source, target, sems):
    z, x = places(group)[2:]

    def load(s):
        return pltpu.make_async_copy(source.at[s], target.at[s], sems.at[s])

    def body(j, carry):
        d = farthest(z, group // 2, j // 2)
        load(2 * d + jnp.where(lax.rem(j, 2) == 0, 1 - x, x)).start()
        return carry

    lax.fori_loop(0, group, body, 0)
    return lambda s: load(s).wait()


def pick_rows(gates):
    tokens = gates.shape[1]
    down = lax.broadcasted_iota(jnp.int32, (tokens, tokens), 0)
    along = lax.broadcasted_iota(jnp.int32, (tokens, tokens), 1)
    upper = jnp.where(down <= along, 1.0, 0.0).astype(BRAIN)
    live = jnp.where(gates != 0.0, 1.0, 0.0)
    place = jnp.dot(
        jnp.broadcast_to(live, (8, tokens)).astype(BRAIN), upper, preferred_element_type=FLOAT
    )[0:1] - 1.0
    ranks = lax.broadcasted_iota(jnp.int32, (PICKED, tokens), 0).astype(FLOAT)
    return (ranks == place) & (live > 0.0)


def wide_flow(ins, outs, stages, sems, group):
    own_sems, send_sems, recv_sems = sems
    y, c = places(group)[:2]
    sibling, opposite = {"dp": 2 * y + 1 - c}, {"dp": 2 * (1 - y) + c}
    own, other = 2 * y + c, 2 * (1 - y) + c
    count = len(ins)

    def block(i, q):
        rows = ins[i].shape[0]
        return outs[i].at[pl.ds(pl.multiple_of(q * rows, rows), rows)]

    def copy(i, kind):
        src = block(i, other) if kind == 2 else ins[i]
        dst = block(i, other if kind == 2 else own)
        return remote(src, dst, send_sems.at[i, kind], recv_sems.at[i, kind], opposite if kind == 1 else sibling)

    def load(i):
        return pltpu.make_async_copy(ins[i], stages[i], own_sems.at[i])

    def keep(i):
        return pltpu.make_async_copy(stages[i], block(i, own), own_sems.at[i])

    def begin():
        for i in range(count):
            copy(i, 1).start()
            copy(i, 0).start()
            load(i).start()

    def store():
        for i in range(count):
            load(i).wait()
            keep(i).start()

    def forward(i):
        copy(i, 1).wait_recv()
        copy(i, 2).start()

    def finish():
        for i in range(count):
            copy(i, 0).wait()
            copy(i, 1).wait_send()
            copy(i, 2).wait()
            keep(i).wait()

    return begin, store, forward, finish


def expert_forward_kernel(group, wide, x_hbm, g_ref, in_ref, out_ref, sin_ref, sout_ref, *refs):
    wide_ins, (y_ref, xe_ref, gu_ref, sgu_ref), refs = refs[:wide], refs[wide : wide + 4], refs[wide + 4 :]
    wide_outs, stages, refs = refs[:wide], refs[wide : 2 * wide], refs[2 * wide :]
    rows_ref, held, sent, crossed, below, above, *sems = refs
    y, c, z, x = places(group)
    wait_load = load_blocks(group, x_hbm, rows_ref, sems[6])
    peers = line_peers(z, x, group // 2)
    if wide:
        peers += [(None, {"dp": 2 * y + 1 - c}), (None, {"dp": 2 * (1 - y) + c})]
    greet(peers)
    if wide:
        begin, store, forward, finish = wide_flow(wide_ins, wide_outs, stages, sems[7:], group)
        begin()
    start_cross, chain, last, settle = fold(group, held, sent, crossed, below, above, y_ref, sems[:6])

    def compute(s):
        wait_load(s)
        rows = rows_ref[s]
        shared_gu = jnp.dot(rows, sin_ref[...], preferred_element_type=FLOAT)
        half = shared_gu.shape[1] // 2
        shared_mid = (silu_of(shared_gu[:, :half]) * shared_gu[:, half:]).astype(BRAIN)
        sgu_ref[s] = shared_gu.astype(sgu_ref.dtype)
        total = matmul_nt(shared_mid, sout_ref[...])
        for e in range(in_ref.shape[0]):
            gates = g_ref[s, e : e + 1, :]
            hit = pick_rows(gates)
            picked = jnp.dot(
                jnp.where(hit, 1.0, 0.0).astype(BRAIN), rows, preferred_element_type=FLOAT
            ).astype(BRAIN)
            gate_up = jnp.dot(picked, in_ref[e], preferred_element_type=FLOAT)
            width = gate_up.shape[1] // 2
            inner = (silu_of(gate_up[:, :width]) * gate_up[:, width:]).astype(BRAIN)
            result = matmul_nt(inner, out_ref[e]).astype(BRAIN)
            total = total + matmul_tn(jnp.where(hit, gates, 0.0).astype(BRAIN), result)
            xe_ref[e, s] = picked
            gu_ref[e, s] = gate_up.astype(gu_ref.dtype)
        return total

    def between(turn, turns):
        if wide and turn == 0:
            store()
        if wide and turn == turns - 1:
            for i in range(wide - 1):
                forward(i)

    run_blocks(group, compute, held, sent, start_cross, chain, last, between)
    if wide:
        forward(wide - 1)
        finish()
    settle()


def expert_forward(rows, gates, expert_in, expert_out, shared_in, shared_out, wide, number):
    group, tokens, width = rows.shape
    local = expert_in.shape[0]
    inner = expert_in.shape[2]
    vmem = pl.BlockSpec(memory_space=pltpu.VMEM)
    any_spec = pl.BlockSpec(memory_space=pl.ANY)
    dma = pltpu.SemaphoreType.DMA
    return pl.pallas_call(
        functools.partial(expert_forward_kernel, group, len(wide)),
        out_shape=[
            jax.ShapeDtypeStruct((tokens, width), FLOAT),
            jax.ShapeDtypeStruct((local, group, PICKED, width), BRAIN),
            jax.ShapeDtypeStruct((local, group, PICKED, inner), BRAIN),
            jax.ShapeDtypeStruct((group, tokens, shared_in.shape[1]), BRAIN),
        ]
        + [jax.ShapeDtypeStruct((4 * a.shape[0], a.shape[1]), a.dtype) for a in wide],
        in_specs=[any_spec] + [vmem] * 5 + [any_spec] * len(wide),
        out_specs=[vmem] * 4 + [any_spec] * len(wide),
        scratch_shapes=[pltpu.VMEM(a.shape, a.dtype) for a in wide]
        + [pltpu.VMEM(rows.shape, BRAIN)]
        + fold_scratch(group, tokens, width)
        + [dma((group,))]
        + ([dma((len(wide),)), dma((len(wide), 3)), dma((len(wide), 3))] if wide else []),
        compiler_params=pltpu.CompilerParams(collective_id=number, has_side_effects=True, vmem_limit_bytes=60 * MIB),
        name="expert_forward",
    )(rows, gates, expert_in, expert_out, shared_in, shared_out, *wide)


def swiglu_back(gate, up, grad):
    sig = jax.nn.sigmoid(gate)
    act = gate * sig
    return grad * up * (sig + act * (1.0 - sig)), grad * act, act * up


TILE = 256


def expert_backward_kernel(
    group, d_hbm, xe_hbm, gu_hbm, g_ref, sgu_ref, in_ref, out_ref, sin_ref, sout_ref,
    dx_ref, dg_ref, win_hbm, wout_hbm, dsgu_ref, smid_ref,
    rows_ref, xe_ref, gu_ref, dres_ref, mid_ref, win_stage, wout_stage, dgates, held, sent, crossed, below, above, *sems,
):
    z, x = places(group)[2:]
    me = 2 * z + x
    gate_send, gate_recv, fetch_sems, stage_sems = sems[7:11]
    wait_load = load_blocks(group, d_hbm, rows_ref, sems[6])
    fetch_gu = pltpu.make_async_copy(gu_hbm, gu_ref, fetch_sems.at[0])
    fetch_xe = pltpu.make_async_copy(xe_hbm, xe_ref, fetch_sems.at[1])
    fetch_gu.start()
    fetch_xe.start()
    greet([(None, {"expert": lax.rem(me + k, group)}) for k in range(1, group)])
    start_cross, chain, last, settle = fold(group, held, sent, crossed, below, above, dx_ref, sems[:6])
    fetch_gu.wait()

    def give(s):
        return remote(dgates.at[s], dg_ref.at[me], gate_send.at[s], gate_recv.at[me], {"expert": s})

    def compute(s):
        wait_load(s)
        grads = rows_ref[s]
        shared_gu = sgu_ref[s].astype(FLOAT)
        half = shared_gu.shape[1] // 2
        dmid = jnp.dot(grads, sout_ref[...], preferred_element_type=FLOAT)
        dgate, dup, shared_mid = swiglu_back(shared_gu[:, :half], shared_gu[:, half:], dmid)
        shared_d = jnp.concatenate([dgate, dup], axis=1).astype(BRAIN)
        dsgu_ref[s] = shared_d
        smid_ref[s] = shared_mid.astype(BRAIN)
        total = matmul_nt(shared_d, sin_ref[...])
        for e in range(in_ref.shape[0]):
            gates = g_ref[s, e : e + 1, :]
            hit = pick_rows(gates)
            chosen = jnp.where(hit, 1.0, 0.0).astype(BRAIN)
            weight = jnp.sum(jnp.where(hit, gates, 0.0), axis=1, keepdims=True)
            picked = jnp.dot(chosen, grads, preferred_element_type=FLOAT)
            dres_ref[e, s] = (picked * weight).astype(BRAIN)
            raw = jnp.dot(picked.astype(BRAIN), out_ref[e], preferred_element_type=FLOAT)
            gate_up = gu_ref[e, s].astype(FLOAT)
            width = gate_up.shape[1] // 2
            dgate, dup, inner = swiglu_back(gate_up[:, :width], gate_up[:, width:], raw * weight)
            inner_low = inner.astype(BRAIN)
            mid_ref[e, s] = inner_low
            dweight = jnp.sum(raw * inner_low.astype(FLOAT), axis=1, keepdims=True)
            dgates[s, e : e + 1, :] = jnp.sum(jnp.where(hit, dweight, 0.0), axis=0, keepdims=True)
            dgu = jnp.concatenate([dgate, dup], axis=1).astype(BRAIN)
            gu_ref[e, s] = dgu
            back = matmul_nt(dgu, in_ref[e]).astype(BRAIN)
            total = total + matmul_tn(chosen, back)
        pl.when(s != me)(lambda: give(s).start())
        return total

    local, depth, inner = in_ref.shape
    tiles = depth // TILE

    def stores(n):
        e, t, slot = n // tiles, lax.rem(n, tiles), lax.rem(n, 2)
        at = pl.ds(pl.multiple_of(t * TILE, TILE), TILE)
        return (
            pltpu.make_async_copy(win_stage.at[slot], win_hbm.at[e, at], stage_sems.at[0, slot]),
            pltpu.make_async_copy(wout_stage.at[slot], wout_hbm.at[e, at], stage_sems.at[1, slot]),
        )

    def weight_tile(n, carry):
        e, t, slot = n // tiles, lax.rem(n, tiles), lax.rem(n, 2)
        at = pl.ds(pl.multiple_of(t * TILE, TILE), TILE)

        @pl.when(n >= 2)
        def _():
            for store in stores(n - 2):
                store.wait()

        flat = lambda array: array.reshape(-1, array.shape[-1])
        win_stage[slot] = matmul_tn(flat(xe_ref[e, :, :, at]), flat(gu_ref[e])).astype(BRAIN)
        wout_stage[slot] = matmul_tn(flat(dres_ref[e, :, :, at]), flat(mid_ref[e])).astype(BRAIN)
        for store in stores(n):
            store.start()
        return carry

    def between(turn, turns):
        if turn == 0:
            fetch_xe.wait()
        count = local * tiles
        lax.fori_loop(count * turn // turns, count * (turn + 1) // turns, weight_tile, 0)

    run_blocks(group, compute, held, sent, start_cross, chain, last, between)
    for n in (local * tiles - 2, local * tiles - 1):
        for store in stores(n):
            store.wait()
    dg_ref[me] = dgates[me]
    for k in range(1, group):
        source = lax.rem(me + k, group)
        remote(dgates.at[source], dg_ref.at[source], gate_send.at[source], gate_recv.at[source], {"expert": source}).wait_recv()
        give(source).wait_send()
    settle()


def expert_backward(grads, picked, gates, gate_up, shared_gu, expert_in, expert_out, shared_in, shared_out, number):
    group, tokens, width = grads.shape
    local = expert_in.shape[0]
    inner = expert_in.shape[2]
    vmem = pl.BlockSpec(memory_space=pltpu.VMEM)
    any_spec = pl.BlockSpec(memory_space=pl.ANY)
    dma = pltpu.SemaphoreType.DMA
    return pl.pallas_call(
        functools.partial(expert_backward_kernel, group),
        out_shape=[
            jax.ShapeDtypeStruct((tokens, width), FLOAT),
            jax.ShapeDtypeStruct((group, local, tokens), FLOAT),
            jax.ShapeDtypeStruct((local, width, inner), BRAIN),
            jax.ShapeDtypeStruct((local, width, inner // 2), BRAIN),
            jax.ShapeDtypeStruct(shared_gu.shape, BRAIN),
            jax.ShapeDtypeStruct(shared_gu.shape[:2] + (shared_gu.shape[2] // 2,), BRAIN),
        ],
        in_specs=[any_spec] * 3 + [vmem] * 6,
        out_specs=[vmem] * 2 + [any_spec] * 2 + [vmem] * 2,
        scratch_shapes=[
            pltpu.VMEM(grads.shape, BRAIN),
            pltpu.VMEM(picked.shape, BRAIN),
            pltpu.VMEM(gate_up.shape, BRAIN),
            pltpu.VMEM((local, group, PICKED, width), BRAIN),
            pltpu.VMEM((local, group, PICKED, inner // 2), BRAIN),
            pltpu.VMEM((2, TILE, inner), BRAIN),
            pltpu.VMEM((2, TILE, inner // 2), BRAIN),
            pltpu.VMEM((group, local, tokens), FLOAT),
        ]
        + fold_scratch(group, tokens, width)
        + [dma((group,))] * 3
        + [dma((2,)), dma((2, 2))],
        compiler_params=pltpu.CompilerParams(collective_id=number, has_side_effects=True, vmem_limit_bytes=63 * MIB),
        name="expert_backward",
    )(grads, picked, gate_up, gates, shared_gu, expert_in, expert_out, shared_in, shared_out)


def moe_forward(hidden, routes, valid, norm_gain, router, pieces, wide, number):
    group = lax.axis_size("expert")
    local = pieces[0].shape[0]
    normed, norm_back = jax.vjp(rms_norm, hidden, norm_gain)
    normed_low = normed.astype(BRAIN)
    logits = matmul(normed_low, router)
    chosen = jnp.any(routes[:, :, None] == jnp.arange(router.shape[1])[None, None, :], axis=1)
    largest = jnp.max(jnp.where(chosen, logits, -jnp.inf), axis=1, keepdims=True)
    raised = jnp.where(chosen, jnp.exp(jnp.where(chosen, logits - largest, 0.0)), 0.0)
    probs = raised / jnp.sum(raised, axis=1, keepdims=True)
    gates = probs * valid[:, None]
    if lax.axis_size("dp") == 4:
        rows_all, gates_all, expert_in, expert_out, shared = spread([normed_low, gates.T], pieces, [], group, 1)
    else:
        rows_all, gates_all = spread([normed_low, gates.T], [], [], group, 1)
        expert_in, expert_out, shared = [lax.all_gather(p, "dp", axis=1, tiled=True) for p in pieces]
    part = shared.shape[2] // 3
    weights = (router, shared[0, :, : 2 * part], shared[0, :, 2 * part :], expert_in, expert_out)
    own_gates = lax.dynamic_slice_in_dim(gates_all, lax.axis_index("expert") * local, local, axis=1)
    four = lax.axis_size("dp") == 4
    routed, picked, gate_up, shared_gu, *gathered = expert_forward(
        rows_all, own_gates, expert_in, expert_out, *weights[1:3], wide if four else [], number
    )
    if not four:
        gathered = [lax.all_gather(array, "dp", axis=0, tiled=True) for array in wide]
    return hidden + routed, gathered, (norm_back, normed_low, probs, rows_all, own_gates, picked, gate_up, shared_gu, weights)


def moe_backward(grad_out, saved, valid, grads_all, earlier):
    norm_back, normed_low, probs, rows_all, own_gates, picked, gate_up, shared_gu, weights = saved
    router, shared_in, shared_out, expert_in, expert_out = weights
    group = lax.axis_size("expert")
    if grads_all is None:
        if lax.axis_size("dp") == 4:
            grads_all, *earlier = spread([grad_out.astype(BRAIN)], [], earlier, group, 3)
        else:
            grads_all = spread([grad_out.astype(BRAIN)], [], [], group, 3)[0]
            earlier = [scatter_expert(s) for s in earlier]
    grad_normed, grad_gates, grad_in, grad_out_weight, dshared, shared_mid = expert_backward(
        grads_all, picked, own_gates, gate_up, shared_gu, expert_in, expert_out, shared_in, shared_out, 4
    )
    flat = lambda array: array.reshape(-1, array.shape[-1])
    shared_grads = [matmul_tn(flat(rows_all), flat(dshared)), matmul_tn(flat(grads_all), flat(shared_mid))]
    sums = [
        jnp.concatenate(shared_grads, axis=1).astype(BRAIN)[None],
        grad_in,
        grad_out_weight,
    ]
    grad_probs = grad_gates.reshape(-1, grad_gates.shape[2]).T * valid[:, None]
    grad_logits = probs * (grad_probs - jnp.sum(probs * grad_probs, axis=1, keepdims=True))
    logits_low = grad_logits.astype(BRAIN)
    grad_router = matmul_tn(normed_low, logits_low).astype(BRAIN)
    grad_hidden, grad_gain = norm_back(grad_normed + matmul_nt(logits_low, router))
    return grad_out + grad_hidden, grad_gain, grad_router, sums, earlier


def attend_scores(query, key_rows):
    length = query.shape[0]
    down = lax.broadcasted_iota(jnp.int32, (length, length), 0)
    along = lax.broadcasted_iota(jnp.int32, (length, length), 1)
    scores = jnp.where(down >= along, matmul_nt(query, key_rows) * AHDIM ** (-0.5), -1e30)
    raised = jnp.exp(scores - jnp.max(scores, axis=1, keepdims=True))
    return raised / jnp.sum(raised, axis=1, keepdims=True)


def attention_forward_kernel(q_ref, k_ref, v_ref, o_ref):
    for j in range(AHEADS // KVHEADS):
        part = slice(j * AHDIM, (j + 1) * AHDIM)
        probs = attend_scores(q_ref[:, part], k_ref[...])
        o_ref[:, part] = matmul(probs.astype(BRAIN), v_ref[...]).astype(BRAIN)


def attention_specs(length):
    queries = pl.BlockSpec((length, QD // KVHEADS), lambda h: (0, h))
    keys = pl.BlockSpec((length, AHDIM), lambda h: (0, QD // AHDIM + h))
    values = pl.BlockSpec((length, AHDIM), lambda h: (0, (QD + KVD) // AHDIM + h))
    return [queries, keys, values]


def attention_core(qkv):
    length = qkv.shape[0]
    specs = attention_specs(length)
    return pl.pallas_call(
        attention_forward_kernel,
        grid=(KVHEADS,),
        out_shape=jax.ShapeDtypeStruct((length, QD), BRAIN),
        in_specs=specs,
        out_specs=specs[0],
        compiler_params=pltpu.CompilerParams(vmem_limit_bytes=32 * MIB),
        name="attention_forward",
    )(qkv, qkv, qkv)


def attention_backward_kernel(q_ref, k_ref, v_ref, d_ref, dq_ref, dk_ref, dv_ref):
    keys = k_ref[...]
    values = v_ref[...]
    dkeys = jnp.zeros(keys.shape, FLOAT)
    dvalues = jnp.zeros(keys.shape, FLOAT)
    for j in range(AHEADS // KVHEADS):
        part = slice(j * AHDIM, (j + 1) * AHDIM)
        query = q_ref[:, part]
        grads = d_ref[:, part]
        probs = attend_scores(query, keys)
        dprobs = matmul_nt(grads, values)
        dvalues = dvalues + matmul_tn(probs.astype(BRAIN), grads)
        inner = jnp.sum(probs * dprobs, axis=1, keepdims=True)
        draw = (probs * (dprobs - inner) * AHDIM ** (-0.5)).astype(BRAIN)
        dq_ref[:, part] = matmul(draw, keys).astype(BRAIN)
        dkeys = dkeys + matmul_tn(draw, query)
    dk_ref[...] = dkeys.astype(BRAIN)
    dv_ref[...] = dvalues.astype(BRAIN)


def attention_core_back(qkv, grads):
    length = qkv.shape[0]
    specs = attention_specs(length)
    head_block = pl.BlockSpec((length, AHDIM), lambda h: (0, h))
    return pl.pallas_call(
        attention_backward_kernel,
        grid=(KVHEADS,),
        out_shape=[
            jax.ShapeDtypeStruct((length, QD), BRAIN),
            jax.ShapeDtypeStruct((length, KVD), BRAIN),
            jax.ShapeDtypeStruct((length, KVD), BRAIN),
        ],
        in_specs=specs + [specs[0]],
        out_specs=[specs[0], head_block, head_block],
        compiler_params=pltpu.CompilerParams(vmem_limit_bytes=32 * MIB),
        name="attention_backward",
    )(qkv, qkv, qkv, grads)


def attention_forward(hidden, norm_gain, attn_qkv, attn_out):
    normed, norm_back = jax.vjp(rms_norm, hidden, norm_gain)
    normed_low = normed.astype(BRAIN)
    qkv = matmul(normed_low, attn_qkv).astype(BRAIN)
    attended = attention_core(qkv)
    output = hidden + matmul_nt(attended, attn_out)
    return output, (norm_back, normed_low, qkv, attended)


def attention_backward(grad_out, saved, attn_qkv, attn_out):
    norm_back, normed_low, qkv, attended = saved
    grad_low = grad_out.astype(BRAIN)
    grad_attn_out = matmul_tn(grad_low, attended).astype(BRAIN)
    grad_attended = matmul(grad_low, attn_out).astype(BRAIN)
    grad_qkv = jnp.concatenate(attention_core_back(qkv, grad_attended), axis=1)
    grad_attn_qkv = matmul_tn(normed_low, grad_qkv).astype(BRAIN)
    grad_hidden, grad_gain = norm_back(matmul_nt(grad_qkv, attn_qkv))
    return grad_out + grad_hidden, grad_gain, grad_attn_qkv, grad_attn_out


def gather_dense(array):
    return lax.all_gather(array, BOTH, axis=0, tiled=True)


def scatter_dense(array):
    return lax.psum_scatter(array, BOTH, scatter_dimension=0, tiled=True).astype(FLOAT)


def scatter_expert(array):
    return lax.psum_scatter(array, "dp", scatter_dimension=1, tiled=True).astype(FLOAT)


def shared_columns(shared):
    group = lax.axis_size("expert")
    rows = shared[0].shape[0]
    pieces = []
    for shared_in, shared_out in zip(shared[0::2], shared[1::2]):
        half = shared_in.shape[1] // 2
        pieces += [shared_in[:, :half], shared_in[:, half:], shared_out]
    cut = [piece.reshape(rows, group, -1) for piece in pieces]
    return jnp.transpose(jnp.concatenate(cut, axis=2), (1, 0, 2))


def shared_whole(own):
    part = own.shape[2] // 6

    def columns(index):
        piece = jnp.transpose(own[:, :, index * part : (index + 1) * part], (1, 0, 2))
        return piece.reshape(piece.shape[0], -1)

    return [
        jnp.concatenate([columns(0), columns(1)], axis=1),
        columns(2),
        jnp.concatenate([columns(3), columns(4)], axis=1),
        columns(5),
    ]


def exchange(blocks):
    return lax.all_to_all(blocks, "expert", split_axis=0, concat_axis=0, tiled=True)


def first_gather(dense, shared, rows):
    if lax.axis_size("dp") == 4:
        *dense, shared, rows = head_exchange(dense, shared, rows, 5)
        return [array.reshape(-1, array.shape[2]) for array in dense], shared, rows
    rows = spread([rows], [], [], lax.axis_size("expert"), 3)[0]
    return [gather_dense(array) for array in dense], exchange(shared), rows


def last_sums(left, right, routers, small, sums_a, shared_b):
    group = lax.axis_size("expert")
    cut = lambda array: array.reshape(group, -1, array.shape[-1])
    shared_b = cut(shared_b.astype(BRAIN))
    if lax.axis_size("dp") == 4:
        routers = routers.reshape(4 * group, -1, routers.shape[1])
        return tail_exchange(left.T, right, routers, shared_b, small, sums_a, 6)
    mix = matmul_tn(left, right).astype(BRAIN)
    shared_a, *sums_a = [scatter_expert(s) for s in sums_a]
    shared_a = exchange(cut(shared_a.astype(BRAIN)))
    return scatter_dense(mix), scatter_dense(routers), exchange(shared_b), lax.psum(small, BOTH), shared_a, *sums_a


def per_device(
    layer_input, cotangent, lengths, routes_a, routes_b,
    mixer_in, mixer_out, router_a, shared_in_a, shared_out_a, expert_in_a, expert_out_a,
    attn_qkv, attn_out, router_b, shared_in_b, shared_out_b, expert_in_b, expert_out_b,
    norm_gains, mixer_gain, conv_weight, conv_bias, decay_log, step_bias, skip_gain,
):
    small = {
        "conv_weight": conv_weight,
        "conv_bias": conv_bias,
        "decay_log": decay_log,
        "step_bias": step_bias,
        "skip_gain": skip_gain,
        "mixer_gain": mixer_gain,
    }
    assert lengths.shape[0] == 1 and layer_input.shape[0] == SLOT_LEN
    group = lax.axis_size("expert")
    experts = router_a.shape[1]
    valid = (jnp.arange(SLOT_LEN) < lengths[0]).astype(FLOAT)
    grad = cotangent * valid[:, None]
    (w_mixer_in, w_mixer_out, w_routers), w_shared, last_rows = first_gather(
        [mixer_in, mixer_out, jnp.concatenate([router_a, router_b], axis=1)],
        shared_columns([shared_in_a, shared_out_a, shared_in_b, shared_out_b]),
        grad.astype(BRAIN),
    )
    w_shared = w_shared.reshape(1, -1, w_shared.shape[2])
    half = w_shared.shape[2] // 2
    attn_both, w_routers = lax.optimization_barrier((jnp.concatenate([attn_qkv, attn_out], axis=1), w_routers))
    attn_part = lax.all_gather(attn_both, "expert", axis=0, tiled=True)
    hidden = layer_input.astype(FLOAT)
    hidden, saved_mix = mixer_forward(hidden, norm_gains[0], w_mixer_in, w_mixer_out, small)
    hidden, (w_qkv, w_attn_out), saved_a = moe_forward(
        hidden,
        routes_a,
        valid,
        norm_gains[1],
        w_routers[:, :experts],
        [expert_in_a, expert_out_a, w_shared[:, :, :half]],
        [attn_part[:, :QKV], attn_part[:, QKV:]],
        2,
    )
    hidden, saved_attn = attention_forward(hidden, norm_gains[2], w_qkv, w_attn_out)
    layer_output, _, saved_b = moe_forward(
        hidden,
        routes_b,
        valid,
        norm_gains[3],
        w_routers[:, experts:],
        [expert_in_b, expert_out_b, w_shared[:, :, half:]],
        [],
        7,
    )
    grad, gain_four, d_router_b, sums_b, _ = moe_backward(grad, saved_b, valid, last_rows, [])
    grad, gain_three, d_qkv, d_attn_out = attention_backward(grad, saved_attn, w_qkv, w_attn_out)
    grad, d_qkv, d_attn_out = lax.optimization_barrier((grad, d_qkv, d_attn_out))
    d_qkv, d_attn_out = scatter_dense(d_qkv), scatter_dense(d_attn_out)
    grad, gain_two, d_router_a, sums_a, sums_b = moe_backward(grad, saved_a, valid, None, sums_b)
    d_shared_b, d_in_b, d_out_b = sums_b
    grad, gain_one, mix_left, mix_right, d_mixer_out, grad_small = mixer_backward(
        grad, saved_mix, w_mixer_in, w_mixer_out, small
    )
    d_mixer_out = scatter_dense(d_mixer_out)
    parts = [jnp.stack([gain_one, gain_two, gain_three, gain_four])] + list(grad_small)
    flat = jnp.concatenate([part.reshape(-1) for part in parts])
    padded = jnp.pad(flat, (0, -flat.shape[0] % 1024)).reshape(-1, 128)
    d_mixer_in, d_routers, d_shared_b, summed, d_shared_a, d_in_a, d_out_a = last_sums(
        mix_left, mix_right, jnp.concatenate([d_router_a, d_router_b], axis=1), padded, sums_a, d_shared_b
    )
    d_in_a, d_out_a = d_in_a.astype(FLOAT), d_out_a.astype(FLOAT)
    d_shared = shared_whole(jnp.concatenate([d_shared_a, d_shared_b], axis=2).astype(FLOAT))
    summed = summed.reshape(-1)
    sums = []
    place = 0
    for part in parts:
        sums.append(summed[place : place + part.size].reshape(part.shape))
        place += part.size
    return (
        layer_output, grad,
        d_mixer_in, d_mixer_out, d_routers[:, :experts], d_shared[0], d_shared[1], d_in_a, d_out_a,
        d_qkv, d_attn_out, d_routers[:, experts:], d_shared[2], d_shared[3], d_in_b, d_out_b,
        *sums,
    )


def solution(mesh):
    rows = P(BOTH, None)
    expert = P("expert", "dp", None)
    first = (rows, rows, rows, rows, rows, expert, expert)
    second = (rows, rows, rows, rows, rows, expert, expert)
    return jax.shard_map(
        per_device,
        mesh=mesh,
        in_specs=(rows, rows, P(BOTH), rows, rows) + first + second + (P(),) * 7,
        out_specs=(rows, rows) + first + second + (P(),) * 7,
        check_vma=False,
    )
```

```python
import functools

import jax
import jax.numpy as jnp
from jax import lax
from jax.experimental import pallas as pl
from jax.experimental.pallas import tpu as pltpu
from jax.sharding import PartitionSpec as P

MHEADS = 48
MHDIM = 64
NSTATE = 128
KCONV = 4
AHEADS = 12
KVHEADS = 4
AHDIM = 128
SLOT_LEN = 256
HALF = 128
CAP = 60
DI = 3072
CONVCH = 3328
QD = 1536
KVD = 512
QKV = 2560

EPS = 1e-05
HIGH = lax.Precision.HIGHEST
FLOAT = jnp.float32
BRAIN = jnp.bfloat16
MESH = pl.DeviceIdType.MESH
BOTH = ("dp", "expert")
PICKED = SLOT_LEN // HALF * 64
MIB = 2**20


def matmul(left, right):
    return jnp.dot(left, right, preferred_element_type=FLOAT)


def matmul_nt(left, right):
    return lax.dot_general(left, right, (((1,), (1,)), ((), ())), preferred_element_type=FLOAT)


def matmul_tn(left, right):
    return lax.dot_general(left, right, (((0,), (0,)), ((), ())), preferred_element_type=FLOAT)


def silu_of(values):
    return values * jax.nn.sigmoid(values)


def softplus_of(values):
    return jnp.log1p(jnp.exp(values))


def rms_norm(values, norm_gain):
    return values * lax.rsqrt(jnp.mean(values * values, axis=-1, keepdims=True) + EPS) * norm_gain


def whole_spec(shape):
    return pl.BlockSpec(shape, lambda *at: (0,) * len(shape), pipeline_mode=pl.Buffered(1))


def places(group):
    q = lax.axis_index("dp")
    e = lax.axis_index("expert")
    return q // 2, lax.rem(q, 2), e // 2, lax.rem(e, 2)


def greet(peers):
    barrier = pltpu.get_barrier_semaphore()
    count = 0
    for condition, device in peers:

        def hello():
            pl.semaphore_signal(barrier, inc=1, device_id=device, device_id_type=MESH)

        if condition is None:
            hello()
            count = count + 1
        else:
            pl.when(condition)(hello)
            count = count + jnp.where(condition, 1, 0)
    pl.semaphore_wait(barrier, count)


def line_peers(z, x, line):
    return [
        (None, {"expert": 2 * z + 1 - x}),
        (z > 0, {"expert": 2 * (z - 1) + x}),
        (z < line - 1, {"expert": 2 * (z + 1) + x}),
    ]


def remote(src, dst, send_sem, recv_sem, device):
    return pltpu.make_async_remote_copy(
        src_ref=src, dst_ref=dst, send_sem=send_sem, recv_sem=recv_sem, device_id=device, device_id_type=MESH
    )


def spread_kernel(count, wide, sums, group, *refs):
    total = count + wide
    every = total + sums
    ins, outs = refs[:every], refs[every : 2 * every]
    stages = refs[2 * every : 2 * every + wide]
    sum_bufs = refs[2 * every + wide : 2 * every + wide + 3 * sums]
    sems = refs[2 * every + wide + 3 * sums :]
    sum_sems = sems[-5:]
    up_sems, down_sems, cross_sems, recv_sems, own_sems = sems[:5]
    line = group // 2
    y, c, z, x = places(group)
    sibling, opposite = {"dp": 2 * y + 1 - c}, {"dp": 2 * (1 - y) + c}
    greet(line_peers(z, x, line) + ([(None, sibling), (None, opposite)] if wide or sums else []))

    def copy(i, src, place, sem, device):
        return remote(src, outs[i].at[place], sem, recv_sems.at[i, place], {"expert": device})

    def moves(i, s, rising):
        zz = z - s if rising else z + s
        place = 2 * zz + x
        src = ins[i] if s == 0 else outs[i].at[place]
        up = functools.partial(copy, i, src, place, up_sems.at[i, s], 2 * (z + 1) + x)
        down = functools.partial(copy, i, src, place, down_sems.at[i, s], 2 * (z - 1) + x)
        cross = functools.partial(copy, i, src, place, cross_sems.at[i, zz], 2 * z + 1 - x)
        return up, down, cross

    def steps(act):
        for s in range(line):
            for rising in (True, False) if s else (True,):
                valid = (z - s >= 0) if rising else (z + s < line)

                @pl.when(valid)
                def _():
                    for i in range(count):
                        act(i, s, rising, *moves(i, s, rising))

    def block(i, q):
        rows = ins[i].shape[1]
        return outs[i].at[:, pl.ds(pl.multiple_of(q * rows, rows), rows), :]

    def wide_copy(i, kind):
        wide_send, wide_recv = sems[5:7]
        own, other = 2 * y + c, 2 * (1 - y) + c
        k = i - count
        if kind == 0:
            return remote(ins[i], block(i, own), wide_send.at[k, 0], wide_recv.at[k, 0], sibling)
        if kind == 1:
            return remote(ins[i], block(i, own), wide_send.at[k, 1], wide_recv.at[k, 1], opposite)
        return remote(block(i, other), block(i, other), wide_send.at[k, 2], wide_recv.at[k, 2], sibling)

    def own_copy(i):
        if i < count:
            return pltpu.make_async_copy(ins[i], outs[i].at[2 * z + x], own_sems.at[i])
        return pltpu.make_async_copy(ins[i], stages[i - count], own_sems.at[i])

    def own_store(i):
        return pltpu.make_async_copy(stages[i - count], block(i, 2 * y + c), own_sems.at[i])

    def forward(i, s, rising, up, down, cross):
        if s:
            cross().wait_recv()
        if rising:
            pl.when(z < line - 1)(lambda: up().start())
        if not rising or s == 0:
            pl.when(z > 0)(lambda: down().start())
        cross().start()

    def settle(i, s, rising, up, down, cross):
        if rising:
            pl.when(z < line - 1)(lambda: up().wait_send())
        if not rising or s == 0:
            pl.when(z > 0)(lambda: down().wait_send())
        cross().wait_send()

    def sum_parts(k):
        kept, landed, arrived = sum_bufs[3 * k : 3 * k + 3]
        own, core_send, core_recv, side_send, side_recv = sum_sems
        source = ins[total + k]
        rows = source.shape[1] // 4

        def piece(q):
            return source.at[:, pl.ds(pl.multiple_of(q * rows, rows), rows), :]

        def load(h):
            return pltpu.make_async_copy(piece(2 * h + c), kept.at[h], own.at[k, h])

        def to_sibling(h):
            return remote(piece(2 * h + 1 - c), landed.at[h], core_send.at[k, h], core_recv.at[k, h], sibling)

        def to_opposite():
            return remote(kept.at[1 - y], arrived, side_send.at[k], side_recv.at[k], opposite)

        def add(target, lead, sources):
            for e in range(source.shape[0]):
                add_blocks((target, lead + (e,), None), [(ref, at + (e,), None) for ref, at in sources], rows)

        return kept, landed, arrived, load, to_sibling, to_opposite, add

    for k in range(sums):
        load, to_sibling = sum_parts(k)[3:5]
        for h in (1 - y, y):
            to_sibling(h).start()
            load(h).start()
    for i in range(count, total):
        wide_copy(i, 1).start()
        wide_copy(i, 0).start()
    for i in range(total):
        own_copy(i).start()
    for i in range(count, total):
        own_copy(i).wait()
        own_store(i).start()
    if sums:
        steps(lambda *move: forward(*move) if move[1] == 0 else None)
        for k in range(sums):
            kept, landed, arrived, load, to_sibling, to_opposite, add = sum_parts(k)
            load(1 - y).wait()
            to_sibling(1 - y).wait_recv()
            add(kept, (1 - y,), [(kept, (1 - y,)), (landed, (1 - y,))])
            to_opposite().start()
        steps(lambda *move: forward(*move) if move[1] else None)
    else:
        steps(forward)
    for i in range(count, total):
        wide_copy(i, 1).wait_recv()
        wide_copy(i, 2).start()
    for i in range(count):
        for zz in range(line):
            place = 2 * zz + 1 - x
            copy(i, ins[i], place, own_sems.at[i], 2 * z + 1 - x).wait_recv()
    steps(settle)
    for i in range(count, total):
        wide_copy(i, 0).wait()
        wide_copy(i, 1).wait_send()
        wide_copy(i, 2).wait()
    for i in range(count):
        own_copy(i).wait()
    for i in range(count, total):
        own_store(i).wait()
    for k in range(sums):
        kept, landed, arrived, load, to_sibling, to_opposite, add = sum_parts(k)
        load(y).wait()
        to_sibling(y).wait_recv()
        to_opposite().wait_recv()
        add(outs[total + k], (), [(kept, (y,)), (landed, (y,)), (arrived, ())])
        for h in range(2):
            to_sibling(h).wait_send()
        to_opposite().wait_send()


def spread(arrays, wide, sums, group, number):
    n, w, s, line = len(arrays), len(wide), len(sums), group // 2
    split = lax.axis_size("dp")
    dma = pltpu.SemaphoreType.DMA
    any_spec = pl.BlockSpec(memory_space=pl.ANY)
    vmem = pl.BlockSpec(memory_space=pltpu.VMEM)
    shapes = [jax.ShapeDtypeStruct((group,) + a.shape, a.dtype) for a in arrays]
    shapes += [jax.ShapeDtypeStruct((a.shape[0], split * a.shape[1], a.shape[2]), a.dtype) for a in wide]
    scratch = [pltpu.VMEM(a.shape, a.dtype) for a in wide]
    for a in sums:
        part = (a.shape[0], a.shape[1] // 4, a.shape[2])
        scratch += [pltpu.VMEM((2,) + part, a.dtype)] * 2 + [pltpu.VMEM(part, a.dtype)]
        shapes.append(jax.ShapeDtypeStruct(part, FLOAT))
    scratch += [dma((n, line)), dma((n, line)), dma((n, line)), dma((n, group)), dma((n + w,))]
    if w:
        scratch += [dma((w, 3)), dma((w, 3))]
    if s:
        scratch += [dma((s, 2))] * 3 + [dma((s,))] * 2
    return pl.pallas_call(
        functools.partial(spread_kernel, n, w, s, group),
        out_shape=shapes,
        in_specs=[any_spec] * (n + w + s),
        out_specs=[any_spec] * (n + w) + [vmem] * s,
        scratch_shapes=scratch,
        compiler_params=pltpu.CompilerParams(collective_id=number, has_side_effects=True, vmem_limit_bytes=40 * MIB),
        name="spread%d" % number,
    )(*arrays, *wide, *sums)


def add_blocks(target, sources, rows):
    step = min(rows, 16)

    def body(j, carry):
        at = pl.ds(pl.multiple_of(j * step, step), step)

        def view(item):
            ref, lead, columns = item
            return ref, tuple(lead) + (at,) + (() if columns is None else (columns,))

        total = None
        for item in sources:
            ref, index = view(item)
            value = ref[index].astype(FLOAT)
            total = value if total is None else total + value
        ref, index = view(target)
        ref[index] = total.astype(ref.dtype)
        return carry

    lax.fori_loop(0, rows // step, body, 0)


def head_kernel(group, cut, dense, *refs):
    ins, outs = refs[: dense + 2], refs[dense + 2 : 2 * dense + 4]
    own_sems, send_sems, recv_sems, swap_send, swap_recv, row_send, row_recv = refs[2 * dense + 4 :]
    shared_ref, shared_out = ins[dense], outs[dense]
    row_ref, row_out = ins[dense + 1], outs[dense + 1]
    line = group // 2
    y, c, z, x = places(group)
    sibling, opposite = {"dp": 2 * y + 1 - c}, {"dp": 2 * (1 - y) + c}
    rising, falling, across = {"expert": 2 * (z + 1) + x}, {"expert": 2 * (z - 1) + x}, {"expert": 2 * z + 1 - x}
    me = 2 * z + x
    peers = [(None, {"expert": lax.rem(me + k, group)}) for k in range(1, group)]
    greet(peers + [(None, sibling), (None, opposite)])
    width = ins[0].shape[1]
    pieces = [(0, pl.ds(0, cut), True), (0, pl.ds(cut, width - cut), False)]
    pieces += [(i, pl.ds(0, ins[i].shape[1]), True) for i in range(1, dense)]
    count = len(pieces)

    def copy(p, yy, cc, zz, xx, way, device, own=False):
        i, columns, _ = pieces[p]
        place = (2 * yy + cc) * group + 2 * zz + xx
        dst = outs[i].at[place, :, columns]
        src = ins[i].at[:, columns] if own else dst
        slot = yy * group + 2 * zz + xx
        return remote(src, dst, send_sems.at[p, slot, way], recv_sems.at[p, place], device)

    def row_copy(zz, xx, way, device, own=False):
        dst = row_out.at[2 * zz + xx]
        return remote(row_ref if own else dst, dst, row_send.at[zz, way], row_recv.at[2 * zz + xx], device)

    def swap(k):
        to = lax.rem(me + k, group)
        return remote(shared_ref.at[to], shared_out.at[me], swap_send.at[k], swap_recv.at[me], {"expert": to})

    def own_copy(i):
        if i < dense:
            return pltpu.make_async_copy(ins[i], outs[i].at[(2 * y + c) * group + me], own_sems.at[i])
        if i == dense:
            return pltpu.make_async_copy(shared_ref.at[me], shared_out.at[me], own_sems.at[i])
        return pltpu.make_async_copy(row_ref, row_out.at[me], own_sems.at[i])

    def steps(act):
        for s in range(line):
            for up in (True, False) if s else (True,):
                zz = z - s if up else z + s
                valid = (z - s >= 0) if up else (z + s < line)

                @pl.when(valid)
                def _():
                    act(s, up, zz)

    def column_moves(p, s, up, zz):
        own = s == 0
        make = functools.partial(row_copy, zz, x) if p is None else functools.partial(copy, p, y, c, zz, x)
        moves = []
        if up:
            moves.append((z < line - 1, functools.partial(make, 0, rising, own)))
        if not up or own:
            moves.append((z > 0, functools.partial(make, 1, falling, own)))
        moves.append((None, functools.partial(make, 2, across, own)))
        if p is not None:
            moves.append((None, functools.partial(make, 3, opposite, own)))
            moves.append((None, functools.partial(make, 4, sibling, own)))
        return moves

    def run(moves, act):
        for condition, move in moves:
            if condition is None:
                act(move())
            else:
                pl.when(condition)(lambda: act(move()))

    def later_moves(p):
        if pieces[p][2]:
            return [
                (0, [(3, opposite), (4, sibling)], (y, 1 - x)),
                (1, [(4, sibling)], (1 - y, x)),
                (1, [(4, sibling)], (1 - y, 1 - x)),
            ]
        return [
            (0, [(2, across), (4, sibling)], (1 - y, x)),
            (1, [(4, sibling)], (y, 1 - x)),
            (1, [(4, sibling)], (1 - y, 1 - x)),
        ]

    everything = list(range(count)) + [None]

    def column(s, up, zz):
        for p in range(count):
            if s:
                copy(p, y, c, zz, x, 4, sibling).wait_recv()
            run(column_moves(p, s, up, zz), lambda item: item.start())
        if s == 0:
            for k in range(1, group):
                swap(k).start()
            for i in range(dense + 2):
                own_copy(i).start()

    def rows(s, up, zz):
        if s:
            row_copy(zz, x, 2, across).wait_recv()
        run(column_moves(None, s, up, zz), lambda item: item.start())

    def later(phase, start):
        def act(s, up, zz):
            for p in range(count):
                for when, sends, (yy, xx) in later_moves(p):
                    if when != phase:
                        continue
                    if start:
                        copy(p, yy, c, zz, xx, 4, sibling).wait_recv()
                    for way, device in sends:
                        item = copy(p, yy, c, zz, xx, way, device)
                        if start:
                            item.start()
                        else:
                            item.wait_send()

        return act

    def finish(s, up, zz):
        row_copy(zz, 1 - x, 2, across).wait_recv()
        for p in range(count):
            for yy in range(2):
                for xx in range(2):
                    copy(p, yy, 1 - c, zz, xx, 4, sibling).wait_recv()

    def settle(s, up, zz):
        for p in everything:
            run(column_moves(p, s, up, zz), lambda item: item.wait_send())

    only = lambda act, k: steps(lambda s, up, zz: act(s, up, zz) if s == k else None)
    for k in range(line + 2):
        if k < line:
            only(column, k)
            only(rows, k)
        if 0 <= k - 1 < line:
            only(later(0, True), k - 1)
        if 0 <= k - 2 < line:
            only(later(1, True), k - 2)
    steps(finish)
    steps(settle)
    steps(later(0, False))
    steps(later(1, False))
    for k in range(1, group):
        source = lax.rem(me + k, group)
        remote(shared_ref.at[source], shared_out.at[source], swap_send.at[k], swap_recv.at[source], across).wait_recv()
        swap(k).wait_send()
    for i in range(dense + 2):
        own_copy(i).wait()


def head_exchange(dense, shared, rows, number):
    group = lax.axis_size("expert")
    total = 4 * group
    count = len(dense) + 1
    dma = pltpu.SemaphoreType.DMA
    any_spec = pl.BlockSpec(memory_space=pl.ANY)
    cut = dense[0].shape[1] * 9 // 10 // 128 * 128
    return pl.pallas_call(
        functools.partial(head_kernel, group, cut, len(dense)),
        out_shape=[jax.ShapeDtypeStruct((total,) + a.shape, a.dtype) for a in dense]
        + [
            jax.ShapeDtypeStruct(shared.shape, shared.dtype),
            jax.ShapeDtypeStruct((group,) + rows.shape, rows.dtype),
        ],
        in_specs=[any_spec] * (len(dense) + 2),
        out_specs=[any_spec] * (len(dense) + 2),
        scratch_shapes=[
            dma((len(dense) + 2,)),
            dma((count, 2 * group, 5)),
            dma((count, total)),
            dma((group,)),
            dma((group,)),
            dma((group // 2, 3)),
            dma((group,)),
        ],
        compiler_params=pltpu.CompilerParams(collective_id=number, has_side_effects=True),
        name="head_exchange",
    )(*dense, shared, rows)


def farthest(z, line, j):
    table = [sorted(range(line), key=lambda d: (-abs(d - k), d)) for k in range(line)]
    return sum(
        jnp.where((z == k) & (j == n), table[k][n], 0) for k in range(line) for n in range(line) if table[k][n]
    )


def tail_kernel(group, sums, steps, *refs):
    (left_ref, right_ref, router_ref, shared_ref, small_ref) = refs[:5]
    sum_ins, refs = refs[5 : 5 + sums], refs[5 + sums :]
    (mix_out, router_out, shared_out, small_out) = refs[:4]
    sum_outs, refs = refs[4 : 4 + sums], refs[4 + sums :]
    bufs = refs[:12]
    made, totals, small_landed = refs[12:15]
    sum_bufs, refs = refs[15 : 15 + 3 * sums], refs[15 + 3 * sums :]
    sum_own, sum_core_send, sum_core_recv, sum_side_send, sum_side_recv, sum_store, late_send, late_recv = refs[-8:]
    (own_sems, core_send, core_recv, one_send, one_recv, two_send, two_recv, line_send, line_recv,
     swap_send, swap_recv, small_send, small_recv, keep_sem) = refs[:-8]
    line = group // 2
    y, c, z, x = places(group)
    sibling, opposite = {"dp": 2 * y + 1 - c}, {"dp": 2 * (1 - y) + c}
    rising, falling, across = {"expert": 2 * (z + 1) + x}, {"expert": 2 * (z - 1) + x}, {"expert": 2 * z + 1 - x}
    me = 2 * z + x

    def partner(axis, bit):
        here = lax.axis_index(axis)
        return {axis: here + bit * (1 - 2 * lax.rem(here // bit, 2))}

    peers = [(None, {"expert": lax.rem(me + k, group)}) for k in range(1, group)]
    greet(peers + [(None, sibling), (None, opposite)])

    outs = (mix_out, router_out)
    held, landed, one, two, below, above = (bufs[0:2], bufs[2:4], bufs[4:6], bufs[6:8], bufs[8:10], bufs[10:12])
    rows, width = mix_out.shape
    pieces = [(0, pl.ds(0, width), False), (1, pl.ds(0, router_ref.shape[2]), True)]
    count = len(pieces)

    def slot(yy, zz, xx):
        return yy * group + 2 * zz + xx

    def load(yy, zz, xx):
        s = slot(yy, zz, xx)
        return pltpu.make_async_copy(router_ref.at[(2 * yy + c) * group + 2 * zz + xx], held[1].at[s], own_sems.at[s])

    def to_sibling(a, yy, zz, xx, turn=0):
        s = slot(yy, zz, xx)
        source = made.at[4 * turn + 2 * yy + xx] if a == 0 else router_ref.at[(2 * yy + 1 - c) * group + 2 * zz + xx]
        return remote(source, landed[a].at[s], core_send.at[a, s], core_recv.at[a, s], sibling)

    def make(cc, zz, target, place_of):
        lefts = []
        for yy in range(2):
            start = pl.multiple_of(((2 * yy + cc) * group + 2 * zz) * rows, 16)
            lefts.append(left_ref[pl.ds(start, 2 * rows)])
        lefts = jnp.concatenate(lefts, axis=0)
        step = 1664
        for start in range(0, width, step):
            columns = slice(start, min(start + step, width))
            product = jnp.dot(lefts, right_ref[:, columns], preferred_element_type=FLOAT).astype(BRAIN)
            for yy in range(2):
                for xx in range(2):
                    place = (2 * yy + xx) * rows
                    target[place_of(yy, xx), :, columns] = product[place : place + rows]

    def stage_one(p, zz, k):
        a, columns, over_y = pieces[p]
        s = slot(1 - y, zz, k) if over_y else slot(k, zz, 1 - x)
        return remote(
            held[a].at[s, :, columns], one[a].at[2 * zz + k, :, columns], one_send.at[p, 2 * zz + k],
            one_recv.at[p, 2 * zz + k], opposite if over_y else across,
        )

    def stage_two(p, zz):
        a, columns, over_y = pieces[p]
        s = slot(y, zz, 1 - x) if over_y else slot(1 - y, zz, x)
        return remote(
            held[a].at[s, :, columns], two[a].at[zz, :, columns], two_send.at[p, zz], two_recv.at[p, zz],
            across if over_y else opposite,
        )

    def rise(a, zz):
        return remote(held[a].at[slot(y, zz, x)], below[a].at[zz], line_send.at[a, 0, zz], line_recv.at[a, 0, zz], rising)

    def fall(a, zz):
        return remote(held[a].at[slot(y, zz, x)], above[a].at[zz], line_send.at[a, 1, zz], line_recv.at[a, 1, zz], falling)

    def swap(k):
        to = lax.rem(me + k, group)
        return remote(shared_ref.at[to], shared_out.at[me], swap_send.at[k], swap_recv.at[me], {"expert": to})

    def small(step):
        axis, bit = steps[step]
        return remote(
            totals.at[step], small_landed.at[step], small_send.at[step], small_recv.at[step], partner(axis, bit)
        )

    keep = pltpu.make_async_copy(shared_ref.at[me], shared_out.at[me], keep_sem)
    keep.start()
    corners = [(yy, xx) for yy in range(2) for xx in range(2)]
    for zz in range(line):
        for yy, xx in corners:
            to_sibling(1, yy, zz, xx).start()
            load(yy, zz, xx).start()
    for k in range(1, group):
        swap(k).start()
    totals[0] = small_ref[...]
    small(0).start()

    def advance(step):
        if step < len(steps):
            small(step).wait()
            totals[step + 1] = totals[step] + small_landed[step]
            if step + 1 < len(steps):
                small(step + 1).start()

    def phase_make(zz, t):
        turn = lax.rem(t, 2)

        @pl.when(t >= 2)
        def _():
            for yy, xx in corners:
                to_sibling(0, yy, farthest(z, line, t - 2), xx, turn).wait_send()

        make(1 - c, zz, made, lambda yy, xx: 4 * turn + 2 * yy + xx)
        for yy, xx in corners:
            to_sibling(0, yy, zz, xx, turn).start()
        make(c, zz, held[0], lambda yy, xx: slot(yy, zz, xx))

    def sum_parts(k):
        kept, landed, arrived = sum_bufs[3 * k : 3 * k + 3]
        source = sum_ins[k]
        height = source.shape[1] // 4

        def piece(q):
            return source.at[:, pl.ds(pl.multiple_of(q * height, height), height), :]

        def take(h):
            return pltpu.make_async_copy(piece(2 * h + c), kept.at[h], sum_own.at[k, h])

        def give(h):
            return remote(piece(2 * h + 1 - c), landed.at[h], sum_core_send.at[k, h], sum_core_recv.at[k, h], sibling)

        def pass_on():
            return remote(kept.at[1 - y], arrived, sum_side_send.at[k], sum_side_recv.at[k], opposite)

        def add(h, extra):
            for e in range(source.shape[0]):
                items = [(kept, (h, e), None), (landed, (h, e), None)] + ([(arrived, (e,), None)] if extra else [])
                add_blocks((kept, (h, e), None), items, height)

        def store():
            return pltpu.make_async_copy(kept.at[y], sum_outs[k], sum_store.at[k])

        return take, give, pass_on, add, store

    def sums_first():
        for k in range(sums):
            take, give, pass_on, add, store = sum_parts(k)
            take(1 - y).wait()
            give(1 - y).wait_recv()
            add(1 - y, False)
            pass_on().start()

    def late(k):
        to = lax.rem(me + k, group)
        height = sum_outs[0].shape[1]
        block = sum_bufs[0].at[y, 0, pl.ds(pl.multiple_of(to * height, 16), height)]
        if k == 0:
            return pltpu.make_async_copy(block, sum_outs[0].at[me], late_send.at[k])
        return remote(block, sum_outs[0].at[me], late_send.at[k], late_recv.at[me], {"expert": to})

    def sums_last(which):
        for k in which:
            take, give, pass_on, add, store = sum_parts(k)
            take(y).wait()
            give(y).wait_recv()
            pass_on().wait_recv()
            add(y, True)
            if k:
                store().start()
            else:
                for n in range(group):
                    late(n).start()

    def sums_settle():
        for k in range(sums):
            take, give, pass_on, add, store = sum_parts(k)
            give(y).wait_send()
            give(1 - y).wait_send()
            pass_on().wait_send()
            if k:
                store().wait()
        late(0).wait()
        for n in range(1, group):
            source = lax.rem(me + n, group)
            remote(
                shared_ref.at[source], sum_outs[0].at[source], late_send.at[n], late_recv.at[source], across
            ).wait_recv()
            late(n).wait_send()

    def phase_a(zz):
        for a in range(2):
            for yy, xx in corners:
                s = slot(yy, zz, xx)
                if a == 1:
                    load(yy, zz, xx).wait()
                to_sibling(a, yy, zz, xx).wait_recv()
                add_blocks((held[a], (s,), None), [(held[a], (s,), None), (landed[a], (s,), None)], rows)
        for p in range(count):
            for k in range(2):
                stage_one(p, zz, k).start()

    def phase_b(zz):
        for p, (a, columns, over_y) in enumerate(pieces):
            for k in (1 - x, x) if over_y else (1 - y, y):
                s = slot(y, zz, k) if over_y else slot(k, zz, x)
                stage_one(p, zz, k).wait_recv()
                add_blocks(
                    (held[a], (s,), columns), [(held[a], (s,), columns), (one[a], (2 * zz + k,), columns)], rows
                )
            stage_two(p, zz).start()

    def phase_c(zz):
        s = slot(y, zz, x)
        for p in range(count):
            stage_two(p, zz).wait_recv()
        for a in range(2):
            base = [(held[a], (s,), None), (two[a], (zz,), None)]
            low = (below[a], (zz,), None)
            high = (above[a], (zz,), None)
            kept = (held[a], (s,), None)

            @pl.when(zz > z)
            def _():
                @pl.when(z > 0)
                def _():
                    rise(a, zz).wait_recv()
                    add_blocks(kept, base + [low], rows)

                @pl.when(z == 0)
                def _():
                    add_blocks(kept, base, rows)

                rise(a, zz).start()

            @pl.when(zz < z)
            def _():
                @pl.when(z < line - 1)
                def _():
                    fall(a, zz).wait_recv()
                    add_blocks(kept, base + [high], rows)

                @pl.when(z == line - 1)
                def _():
                    add_blocks(kept, base, rows)

                fall(a, zz).start()

    def phase_last():
        s = slot(y, z, x)
        for p in range(count):
            stage_two(p, z).wait_recv()
        for a in range(2):
            base = [(held[a], (s,), None), (two[a], (z,), None)]
            low = (below[a], (z,), None)
            high = (above[a], (z,), None)
            final = (outs[a], (), None)

            @pl.when(z == 0)
            def _():
                fall(a, z).wait_recv()
                add_blocks(final, base + [high], rows)

            @pl.when(z == line - 1)
            def _():
                rise(a, z).wait_recv()
                add_blocks(final, base + [low], rows)

            @pl.when((z > 0) & (z < line - 1))
            def _():
                fall(a, z).wait_recv()
                rise(a, z).wait_recv()
                add_blocks(final, base + [low, high], rows)

    for k in range(sums):
        take, give = sum_parts(k)[:2]
        for h in (1 - y, y):
            take(h).start()
            give(h).start()

    def body(t, carry):
        for shift, phase, number in ((0, phase_make, line), (1, phase_a, line), (2, phase_b, line), (3, phase_c, line - 1)):

            @pl.when((t >= shift) & (t - shift < number))
            def _():
                phase(farthest(z, line, t - shift), *([t] if shift == 0 else []))

        pl.when(t == 0)(sums_first)
        pl.when(t == 4)(lambda: sums_last([0]))
        for step in range(len(steps)):
            pl.when(t == step + 1)(functools.partial(advance, step))
        return carry

    lax.fori_loop(0, max(line + 3, len(steps) + 1), body, 0)
    phase_last()
    sums_last(range(1, sums))
    sums_settle()
    for t in (line - 2, line - 1):
        for yy, xx in corners:
            to_sibling(0, yy, farthest(z, line, t), xx, t % 2).wait_send()
    small_out[...] = totals[len(steps)]
    for k in range(1, group):
        source = lax.rem(me + k, group)
        remote(shared_ref.at[source], shared_out.at[source], swap_send.at[k], swap_recv.at[source], across).wait_recv()
        swap(k).wait_send()
    keep.wait()
    for zz in range(line):
        for a in range(2):
            if a == 1:
                for yy, xx in corners:
                    to_sibling(a, yy, zz, xx).wait_send()
            pl.when(zz > z)(lambda: rise(a, zz).wait_send())
            pl.when(zz < z)(lambda: fall(a, zz).wait_send())
        for p in range(count):
            for k in range(2):
                stage_one(p, zz, k).wait_send()
            stage_two(p, zz).wait_send()


def tail_exchange(left, right, routers, shared, small, sums, number):
    group = lax.axis_size("expert")
    line = group // 2
    steps = []
    for axis in BOTH:
        bit = 1
        while bit < lax.axis_size(axis):
            steps.append((axis, bit))
            bit *= 2
    dma = pltpu.SemaphoreType.DMA
    vmem = pl.BlockSpec(memory_space=pltpu.VMEM)
    any_spec = pl.BlockSpec(memory_space=pl.ANY)
    mix = (left.shape[0] // (4 * group), right.shape[1])
    scratch = []
    for blocks in (2 * group, 2 * group, group, line, line, line):
        scratch += [pltpu.VMEM((blocks,) + shape, BRAIN) for shape in (mix, routers.shape[1:])]
    scratch += [pltpu.VMEM((8,) + mix, BRAIN)]
    scratch += [pltpu.VMEM((len(steps) + 1,) + small.shape, FLOAT), pltpu.VMEM((len(steps),) + small.shape, FLOAT)]
    parts = [(a.shape[0], a.shape[1] // 4, a.shape[2]) for a in sums]
    for part in parts:
        scratch += [pltpu.VMEM((2,) + part, BRAIN)] * 2 + [pltpu.VMEM(part, BRAIN)]
    scratch += [dma((2 * group,))] + [dma((2, 2 * group))] * 2
    scratch += [dma((2, group))] * 2 + [dma((2, line))] * 2 + [dma((2, 2, line))] * 2
    scratch += [dma((group,))] * 2 + [dma((len(steps),))] * 2 + [dma]
    scratch += [dma((len(sums), 2))] * 3 + [dma((len(sums),))] * 3 + [dma((group,))] * 2
    return pl.pallas_call(
        functools.partial(tail_kernel, group, len(sums), steps),
        out_shape=[
            jax.ShapeDtypeStruct(mix, FLOAT),
            jax.ShapeDtypeStruct(routers.shape[1:], FLOAT),
            jax.ShapeDtypeStruct(shared.shape, shared.dtype),
            jax.ShapeDtypeStruct(small.shape, FLOAT),
        ]
        + [jax.ShapeDtypeStruct(shared.shape, BRAIN)]
        + [jax.ShapeDtypeStruct(part, BRAIN) for part in parts[1:]],
        in_specs=[vmem, vmem, any_spec, any_spec, vmem] + [any_spec] * len(sums),
        out_specs=[vmem, vmem, any_spec, vmem] + [any_spec] * len(sums),
        scratch_shapes=scratch,
        compiler_params=pltpu.CompilerParams(collective_id=number, has_side_effects=True, vmem_limit_bytes=62 * MIB),
        name="tail_exchange",
    )(left, right, routers, shared, small, *sums)


def state_setup(step_ref, rate_ref, step_t_ref, rate_t_ref, b_ref, c_ref, cum, cum_t, cross):
    length = step_ref.shape[0]
    down = lax.broadcasted_iota(jnp.int32, (length, length), 0)
    along = lax.broadcasted_iota(jnp.int32, (length, length), 1)
    lower = jnp.where(down >= along, 1.0, 0.0)
    upper = jnp.where(down <= along, 1.0, 0.0)
    cum[...] = jnp.dot(
        lower, step_ref[...] * rate_ref[...], precision=HIGH, preferred_element_type=FLOAT
    )
    cum_t[...] = jnp.dot(
        step_t_ref[...] * rate_t_ref[...], upper, precision=HIGH, preferred_element_type=FLOAT
    )
    cross[...] = lax.dot_general(
        c_ref[...], b_ref[...], (((1,), (1,)), ((), ())), precision=HIGH, preferred_element_type=FLOAT
    )


def decay_of(head, cum, cum_t):
    length, heads = cum.shape
    lane = lax.broadcasted_iota(jnp.int32, (length, heads), 1)
    column = jnp.sum(jnp.where(lane == head, cum[...], 0.0), axis=1, keepdims=True)
    spread_out = column - cum_t[pl.ds(head, 1), :]
    down = lax.broadcasted_iota(jnp.int32, (length, length), 0)
    along = lax.broadcasted_iota(jnp.int32, (length, length), 1)
    return jnp.exp(jnp.where(down >= along, spread_out, -1e30))


def state_forward_kernel(
    x_ref, b_ref, c_ref, step_ref, rate_ref, step_t_ref, rate_t_ref, skip_ref, y_ref, cum, cum_t, cross
):
    pair = pl.program_id(0)

    @pl.when(pair == 0)
    def _():
        state_setup(step_ref, rate_ref, step_t_ref, rate_t_ref, b_ref, c_ref, cum, cum_t, cross)

    values = x_ref[...]
    values_low = values.astype(BRAIN)
    total = values * skip_ref[...]
    side = lax.broadcasted_iota(jnp.int32, values.shape, 1) // MHDIM
    for j in range(2):
        head = 2 * pair + j
        mixing = cross[...] * decay_of(head, cum, cum_t) * step_t_ref[pl.ds(head, 1), :]
        part = jnp.dot(mixing.astype(BRAIN), values_low, preferred_element_type=FLOAT)
        total = total + jnp.where(side == j, part, 0.0)
    y_ref[...] = total


def state_specs(length):
    column = lambda place: pl.BlockSpec((length, NSTATE), place)
    return [
        column(lambda i: (0, i)),
        column(lambda i: (0, DI // NSTATE)),
        column(lambda i: (0, DI // NSTATE + 1)),
        whole_spec((length, MHEADS)),
        whole_spec((1, MHEADS)),
        whole_spec((MHEADS, length)),
        whole_spec((MHEADS, 1)),
        pl.BlockSpec((1, 2 * MHDIM), lambda i: (0, i)),
    ]


def state_operands(conv_out, step_size, decay_rate, skip_gain):
    return (
        conv_out,
        conv_out,
        conv_out,
        step_size,
        decay_rate[None, :],
        step_size.T,
        decay_rate[:, None],
        jnp.repeat(skip_gain, MHDIM)[None, :],
    )


def state_forward(conv_out, step_size, decay_rate, skip_gain):
    length = conv_out.shape[0]
    return pl.pallas_call(
        state_forward_kernel,
        grid=(MHEADS // 2,),
        out_shape=jax.ShapeDtypeStruct((length, DI), FLOAT),
        in_specs=state_specs(length),
        out_specs=pl.BlockSpec((length, 2 * MHDIM), lambda i: (0, i)),
        scratch_shapes=[
            pltpu.VMEM((length, MHEADS), FLOAT),
            pltpu.VMEM((MHEADS, length), FLOAT),
            pltpu.VMEM((length, length), FLOAT),
        ],
        compiler_params=pltpu.CompilerParams(vmem_limit_bytes=32 * MIB),
        name="state_forward",
    )(*state_operands(conv_out, step_size, decay_rate, skip_gain))


def state_backward_kernel(
    x_ref, b_ref, c_ref, step_ref, rate_ref, step_t_ref, rate_t_ref, skip_ref, dy_ref,
    dx_ref, db_ref, dc_ref, row_ref, column_ref, cum, cum_t, cross, dcross,
):
    pair = pl.program_id(0)

    @pl.when(pair == 0)
    def _():
        state_setup(step_ref, rate_ref, step_t_ref, rate_t_ref, b_ref, c_ref, cum, cum_t, cross)
        dcross[...] = jnp.zeros_like(dcross)
        row_ref[...] = jnp.zeros_like(row_ref)

    values_low = x_ref[...].astype(BRAIN)
    grads = dy_ref[...]
    total = grads * skip_ref[...]
    side = lax.broadcasted_iota(jnp.int32, grads.shape, 1) // MHDIM
    lane = lax.broadcasted_iota(jnp.int32, row_ref.shape, 1)
    for j in range(2):
        head = 2 * pair + j
        steps = step_t_ref[pl.ds(head, 1), :]
        decay = decay_of(head, cum, cum_t)
        own = jnp.where(side == j, grads, 0.0).astype(BRAIN)
        mixing = cross[...] * decay
        total = total + matmul_tn((mixing * steps).astype(BRAIN), own)
        dmix = matmul_nt(own, values_low)
        dcross[...] += dmix * decay * steps
        weighed = dmix * mixing
        column_ref[pl.ds(head, 1), :] = jnp.sum(weighed, axis=0, keepdims=True)
        row_sum = jnp.sum(weighed * steps, axis=1, keepdims=True)
        row_ref[...] += jnp.where(lane == head, row_sum, 0.0)
    dx_ref[...] = total

    @pl.when(pair == pl.num_programs(0) - 1)
    def _():
        dc_ref[...] = jnp.dot(dcross[...], b_ref[...], precision=HIGH, preferred_element_type=FLOAT)
        db_ref[...] = lax.dot_general(
            dcross[...], c_ref[...], (((0,), (0,)), ((), ())), precision=HIGH, preferred_element_type=FLOAT
        )


def state_backward(conv_out, step_size, decay_rate, skip_gain, grad_mixed):
    length = conv_out.shape[0]
    pair_block = pl.BlockSpec((length, 2 * MHDIM), lambda i: (0, i))
    dx, db, dc, row_sums, column_sums = pl.pallas_call(
        state_backward_kernel,
        grid=(MHEADS // 2,),
        out_shape=[
            jax.ShapeDtypeStruct((length, DI), FLOAT),
            jax.ShapeDtypeStruct((length, NSTATE), FLOAT),
            jax.ShapeDtypeStruct((length, NSTATE), FLOAT),
            jax.ShapeDtypeStruct((length, MHEADS), FLOAT),
            jax.ShapeDtypeStruct((MHEADS, length), FLOAT),
        ],
        in_specs=state_specs(length) + [pair_block],
        out_specs=[
            pair_block,
            pl.BlockSpec((length, NSTATE), lambda i: (0, 0)),
            pl.BlockSpec((length, NSTATE), lambda i: (0, 0)),
            pl.BlockSpec((length, MHEADS), lambda i: (0, 0)),
            pl.BlockSpec((MHEADS, length), lambda i: (0, 0)),
        ],
        scratch_shapes=[
            pltpu.VMEM((length, MHEADS), FLOAT),
            pltpu.VMEM((MHEADS, length), FLOAT),
            pltpu.VMEM((length, length), FLOAT),
            pltpu.VMEM((length, length), FLOAT),
        ],
        compiler_params=pltpu.CompilerParams(vmem_limit_bytes=32 * MIB),
        name="state_backward",
    )(*state_operands(conv_out, step_size, decay_rate, skip_gain), grad_mixed)
    column_sums = column_sums.T
    dcum = row_sums - column_sums * step_size
    places = jnp.arange(length)
    upper = (places[:, None] <= places[None, :]).astype(FLOAT)
    drate_step = jnp.dot(upper, dcum, precision=HIGH, preferred_element_type=FLOAT)
    grad_step = column_sums + drate_step * decay_rate
    grad_decay_log = jnp.sum(drate_step * step_size, axis=0) * decay_rate
    return dx, db, dc, grad_step, grad_decay_log


def convolve(conv_in, conv_weight, conv_bias):
    length = conv_in.shape[0]
    padded = jnp.pad(conv_in, ((KCONV - 1, 0), (0, 0)))
    total = conv_bias + padded[0:length] * conv_weight[0]
    for tap in range(1, KCONV):
        total = total + padded[tap : tap + length] * conv_weight[tap]
    return silu_of(total)


def gated_norm(mixed, gate_z, mixer_gain):
    return rms_norm(mixed * silu_of(gate_z), mixer_gain)


def step_of(step_raw, step_bias):
    return softplus_of(step_raw + step_bias)


def mixer_forward(hidden, norm_gain, mixer_in, mixer_out, small):
    normed, norm_back = jax.vjp(rms_norm, hidden, norm_gain)
    normed_low = normed.astype(BRAIN)
    projected = matmul(normed_low, mixer_in)
    gate_z = projected[:, :DI]
    conv_in = projected[:, DI : DI + CONVCH]
    step_raw = projected[:, DI + CONVCH :]
    conv_out, conv_back = jax.vjp(convolve, conv_in, small["conv_weight"], small["conv_bias"])
    step_size, step_back = jax.vjp(step_of, step_raw, small["step_bias"])
    decay_rate = -jnp.exp(small["decay_log"])
    mixed = state_forward(conv_out, step_size, decay_rate, small["skip_gain"])
    mixer_norm, gated_back = jax.vjp(gated_norm, mixed, gate_z, small["mixer_gain"])
    mixer_low = mixer_norm.astype(BRAIN)
    output = hidden + matmul_nt(mixer_low, mixer_out)
    saved = (norm_back, normed_low, conv_out, conv_back, step_size, step_back, decay_rate, gated_back, mixer_low)
    return output, saved


def mixer_backward(grad_out, saved, mixer_in, mixer_out, small):
    norm_back, normed_low, conv_out, conv_back, step_size, step_back, decay_rate, gated_back, mixer_low = saved
    grad_low = grad_out.astype(BRAIN)
    grad_mixer_out = matmul_tn(grad_low, mixer_low).astype(BRAIN)
    grad_norm, grad_mixer_out = lax.optimization_barrier((matmul(grad_low, mixer_out), grad_mixer_out))
    grad_mixed, grad_gate, grad_mixer_gain = gated_back(grad_norm)
    dx, db, dc, grad_step, grad_decay_log = state_backward(
        conv_out, step_size, decay_rate, small["skip_gain"], grad_mixed
    )
    grad_skip = jnp.sum(jnp.sum(grad_mixed * conv_out[:, :DI], axis=0).reshape(MHEADS, MHDIM), axis=1)
    grad_conv_in, grad_conv_weight, grad_conv_bias = conv_back(jnp.concatenate([dx, db, dc], axis=1))
    grad_step_raw, grad_step_bias = step_back(grad_step)
    grad_proj = jnp.concatenate([grad_gate, grad_conv_in, grad_step_raw], axis=1).astype(BRAIN)
    grad_hidden, grad_gain = norm_back(matmul_nt(grad_proj, mixer_in))
    grad_small = (
        grad_mixer_gain, grad_conv_weight, grad_conv_bias, grad_decay_log, grad_step_bias, grad_skip
    )
    return grad_out + grad_hidden, grad_gain, normed_low, grad_proj, grad_mixer_out, grad_small


PARTS = 2


def fold(group, held, sent, crossed, passing, out_ref, sems):
    cross_send, cross_recv, up_send, up_recv, down_send, down_recv = sems
    line = group // 2
    z, x = places(group)[2:]
    rows = held.shape[1] // PARTS

    def piece(ref, d, p):
        return ref.at[d, pl.ds(p * rows, rows)]

    def cross(d, p):
        return remote(
            piece(sent, d, p), piece(crossed, d, p), cross_send.at[d, p], cross_recv.at[d, p], {"expert": 2 * z + 1 - x}
        )

    def rise(d, p):
        return remote(
            piece(held, d, p), piece(passing, d, p), up_send.at[d, p], up_recv.at[d, p], {"expert": 2 * (z + 1) + x}
        )

    def fall(d, p):
        return remote(
            piece(held, d, p),
            piece(passing, jnp.where(d == z - 1, line, d), p),
            down_send.at[d, p],
            down_recv.at[d, p],
            {"expert": 2 * (z - 1) + x},
        )

    def fallen(d, p):
        place = jnp.where(d == z, line, d)
        return remote(
            piece(held, d, p), piece(passing, place, p), down_send.at[d, p], down_recv.at[d, p], {"expert": 2 * (z + 1) + x}
        )

    def add(d, p, final, sources):
        def body(j, carry):
            at = pl.ds(pl.multiple_of(p * rows + j * 16, 16), 16)
            total = held[d, at].astype(FLOAT)
            for source, place in sources:
                total = total + source[place, at].astype(FLOAT)
            if final:
                out_ref[at] = total
            else:
                held[d, at] = total.astype(held.dtype)
            return carry

        lax.fori_loop(0, rows // 16, body, 0)

    def start_cross(d):
        for p in range(PARTS):
            cross(d, p).start()

    def chain(d):
        for p in range(PARTS):
            cross(d, p).wait_recv()

            @pl.when(d > z)
            def _():
                @pl.when(z > 0)
                def _():
                    rise(d, p).wait_recv()
                    add(d, p, False, [(crossed, d), (passing, d)])

                @pl.when(z == 0)
                def _():
                    add(d, p, False, [(crossed, d)])

                rise(d, p).start()

            @pl.when(d < z)
            def _():
                @pl.when(z < line - 1)
                def _():
                    fallen(d, p).wait_recv()
                    add(d, p, False, [(crossed, d), (passing, d)])

                @pl.when(z == line - 1)
                def _():
                    add(d, p, False, [(crossed, d)])

                fall(d, p).start()

    def last():
        for p in range(PARTS):
            cross(z, p).wait_recv()

            @pl.when(z == 0)
            def _():
                fallen(z, p).wait_recv()
                add(z, p, True, [(crossed, z), (passing, line)])

            @pl.when(z == line - 1)
            def _():
                rise(z, p).wait_recv()
                add(z, p, True, [(crossed, z), (passing, z)])

            @pl.when((z > 0) & (z < line - 1))
            def _():
                fallen(z, p).wait_recv()
                rise(z, p).wait_recv()
                add(z, p, True, [(crossed, z), (passing, z), (passing, line)])

    def settle():
        for d in range(line):
            for p in range(PARTS):
                cross(d, p).wait_send()
                pl.when(d > z)(lambda: rise(d, p).wait_send())
                pl.when(d < z)(lambda: fall(d, p).wait_send())

    return start_cross, chain, last, settle


def fold_scratch(group, tokens, width):
    line = group // 2
    dma = pltpu.SemaphoreType.DMA
    blocks = [pltpu.VMEM((line, tokens, width), BRAIN)] * 3 + [pltpu.VMEM((line + 1, tokens, width), BRAIN)]
    return blocks + [dma((line, PARTS))] * 6


def run_blocks(group, compute, held, sent, start_cross, chain, last, between=None, early=None):
    line = group // 2
    z, x = places(group)[2:]

    def body(j, carry):
        d = farthest(z, line, j // 2)
        crossing = lax.rem(j, 2) == 0

        if early is not None:
            pl.when(j == 2)(early)

        @pl.when(j == group - 2)
        def _():
            chain(farthest(z, line, 0))

        total = compute(2 * d + jnp.where(crossing, 1 - x, x)).astype(BRAIN)

        @pl.when(crossing)
        def _():
            sent[d] = total
            start_cross(d)

        @pl.when(jnp.logical_not(crossing))
        def _():
            held[d] = total

        return carry

    lax.fori_loop(0, group, body, 0)
    for j in range(1, line - 1):
        chain(farthest(z, line, j))
        if between is not None:
            between(j - 1, line - 2)
    last()


def load_blocks(group, source, target, sems):
    z, x = places(group)[2:]

    def load(s):
        return pltpu.make_async_copy(source.at[s], target.at[s], sems.at[s])

    def body(j, carry):
        d = farthest(z, group // 2, j // 2)
        load(2 * d + jnp.where(lax.rem(j, 2) == 0, 1 - x, x)).start()
        return carry

    lax.fori_loop(0, group, body, 0)
    return lambda s: load(s).wait()


def pick_rows(gates):
    tokens = gates.shape[1]
    down = lax.broadcasted_iota(jnp.int32, (tokens, tokens), 0)
    along = lax.broadcasted_iota(jnp.int32, (tokens, tokens), 1)
    upper = jnp.where(down <= along, 1.0, 0.0).astype(BRAIN)
    live = jnp.where(gates != 0.0, 1.0, 0.0)
    place = jnp.dot(
        jnp.broadcast_to(live, (8, tokens)).astype(BRAIN), upper, preferred_element_type=FLOAT
    )[0:1] - 1.0
    ranks = lax.broadcasted_iota(jnp.int32, (PICKED, tokens), 0).astype(FLOAT)
    return (ranks == place) & (live > 0.0)


def sum_flow(ins, outs, bufs, sems, group):
    own, core_send, core_recv, side_send, side_recv, keep = sems
    y, c = places(group)[:2]
    sibling, opposite = {"dp": 2 * y + 1 - c}, {"dp": 2 * (1 - y) + c}

    def parts(k):
        kept, landed, arrived = bufs[3 * k : 3 * k + 3]
        source = ins[k]
        height = source.shape[1] // 4

        def piece(q):
            return source.at[:, pl.ds(pl.multiple_of(q * height, height), height), :]

        def take(h):
            return pltpu.make_async_copy(piece(2 * h + c), kept, own.at[k, h])

        def give(h):
            return remote(piece(2 * h + 1 - c), landed.at[h], core_send.at[k, h], core_recv.at[k, h], sibling)

        def pass_on():
            return remote(kept, arrived, side_send.at[k], side_recv.at[k], opposite)

        def add(h, extra):
            for e in range(source.shape[0]):
                items = [(kept, (e,), None), (landed, (h, e), None)] + ([(arrived, (e,), None)] if extra else [])
                add_blocks((kept, (e,), None), items, height)

        def store():
            return pltpu.make_async_copy(kept, outs[k], keep.at[k])

        return take, give, pass_on, add, store

    def begin():
        for k in range(len(ins)):
            take, give = parts(k)[:2]
            take(1 - y).start()
            for h in (1 - y, y):
                give(h).start()

    def cross():
        for k in range(len(ins)):
            take, give, pass_on, add, store = parts(k)
            take(1 - y).wait()
            give(1 - y).wait_recv()
            add(1 - y, False)
            pass_on().start()

    def finish():
        for k in range(len(ins)):
            take, give, pass_on, add, store = parts(k)
            pass_on().wait_send()
            take(y).start()
            take(y).wait()
            give(y).wait_recv()
            pass_on().wait_recv()
            add(y, True)
            store().start()
        for k in range(len(ins)):
            take, give, pass_on, add, store = parts(k)
            give(y).wait_send()
            give(1 - y).wait_send()
            store().wait()

    return begin, cross, finish


def sum_parts_of(sums):
    return [(a.shape[0], a.shape[1] // 4, a.shape[2]) for a in sums]


def sum_scratch(sums):
    scratch = []
    for part in sum_parts_of(sums):
        scratch += [pltpu.VMEM(part, BRAIN), pltpu.VMEM((2,) + part, BRAIN), pltpu.VMEM(part, BRAIN)]
    return scratch


def sum_sems(count):
    dma = pltpu.SemaphoreType.DMA
    return [dma((count, 2))] * 3 + [dma((count,))] * 3


def wide_flow(ins, outs, stages, sems, group):
    own_sems, send_sems, recv_sems = sems
    y, c = places(group)[:2]
    sibling, opposite = {"dp": 2 * y + 1 - c}, {"dp": 2 * (1 - y) + c}
    own, other = 2 * y + c, 2 * (1 - y) + c
    count = len(ins)

    def block(i, q):
        rows = ins[i].shape[0]
        return outs[i].at[pl.ds(pl.multiple_of(q * rows, rows), rows)]

    def copy(i, kind):
        src = block(i, other) if kind == 2 else ins[i]
        dst = block(i, other if kind == 2 else own)
        return remote(src, dst, send_sems.at[i, kind], recv_sems.at[i, kind], opposite if kind == 1 else sibling)

    def load(i):
        return pltpu.make_async_copy(ins[i], stages[i], own_sems.at[i])

    def keep(i):
        return pltpu.make_async_copy(stages[i], block(i, own), own_sems.at[i])

    def begin():
        for i in range(count):
            copy(i, 1).start()
            copy(i, 0).start()
            load(i).start()

    def store():
        for i in range(count):
            load(i).wait()
            keep(i).start()

    def forward(i):
        copy(i, 1).wait_recv()
        copy(i, 2).start()

    def finish():
        for i in range(count):
            copy(i, 0).wait()
            copy(i, 1).wait_send()
            copy(i, 2).wait()
            keep(i).wait()

    return begin, store, forward, finish


def expert_forward_kernel(group, wide, x_hbm, g_ref, in_ref, out_ref, sin_ref, sout_ref, *refs):
    wide_ins, (y_ref, xe_ref, gu_ref, sgu_ref), refs = refs[:wide], refs[wide : wide + 4], refs[wide + 4 :]
    wide_outs, stages, refs = refs[:wide], refs[wide : 2 * wide], refs[2 * wide :]
    rows_ref, held, sent, crossed, passing, *sems = refs
    y, c, z, x = places(group)
    wait_load = load_blocks(group, x_hbm, rows_ref, sems[6])
    peers = line_peers(z, x, group // 2)
    if wide:
        peers += [(None, {"dp": 2 * y + 1 - c}), (None, {"dp": 2 * (1 - y) + c})]
    greet(peers)
    if wide:
        begin, store, forward, finish = wide_flow(wide_ins, wide_outs, stages, sems[7:], group)
        begin()
    start_cross, chain, last, settle = fold(group, held, sent, crossed, passing, y_ref, sems[:6])

    def compute(s):
        wait_load(s)
        rows = rows_ref[s]
        shared_gu = jnp.dot(rows, sin_ref[...], preferred_element_type=FLOAT)
        half = shared_gu.shape[1] // 2
        shared_mid = (silu_of(shared_gu[:, :half]) * shared_gu[:, half:]).astype(BRAIN)
        sgu_ref[s] = shared_gu.astype(sgu_ref.dtype)
        total = matmul_nt(shared_mid, sout_ref[...])
        for e in range(in_ref.shape[0]):
            gates = g_ref[s, e : e + 1, :]
            hit = pick_rows(gates)
            picked = jnp.dot(
                jnp.where(hit, 1.0, 0.0).astype(BRAIN), rows, preferred_element_type=FLOAT
            ).astype(BRAIN)
            gate_up = jnp.dot(picked, in_ref[e], preferred_element_type=FLOAT)
            width = gate_up.shape[1] // 2
            inner = (silu_of(gate_up[:, :width]) * gate_up[:, width:]).astype(BRAIN)
            result = matmul_nt(inner, out_ref[e]).astype(BRAIN)
            total = total + matmul_tn(jnp.where(hit, gates, 0.0).astype(BRAIN), result)
            xe_ref[e, s] = picked
            gu_ref[e, s] = gate_up.astype(gu_ref.dtype)
        return total

    def between(turn, turns):
        if wide and turn == 0:
            store()
        if wide and turn == turns - 1:
            for i in range(wide - 1):
                forward(i)

    run_blocks(group, compute, held, sent, start_cross, chain, last, between)
    if wide:
        forward(wide - 1)
        finish()
    settle()


def expert_forward(rows, gates, expert_in, expert_out, shared_in, shared_out, wide, number):
    group, tokens, width = rows.shape
    local = expert_in.shape[0]
    inner = expert_in.shape[2]
    vmem = pl.BlockSpec(memory_space=pltpu.VMEM)
    any_spec = pl.BlockSpec(memory_space=pl.ANY)
    dma = pltpu.SemaphoreType.DMA
    return pl.pallas_call(
        functools.partial(expert_forward_kernel, group, len(wide)),
        out_shape=[
            jax.ShapeDtypeStruct((tokens, width), FLOAT),
            jax.ShapeDtypeStruct((local, group, PICKED, width), BRAIN),
            jax.ShapeDtypeStruct((local, group, PICKED, inner), BRAIN),
            jax.ShapeDtypeStruct((group, tokens, shared_in.shape[1]), BRAIN),
        ]
        + [jax.ShapeDtypeStruct((4 * a.shape[0], a.shape[1]), a.dtype) for a in wide],
        in_specs=[any_spec] + [vmem] * 5 + [any_spec] * len(wide),
        out_specs=[vmem] * 4 + [any_spec] * len(wide),
        scratch_shapes=[pltpu.VMEM(a.shape, a.dtype) for a in wide]
        + [pltpu.VMEM(rows.shape, BRAIN)]
        + fold_scratch(group, tokens, width)
        + [dma((group,))]
        + ([dma((len(wide),)), dma((len(wide), 3)), dma((len(wide), 3))] if wide else []),
        compiler_params=pltpu.CompilerParams(collective_id=number, has_side_effects=True, vmem_limit_bytes=60 * MIB),
        name="expert_forward",
    )(rows, gates, expert_in, expert_out, shared_in, shared_out, *wide)


def swiglu_back(gate, up, grad):
    sig = jax.nn.sigmoid(gate)
    act = gate * sig
    return grad * up * (sig + act * (1.0 - sig)), grad * act, act * up


TILE = 128


def expert_backward_kernel(
    group, sums, d_hbm, xe_hbm, gu_hbm, sgu_hbm, g_ref, in_ref, out_ref, sin_ref, sout_ref, *refs
):
    sum_ins, refs = refs[:sums], refs[sums:]
    (dx_ref, dg_ref, win_hbm, wout_hbm, dsgu_ref, smid_ref), refs = refs[:6], refs[6:]
    sum_outs, sum_bufs, refs = refs[:sums], refs[sums : 4 * sums], refs[4 * sums :]
    rows_ref, xe_ref, gu_ref, mid_ref, win_stage, wout_stage, dgates, held, sent, crossed, passing, *sems = refs
    y, c, z, x = places(group)
    me = 2 * z + x
    gate_send, gate_recv, fetch_sems, stage_sems = sems[7:11]
    wait_load = load_blocks(group, d_hbm, rows_ref, sems[6])
    fetch_gu = pltpu.make_async_copy(gu_hbm, gu_ref, fetch_sems.at[0])
    fetch_xe = pltpu.make_async_copy(xe_hbm, xe_ref, fetch_sems.at[1])
    fetch_gu.start()
    fetch_xe.start()
    fetch_sgu = pltpu.make_async_copy(sgu_hbm, dsgu_ref, fetch_sems.at[2])
    fetch_sgu.start()
    peers = [(None, {"expert": lax.rem(me + k, group)}) for k in range(1, group)]
    if sums:
        peers += [(None, {"dp": 2 * y + 1 - c}), (None, {"dp": 2 * (1 - y) + c})]
    greet(peers)
    start_cross, chain, last, settle = fold(group, held, sent, crossed, passing, dx_ref, sems[:6])
    if sums:
        begin, cross, finish = sum_flow(sum_ins, sum_outs, sum_bufs, sems[11:], group)
        begin()
    fetch_gu.wait()
    fetch_sgu.wait()

    def give(s):
        return remote(dgates.at[s], dg_ref.at[me], gate_send.at[s], gate_recv.at[me], {"expert": s})

    def compute(s):
        wait_load(s)
        grads = rows_ref[s]
        shared_gu = dsgu_ref[s].astype(FLOAT)
        half = shared_gu.shape[1] // 2
        dmid = jnp.dot(grads, sout_ref[...], preferred_element_type=FLOAT)
        dgate, dup, shared_mid = swiglu_back(shared_gu[:, :half], shared_gu[:, half:], dmid)
        shared_d = jnp.concatenate([dgate, dup], axis=1).astype(BRAIN)
        dsgu_ref[s] = shared_d
        smid_ref[s] = shared_mid.astype(BRAIN)
        total = matmul_nt(shared_d, sin_ref[...])
        results = []
        for e in range(in_ref.shape[0]):
            gates = g_ref[s, e : e + 1, :]
            hit = pick_rows(gates)
            chosen = jnp.where(hit, 1.0, 0.0).astype(BRAIN)
            weight = jnp.sum(jnp.where(hit, gates, 0.0), axis=1, keepdims=True)
            picked = jnp.dot(chosen, grads, preferred_element_type=FLOAT)
            results.append((picked * weight).astype(BRAIN))
            raw = jnp.dot(picked.astype(BRAIN), out_ref[e], preferred_element_type=FLOAT)
            gate_up = gu_ref[e, s].astype(FLOAT)
            width = gate_up.shape[1] // 2
            dgate, dup, inner = swiglu_back(gate_up[:, :width], gate_up[:, width:], raw * weight)
            inner_low = inner.astype(BRAIN)
            mid_ref[e, s] = inner_low
            dweight = jnp.sum(raw * inner_low.astype(FLOAT), axis=1, keepdims=True)
            dgates[s, e : e + 1, :] = jnp.sum(jnp.where(hit, dweight, 0.0), axis=0, keepdims=True)
            dgu = jnp.concatenate([dgate, dup], axis=1).astype(BRAIN)
            gu_ref[e, s] = dgu
            back = matmul_nt(dgu, in_ref[e]).astype(BRAIN)
            total = total + matmul_tn(chosen, back)
        for e, result in enumerate(results):
            rows_ref[s, e * PICKED : (e + 1) * PICKED] = result
        pl.when(s != me)(lambda: give(s).start())
        return total

    local, depth, inner = in_ref.shape
    tiles = depth // TILE

    def stores(n):
        e, t, slot = n // tiles, lax.rem(n, tiles), lax.rem(n, 2)
        at = pl.ds(pl.multiple_of(t * TILE, TILE), TILE)
        return (
            pltpu.make_async_copy(win_stage.at[slot], win_hbm.at[e, at], stage_sems.at[0, slot]),
            pltpu.make_async_copy(wout_stage.at[slot], wout_hbm.at[e, at], stage_sems.at[1, slot]),
        )

    def weight_tile(n, carry):
        e, t, slot = n // tiles, lax.rem(n, tiles), lax.rem(n, 2)
        at = pl.ds(pl.multiple_of(t * TILE, TILE), TILE)

        @pl.when(n >= 2)
        def _():
            for store in stores(n - 2):
                store.wait()

        flat = lambda array: array.reshape(-1, array.shape[-1])
        win_stage[slot] = matmul_tn(flat(xe_ref[e, :, :, at]), flat(gu_ref[e])).astype(BRAIN)
        own = pl.ds(pl.multiple_of(e * PICKED, PICKED), PICKED)
        wout_stage[slot] = matmul_tn(flat(rows_ref[:, own, at]), flat(mid_ref[e])).astype(BRAIN)
        for store in stores(n):
            store.start()
        return carry

    def between(turn, turns):
        if turn == 0:
            fetch_xe.wait()
        count = local * tiles
        lax.fori_loop(count * turn // turns, count * (turn + 1) // turns, weight_tile, 0)

    run_blocks(group, compute, held, sent, start_cross, chain, last, between, cross if sums else None)
    if sums:
        finish()
    for n in (local * tiles - 2, local * tiles - 1):
        for store in stores(n):
            store.wait()
    dg_ref[me] = dgates[me]
    for k in range(1, group):
        source = lax.rem(me + k, group)
        remote(dgates.at[source], dg_ref.at[source], gate_send.at[source], gate_recv.at[source], {"expert": source}).wait_recv()
        give(source).wait_send()
    settle()


def local_rows(expert_in):
    return expert_in.shape[0] * PICKED


def expert_backward(grads, picked, gates, gate_up, shared_gu, expert_in, expert_out, shared_in, shared_out, sums, number):
    assert local_rows(expert_in) == grads.shape[1]
    group, tokens, width = grads.shape
    local = expert_in.shape[0]
    inner = expert_in.shape[2]
    vmem = pl.BlockSpec(memory_space=pltpu.VMEM)
    any_spec = pl.BlockSpec(memory_space=pl.ANY)
    dma = pltpu.SemaphoreType.DMA
    return pl.pallas_call(
        functools.partial(expert_backward_kernel, group, len(sums)),
        out_shape=[
            jax.ShapeDtypeStruct((tokens, width), FLOAT),
            jax.ShapeDtypeStruct((group, local, tokens), FLOAT),
            jax.ShapeDtypeStruct((local, width, inner), BRAIN),
            jax.ShapeDtypeStruct((local, width, inner // 2), BRAIN),
            jax.ShapeDtypeStruct(shared_gu.shape, BRAIN),
            jax.ShapeDtypeStruct(shared_gu.shape[:2] + (shared_gu.shape[2] // 2,), BRAIN),
        ]
        + [jax.ShapeDtypeStruct(part, BRAIN) for part in sum_parts_of(sums)],
        in_specs=[any_spec] * 4 + [vmem] * 5 + [any_spec] * len(sums),
        out_specs=[vmem] * 2 + [any_spec] * 2 + [vmem] * 2 + [any_spec] * len(sums),
        scratch_shapes=sum_scratch(sums)
        + [
            pltpu.VMEM(grads.shape, BRAIN),
            pltpu.VMEM(picked.shape, BRAIN),
            pltpu.VMEM(gate_up.shape, BRAIN),
            pltpu.VMEM((local, group, PICKED, inner // 2), BRAIN),
            pltpu.VMEM((2, TILE, inner), BRAIN),
            pltpu.VMEM((2, TILE, inner // 2), BRAIN),
            pltpu.VMEM((group, local, tokens), FLOAT),
        ]
        + fold_scratch(group, tokens, width)
        + [dma((group,))] * 3
        + [dma((3,)), dma((2, 2))]
        + (sum_sems(len(sums)) if sums else []),
        compiler_params=pltpu.CompilerParams(collective_id=number, has_side_effects=True, vmem_limit_bytes=63 * MIB),
        name="expert_backward",
    )(grads, picked, gate_up, shared_gu, gates, expert_in, expert_out, shared_in, shared_out, *sums)


def moe_forward(hidden, routes, valid, norm_gain, router, pieces, wide, number):
    group = lax.axis_size("expert")
    local = pieces[0].shape[0]
    normed, norm_back = jax.vjp(rms_norm, hidden, norm_gain)
    normed_low = normed.astype(BRAIN)
    logits = matmul(normed_low, router)
    chosen = jnp.any(routes[:, :, None] == jnp.arange(router.shape[1])[None, None, :], axis=1)
    largest = jnp.max(jnp.where(chosen, logits, -jnp.inf), axis=1, keepdims=True)
    raised = jnp.where(chosen, jnp.exp(jnp.where(chosen, logits - largest, 0.0)), 0.0)
    probs = raised / jnp.sum(raised, axis=1, keepdims=True)
    gates = probs * valid[:, None]
    if lax.axis_size("dp") == 4:
        rows_all, gates_all, expert_in, expert_out, shared = spread([normed_low, gates.T], pieces, [], group, 1)
    else:
        rows_all, gates_all = spread([normed_low, gates.T], [], [], group, 1)
        expert_in, expert_out, shared = [lax.all_gather(p, "dp", axis=1, tiled=True) for p in pieces]
    part = shared.shape[2] // 3
    weights = (router, shared[0, :, : 2 * part], shared[0, :, 2 * part :], expert_in, expert_out)
    own_gates = lax.dynamic_slice_in_dim(gates_all, lax.axis_index("expert") * local, local, axis=1)
    four = lax.axis_size("dp") == 4
    routed, picked, gate_up, shared_gu, *gathered = expert_forward(
        rows_all, own_gates, expert_in, expert_out, *weights[1:3], wide if four else [], number
    )
    if not four:
        gathered = [lax.all_gather(array, "dp", axis=0, tiled=True) for array in wide]
    return hidden + routed, gathered, (norm_back, normed_low, probs, rows_all, own_gates, picked, gate_up, shared_gu, weights)


def moe_backward(grad_out, saved, valid, grads_all, before, beside, number):
    norm_back, normed_low, probs, rows_all, own_gates, picked, gate_up, shared_gu, weights = saved
    router, shared_in, shared_out, expert_in, expert_out = weights
    group = lax.axis_size("expert")
    if grads_all is None:
        if lax.axis_size("dp") == 4:
            grads_all, *before = spread([grad_out.astype(BRAIN)], [], before, group, 3)
        else:
            grads_all = spread([grad_out.astype(BRAIN)], [], [], group, 3)[0]
            before = [scatter_expert(s) for s in before]
    four = lax.axis_size("dp") == 4
    grad_normed, grad_gates, grad_in, grad_out_weight, dshared, shared_mid, *summed = expert_backward(
        grads_all, picked, own_gates, gate_up, shared_gu, expert_in, expert_out, shared_in, shared_out,
        beside if four else [], number,
    )
    beside = summed if four else [scatter_expert(s) for s in beside]
    flat = lambda array: array.reshape(-1, array.shape[-1])
    shared_grads = [matmul_tn(flat(rows_all), flat(dshared)), matmul_tn(flat(grads_all), flat(shared_mid))]
    sums = [
        jnp.concatenate(shared_grads, axis=1).astype(BRAIN)[None],
        grad_in,
        grad_out_weight,
    ]
    grad_probs = grad_gates.reshape(-1, grad_gates.shape[2]).T * valid[:, None]
    grad_logits = probs * (grad_probs - jnp.sum(probs * grad_probs, axis=1, keepdims=True))
    logits_low = grad_logits.astype(BRAIN)
    grad_router = matmul_tn(normed_low, logits_low).astype(BRAIN)
    grad_hidden, grad_gain = norm_back(grad_normed + matmul_nt(logits_low, router))
    return grad_out + grad_hidden, grad_gain, grad_router, sums, before, beside


def attend_scores(query, key_rows):
    length = query.shape[0]
    down = lax.broadcasted_iota(jnp.int32, (length, length), 0)
    along = lax.broadcasted_iota(jnp.int32, (length, length), 1)
    scores = jnp.where(down >= along, matmul_nt(query, key_rows) * AHDIM ** (-0.5), -1e30)
    raised = jnp.exp(scores - jnp.max(scores, axis=1, keepdims=True))
    return raised / jnp.sum(raised, axis=1, keepdims=True)


def attention_forward_kernel(q_ref, k_ref, v_ref, o_ref):
    for j in range(AHEADS // KVHEADS):
        part = slice(j * AHDIM, (j + 1) * AHDIM)
        probs = attend_scores(q_ref[:, part], k_ref[...])
        o_ref[:, part] = matmul(probs.astype(BRAIN), v_ref[...]).astype(BRAIN)


def attention_specs(length):
    queries = pl.BlockSpec((length, QD // KVHEADS), lambda h: (0, h))
    keys = pl.BlockSpec((length, AHDIM), lambda h: (0, QD // AHDIM + h))
    values = pl.BlockSpec((length, AHDIM), lambda h: (0, (QD + KVD) // AHDIM + h))
    return [queries, keys, values]


def attention_core(qkv):
    length = qkv.shape[0]
    specs = attention_specs(length)
    return pl.pallas_call(
        attention_forward_kernel,
        grid=(KVHEADS,),
        out_shape=jax.ShapeDtypeStruct((length, QD), BRAIN),
        in_specs=specs,
        out_specs=specs[0],
        compiler_params=pltpu.CompilerParams(vmem_limit_bytes=32 * MIB),
        name="attention_forward",
    )(qkv, qkv, qkv)


def attention_backward_kernel(q_ref, k_ref, v_ref, d_ref, dq_ref, dk_ref, dv_ref):
    keys = k_ref[...]
    values = v_ref[...]
    dkeys = jnp.zeros(keys.shape, FLOAT)
    dvalues = jnp.zeros(keys.shape, FLOAT)
    for j in range(AHEADS // KVHEADS):
        part = slice(j * AHDIM, (j + 1) * AHDIM)
        query = q_ref[:, part]
        grads = d_ref[:, part]
        probs = attend_scores(query, keys)
        dprobs = matmul_nt(grads, values)
        dvalues = dvalues + matmul_tn(probs.astype(BRAIN), grads)
        inner = jnp.sum(probs * dprobs, axis=1, keepdims=True)
        draw = (probs * (dprobs - inner) * AHDIM ** (-0.5)).astype(BRAIN)
        dq_ref[:, part] = matmul(draw, keys).astype(BRAIN)
        dkeys = dkeys + matmul_tn(draw, query)
    dk_ref[...] = dkeys.astype(BRAIN)
    dv_ref[...] = dvalues.astype(BRAIN)


def attention_core_back(qkv, grads):
    length = qkv.shape[0]
    specs = attention_specs(length)
    head_block = pl.BlockSpec((length, AHDIM), lambda h: (0, h))
    return pl.pallas_call(
        attention_backward_kernel,
        grid=(KVHEADS,),
        out_shape=[
            jax.ShapeDtypeStruct((length, QD), BRAIN),
            jax.ShapeDtypeStruct((length, KVD), BRAIN),
            jax.ShapeDtypeStruct((length, KVD), BRAIN),
        ],
        in_specs=specs + [specs[0]],
        out_specs=[specs[0], head_block, head_block],
        compiler_params=pltpu.CompilerParams(vmem_limit_bytes=32 * MIB),
        name="attention_backward",
    )(qkv, qkv, qkv, grads)


def attention_forward(hidden, norm_gain, attn_qkv, attn_out):
    normed, norm_back = jax.vjp(rms_norm, hidden, norm_gain)
    normed_low = normed.astype(BRAIN)
    qkv = matmul(normed_low, attn_qkv).astype(BRAIN)
    attended = attention_core(qkv)
    output = hidden + matmul_nt(attended, attn_out)
    return output, (norm_back, normed_low, qkv, attended)


def attention_backward(grad_out, saved, attn_qkv, attn_out):
    norm_back, normed_low, qkv, attended = saved
    grad_low = grad_out.astype(BRAIN)
    grad_attn_out = matmul_tn(grad_low, attended).astype(BRAIN)
    grad_attended = matmul(grad_low, attn_out).astype(BRAIN)
    grad_qkv = jnp.concatenate(attention_core_back(qkv, grad_attended), axis=1)
    grad_attn_qkv = matmul_tn(normed_low, grad_qkv).astype(BRAIN)
    grad_hidden, grad_gain = norm_back(matmul_nt(grad_qkv, attn_qkv))
    return grad_out + grad_hidden, grad_gain, grad_attn_qkv, grad_attn_out


def gather_dense(array):
    return lax.all_gather(array, BOTH, axis=0, tiled=True)


def scatter_dense(array):
    return lax.psum_scatter(array, BOTH, scatter_dimension=0, tiled=True).astype(FLOAT)


def scatter_expert(array):
    return lax.psum_scatter(array, "dp", scatter_dimension=1, tiled=True).astype(FLOAT)


def shared_columns(shared):
    group = lax.axis_size("expert")
    rows = shared[0].shape[0]
    pieces = []
    for shared_in, shared_out in zip(shared[0::2], shared[1::2]):
        half = shared_in.shape[1] // 2
        pieces += [shared_in[:, :half], shared_in[:, half:], shared_out]
    cut = [piece.reshape(rows, group, -1) for piece in pieces]
    return jnp.transpose(jnp.concatenate(cut, axis=2), (1, 0, 2))


def shared_whole(own):
    part = own.shape[2] // 6

    def columns(index):
        piece = jnp.transpose(own[:, :, index * part : (index + 1) * part], (1, 0, 2))
        return piece.reshape(piece.shape[0], -1)

    return [
        jnp.concatenate([columns(0), columns(1)], axis=1),
        columns(2),
        jnp.concatenate([columns(3), columns(4)], axis=1),
        columns(5),
    ]


def exchange(blocks):
    return lax.all_to_all(blocks, "expert", split_axis=0, concat_axis=0, tiled=True)


def first_gather(dense, shared, rows):
    if lax.axis_size("dp") == 4:
        *dense, shared, rows = head_exchange(dense, shared, rows, 5)
        return [array.reshape(-1, array.shape[2]) for array in dense], shared, rows
    rows = spread([rows], [], [], lax.axis_size("expert"), 3)[0]
    return [gather_dense(array) for array in dense], exchange(shared), rows


def last_sums(left, right, routers, small, sums_a, shared_b):
    group = lax.axis_size("expert")
    cut = lambda array: array.reshape(group, -1, array.shape[-1])
    shared_b = cut(shared_b.astype(BRAIN))
    if lax.axis_size("dp") == 4:
        routers = routers.reshape(4 * group, -1, routers.shape[1])
        return tail_exchange(left.T, right, routers, shared_b, small, sums_a, 6)
    mix = matmul_tn(left, right).astype(BRAIN)
    shared_a, *sums_a = [scatter_expert(s) for s in sums_a]
    shared_a = exchange(cut(shared_a.astype(BRAIN)))
    return scatter_dense(mix), scatter_dense(routers), exchange(shared_b), lax.psum(small, BOTH), shared_a, *sums_a


def per_device(
    layer_input, cotangent, lengths, routes_a, routes_b,
    mixer_in, mixer_out, router_a, shared_in_a, shared_out_a, expert_in_a, expert_out_a,
    attn_qkv, attn_out, router_b, shared_in_b, shared_out_b, expert_in_b, expert_out_b,
    norm_gains, mixer_gain, conv_weight, conv_bias, decay_log, step_bias, skip_gain,
):
    small = {
        "conv_weight": conv_weight,
        "conv_bias": conv_bias,
        "decay_log": decay_log,
        "step_bias": step_bias,
        "skip_gain": skip_gain,
        "mixer_gain": mixer_gain,
    }
    assert lengths.shape[0] == 1 and layer_input.shape[0] == SLOT_LEN
    group = lax.axis_size("expert")
    experts = router_a.shape[1]
    valid = (jnp.arange(SLOT_LEN) < lengths[0]).astype(FLOAT)
    grad = cotangent * valid[:, None]
    (w_mixer_in, w_mixer_out, w_routers), w_shared, last_rows = first_gather(
        [mixer_in, mixer_out, jnp.concatenate([router_a, router_b], axis=1)],
        shared_columns([shared_in_a, shared_out_a, shared_in_b, shared_out_b]),
        grad.astype(BRAIN),
    )
    w_shared = w_shared.reshape(1, -1, w_shared.shape[2])
    half = w_shared.shape[2] // 2
    attn_both, w_routers = lax.optimization_barrier((jnp.concatenate([attn_qkv, attn_out], axis=1), w_routers))
    attn_part = lax.all_gather(attn_both, "expert", axis=0, tiled=True)
    hidden = layer_input.astype(FLOAT)
    hidden, saved_mix = mixer_forward(hidden, norm_gains[0], w_mixer_in, w_mixer_out, small)
    hidden, (w_qkv, w_attn_out), saved_a = moe_forward(
        hidden,
        routes_a,
        valid,
        norm_gains[1],
        w_routers[:, :experts],
        [expert_in_a, expert_out_a, w_shared[:, :, :half]],
        [attn_part[:, :QKV], attn_part[:, QKV:]],
        2,
    )
    hidden, saved_attn = attention_forward(hidden, norm_gains[2], w_qkv, w_attn_out)
    layer_output, _, saved_b = moe_forward(
        hidden,
        routes_b,
        valid,
        norm_gains[3],
        w_routers[:, experts:],
        [expert_in_b, expert_out_b, w_shared[:, :, half:]],
        [],
        7,
    )
    grad, gain_four, d_router_b, sums_b, _, _ = moe_backward(grad, saved_b, valid, last_rows, [], [], 4)
    grad, gain_three, d_qkv, d_attn_out = attention_backward(grad, saved_attn, w_qkv, w_attn_out)
    grad, gain_two, d_router_a, sums_a, d_attn, sums_b = moe_backward(
        grad, saved_a, valid, None, [d_qkv[None], d_attn_out[None]], sums_b, 8
    )
    d_attn = jnp.concatenate([part[0].astype(BRAIN) for part in d_attn], axis=1)
    d_attn = lax.psum_scatter(d_attn, "expert", scatter_dimension=0, tiled=True).astype(FLOAT)
    d_qkv, d_attn_out = d_attn[:, :QKV], d_attn[:, QKV:]
    d_shared_b, d_in_b, d_out_b = [part.astype(FLOAT) for part in sums_b]
    grad, gain_one, mix_left, mix_right, d_mixer_out, grad_small = mixer_backward(
        grad, saved_mix, w_mixer_in, w_mixer_out, small
    )
    d_mixer_out = scatter_dense(d_mixer_out)
    parts = [jnp.stack([gain_one, gain_two, gain_three, gain_four])] + list(grad_small)
    flat = jnp.concatenate([part.reshape(-1) for part in parts])
    padded = jnp.pad(flat, (0, -flat.shape[0] % 1024)).reshape(-1, 128)
    d_mixer_in, d_routers, d_shared_b, summed, d_shared_a, d_in_a, d_out_a = last_sums(
        mix_left, mix_right, jnp.concatenate([d_router_a, d_router_b], axis=1), padded, sums_a, d_shared_b
    )
    d_in_a, d_out_a = d_in_a.astype(FLOAT), d_out_a.astype(FLOAT)
    d_shared = shared_whole(jnp.concatenate([d_shared_a, d_shared_b], axis=2).astype(FLOAT))
    summed = summed.reshape(-1)
    sums = []
    place = 0
    for part in parts:
        sums.append(summed[place : place + part.size].reshape(part.shape))
        place += part.size
    return (
        layer_output, grad,
        d_mixer_in, d_mixer_out, d_routers[:, :experts], d_shared[0], d_shared[1], d_in_a, d_out_a,
        d_qkv, d_attn_out, d_routers[:, experts:], d_shared[2], d_shared[3], d_in_b, d_out_b,
        *sums,
    )


def solution(mesh):
    rows = P(BOTH, None)
    expert = P("expert", "dp", None)
    first = (rows, rows, rows, rows, rows, expert, expert)
    second = (rows, rows, rows, rows, rows, expert, expert)
    return jax.shard_map(
        per_device,
        mesh=mesh,
        in_specs=(rows, rows, P(BOTH), rows, rows) + first + second + (P(),) * 7,
        out_specs=(rows, rows) + first + second + (P(),) * 7,
        check_vma=False,
    )
```
